32 devices in a mesh: grp: 4 (over x, core), blk: 8 (over z, y).
Axes of the slice: x: 2, y: 2, z: 4, core: 2. Of those that a mesh axis runs over, the one named last changes fastest.
Arguments:
- tokens: bfloat16 [8192, 768], P(('grp', 'blk')), may hold values from -6 to 6
- seg_ids: int32 [8192], P(('grp', 'blk')), may hold values from 0 to 1, as said below
- turn_ids: int32 [8192], P(('grp', 'blk')), may hold values from 0 to 8192, as said below
- prev_ids: int32 [8192], P(('grp', 'blk')), may hold values 0 or 1
- answer_table: bfloat16 [2, 768], replicated, may hold values from -3 to 3
- query_weight: bfloat16 [768, 768], replicated, may hold values from -0.21875 to 0.21875
- query_bias: bfloat16 [768], replicated, may hold values from -3 to 3
- key_weight: bfloat16 [768, 768], replicated, may hold values from -0.21875 to 0.21875
- value_weight: bfloat16 [768, 768], replicated, may hold values from -0.21875 to 0.21875
- value_bias: bfloat16 [768], replicated, may hold values from -3 to 3
- out_weight: bfloat16 [768, 768], replicated, may hold values from -3.5 to 3.5
- out_bias: bfloat16 [768], replicated, may hold values from -3 to 3
- norm_gain: bfloat16 [768], replicated, may hold values from 0.5 to 1.5
- norm_shift: bfloat16 [768], replicated, may hold values from -3 to 3
- up_weight: bfloat16 [768, 3072], replicated, may hold values from -0.21875 to 0.21875
- up_bias: bfloat16 [3072], replicated, may hold values from -3 to 3
- down_weight: bfloat16 [3072, 768], replicated, may hold values from -0.109375 to 0.109375
- down_bias: bfloat16 [768], replicated, may hold values from -3 to 3
- final_gain: bfloat16 [768], replicated, may hold values from 0.5 to 1.5
- final_shift: bfloat16 [768], replicated, may hold values from -3 to 3
- cotangent: bfloat16 [8192, 768], P(('grp', 'blk')), may hold values from -6 to 6
Outputs:
- mixed: bfloat16 [8192, 768], P(('grp', 'blk'))
- grad_tokens: float32 [8192, 768], P(('grp', 'blk'))
- grad_answer: float32 [2, 768], P(None, 'blk')
- grad_query_weight: float32 [768, 768], P('blk')
- grad_query_bias: float32 [768], P('blk')
- grad_key_weight: float32 [768, 768], P('blk')
- grad_value_weight: float32 [768, 768], P('blk')
- grad_value_bias: float32 [768], P('blk')
- grad_out_weight: float32 [768, 768], P('blk')
- grad_out_bias: float32 [768], P('blk')
- grad_norm_gain: float32 [768], P('blk')
- grad_norm_shift: float32 [768], P('blk')
- grad_up_weight: float32 [768, 3072], P('blk')
- grad_up_bias: float32 [3072], P('blk')
- grad_down_weight: float32 [3072, 768], P('blk')
- grad_down_bias: float32 [768], P('blk')
- grad_final_gain: float32 [768], P('blk')
- grad_final_shift: float32 [768], P('blk')
The draws below stay inside these ranges and needn't reach their ends.
Inputs may be any that keep to these rules, and one draw needn't show every extreme that they name: `seg_ids`: in each aligned block of 256 tokens the table tokens (0) come first, at least 32 and at most 64 of them, followed by at least one question token; some block has exactly 64. `turn_ids`: 0 exactly on table tokens; the tokens of one question are contiguous, lie within one aligned block of 256 tokens and share one number, which no other question of the group carries.
All inputs are finite; a program needn't handle non-finite values. No bound on the sum of `prev_ids` on one device may be relied on, other than what follows from the above.
Results may differ from the reference program's by a relative error of at most 0.02.
Values may be sent and summed in bfloat16 or wider, within the bound.
No kernel may reach another device: no remote copies, remote signals or barrier semaphores. Data moves between devices by JAX's collectives and lax.ppermute only.
A program may use at most 384 MiB of HBM per device.

```python
import math
import jax
import jax.numpy as jnp
from jax import lax

D = 768
HEADS = 12
HEAD_DIM = 64
FF = 3072
TOK_DEV = 256
TAB_MAX = 64
TOKENS = 8192
N_GRP = 4


def table_layout(key):
    blocks = TOKENS // TOK_DEV
    key_count, key_full, key_marks = jax.random.split(key, 3)
    counts = jax.random.randint(key_count, (blocks,), TAB_MAX // 2, TAB_MAX + 1)
    fullest = jax.random.randint(key_full, (), 0, blocks)
    counts = jnp.where(jnp.arange(blocks) == fullest, TAB_MAX, counts)
    position = jnp.arange(TOK_DEV)[None, :]
    in_table = position < counts[:, None]
    starts = (jax.random.randint(key_marks, (blocks, TOK_DEV), 0, 24) == 0) | (position == counts[:, None])
    starts = starts & jnp.logical_not(in_table)
    running = jnp.cumsum(starts.astype(jnp.int32), axis=1)
    total_starts = running[:, -1:]
    block_end = ((jnp.arange(blocks) + 1) * TOK_DEV)[:, None]
    turn_id = jnp.where(in_table, 0, block_end - (total_starts - running))
    return (in_table, turn_id)


def draw_seg_ids(key, part):
    in_table, turn_id = table_layout(key)
    return jnp.logical_not(in_table).astype(jnp.int32).reshape(TOKENS)


def draw_turn_ids(key, part):
    in_table, turn_id = table_layout(key)
    return turn_id.astype(jnp.int32).reshape(TOKENS)


def with_ends(values, key, low, top_value):
    place = [jax.random.randint(jax.random.fold_in(key, axis), (), 0, length) for axis, length in enumerate(values.shape)]
    main_axis = values.shape.index(max(values.shape))
    neighbour = place[:main_axis] + [(place[main_axis] + 1) % values.shape[main_axis]] + place[main_axis + 1:]
    return values.at[tuple(place)].set(low).at[tuple(neighbour)].set(top_value)


def block_levels(key, shape, pieces, smallest, largest):
    factor_of, own = 1.0, jax.random.fold_in(key, 6)
    for dim, parts in pieces:
        heights = jnp.exp(jax.random.uniform(jax.random.fold_in(own, dim), (parts,), jnp.float32, smallest / len(pieces), largest / len(pieces)))
        factor_of = factor_of * jnp.repeat(heights, shape[dim] // parts).reshape([-1 if axis == dim else 1 for axis in range(len(shape))])
    return factor_of


def normal_values(own_key, dims, scale, bound, cuts=(), dtype=jnp.bfloat16):
    values = scale * jax.random.normal(own_key, dims, jnp.float32)
    if cuts:
        values = values * block_levels(own_key, dims, cuts, -0.22, 0.18)
    return jnp.clip(values, -bound, bound).astype(dtype)


def setup_inputs(seed: int = 0) -> dict:
    key_of = jax.random.split(jax.random.key(seed), 22)
    tokens = normal_values(key_of[0], (TOKENS, D), 1.0, 6.0, ((0, 32),))
    seg_ids = draw_seg_ids(jax.random.fold_in(key_of[21], 71), 0)
    turn_ids = draw_turn_ids(jax.random.fold_in(key_of[21], 71), 0)
    prev_ids = with_ends((jax.random.randint(key_of[3], (TOKENS,), 0, 3) < 1).astype(jnp.int32), jax.random.fold_in(key_of[3], 1), 0, 1)
    answer_table = normal_values(key_of[4], (2, D), 0.5, 3.0)
    query_weight = normal_values(key_of[5], (D, D), D ** -0.5, 0.21875)
    query_bias = normal_values(key_of[6], (D,), 0.5, 3.0)
    key_weight = normal_values(key_of[7], (D, D), D ** -0.5, 0.21875)
    value_weight = normal_values(key_of[8], (D, D), D ** -0.5, 0.21875)
    value_bias = normal_values(key_of[9], (D,), 0.5, 3.0)
    out_weight = normal_values(key_of[10], (D, D), (max(1, D // 256)) ** -0.5, 3.5)
    out_bias = normal_values(key_of[11], (D,), 0.5, 3.0)
    norm_gain = jnp.clip(1.0 + 0.1 * jax.random.normal(key_of[12], (D,), jnp.float32), 0.5, 1.5).astype(jnp.bfloat16)
    norm_shift = normal_values(key_of[13], (D,), 0.5, 3.0)
    up_weight = normal_values(key_of[14], (D, FF), D ** -0.5, 0.21875)
    up_bias = normal_values(key_of[15], (FF,), 0.5, 3.0)
    down_weight = normal_values(key_of[16], (FF, D), FF ** -0.5, 0.109375)
    down_bias = normal_values(key_of[17], (D,), 0.5, 3.0)
    final_gain = jnp.clip(1.0 + 0.1 * jax.random.normal(key_of[18], (D,), jnp.float32), 0.5, 1.5).astype(jnp.bfloat16)
    final_shift = normal_values(key_of[19], (D,), 0.5, 3.0)
    cotangent = normal_values(key_of[20], (TOKENS, D), 1.0, 6.0, ((0, 32),))
    return {"tokens": tokens, "seg_ids": seg_ids, "turn_ids": turn_ids, "prev_ids": prev_ids, "answer_table": answer_table, "query_weight": query_weight, "query_bias": query_bias, "key_weight": key_weight, "value_weight": value_weight, "value_bias": value_bias, "out_weight": out_weight, "out_bias": out_bias, "norm_gain": norm_gain, "norm_shift": norm_shift, "up_weight": up_weight, "up_bias": up_bias, "down_weight": down_weight, "down_bias": down_bias, "final_gain": final_gain, "final_shift": final_shift, "cotangent": cotangent}


@jax.custom_vjp
def low(v):
    return lax.optimization_barrier(v.astype(jnp.bfloat16)).astype(jnp.float32)

@jax.custom_vjp
def low_back(v):
    return v

def low_keep(v):
    return (low(v), None)

def low_pass(kept, grad):
    return (grad,)

def back_keep(v):
    return (v, None)

def back_low(kept, grad):
    return (low(grad),)
low.defvjp(low_keep, low_pass)
low_back.defvjp(back_keep, back_low)
far_below = -1e+30

def row_norm(values, gain_vec, shift_vec):
    average = lax.optimization_barrier(jnp.mean(values, axis=-1, keepdims=True))
    centred = values - average
    spread = lax.optimization_barrier(jnp.mean(centred * centred, axis=-1, keepdims=True))
    return centred * lax.rsqrt(spread + 1e-06) * gain_vec + shift_vec

def reference(tokens, seg_ids, turn_ids, prev_ids, answer_table, query_weight, query_bias, key_weight, value_weight, value_bias, out_weight, out_bias, norm_gain, norm_shift, up_weight, up_bias, down_weight, down_bias, final_gain, final_shift, cotangent):
    highest = lax.Precision.HIGHEST
    score_scale = HEAD_DIM ** (-0.5)

    def attention(queries, key_rows, value_rows):
        head_shape = (N_GRP, -1, HEADS, HEAD_DIM)

        def one_group(group_args):
            query_group, key_group, value_group, seg_group, turn_group = group_args
            group_len = query_group.shape[0]
            block_size = math.gcd(group_len, 512)
            key_open = seg_group == 0

            def one_block(block_args):
                query_block, turn_block = block_args
                scores = low_back(jnp.einsum('qhd,khd->hqk', query_block, key_group, precision=highest) * score_scale)
                allowed = key_open[None, :] | (turn_block[:, None] == turn_group[None, :])
                masked = jnp.where(allowed[None], scores, far_below)
                row_top = lax.optimization_barrier(jnp.max(masked, axis=-1, keepdims=True))
                weights = jnp.where(allowed[None], jnp.exp(masked - row_top), 0.0)
                prob_low = low(weights / lax.optimization_barrier(jnp.sum(weights, axis=-1, keepdims=True)))
                return jnp.einsum('hqk,khd->qhd', prob_low, value_group, precision=highest)
            out_blocks = lax.map(jax.checkpoint(one_block), (query_group.reshape(group_len // block_size, block_size, HEADS, HEAD_DIM), turn_group.reshape(group_len // block_size, block_size)))
            return out_blocks.reshape(group_len, HEADS * HEAD_DIM)
        grouped = lax.map(one_group, (queries.reshape(head_shape), key_rows.reshape(head_shape), value_rows.reshape(head_shape), seg_ids.reshape(N_GRP, -1), turn_ids.reshape(N_GRP, -1)))
        return grouped.reshape(queries.shape)

    def forward(tokens_f, answer_f, query_w, query_b, key_w, value_w, value_b, out_w, out_b, norm_g, norm_s, up_w, up_b, down_w, down_b, final_g, final_s):
        one_hot = (prev_ids[:, None] == jnp.arange(2)[None, :]).astype(jnp.float32)
        resid_in = tokens_f + jnp.dot(one_hot, answer_f, precision=highest)
        layer_input = low(resid_in)
        queries = low_back(low(jnp.dot(layer_input, query_w, precision=highest) + query_b))
        key_rows = low_back(low(jnp.dot(layer_input, key_w, precision=highest)))
        value_rows = low_back(low(jnp.dot(layer_input, value_w, precision=highest) + value_b))
        context = low_back(low(attention(queries, key_rows, value_rows)))
        attn_out = low_back(jnp.dot(context, out_w, precision=highest) + out_b)
        middle = row_norm(resid_in + attn_out, norm_g, norm_s)
        middle_low = low(middle)
        pre_act = low_back(jnp.dot(middle_low, up_w, precision=highest) + up_b)
        act_low = low(jax.nn.gelu(pre_act, approximate=False))
        ffn_out = low_back(jnp.dot(act_low, down_w, precision=highest) + down_b)
        return row_norm(middle + ffn_out, final_g, final_s)
    floats = [array.astype(jnp.float32) for array in (tokens, answer_table, query_weight, query_bias, key_weight, value_weight, value_bias, out_weight, out_bias, norm_gain, norm_shift, up_weight, up_bias, down_weight, down_bias, final_gain, final_shift)]
    output, pullback = jax.vjp(forward, *floats)
    gradients = pullback(cotangent.astype(jnp.float32))
    return (output.astype(jnp.bfloat16), gradients[0], gradients[1], gradients[2], gradients[3], gradients[4], gradients[5], gradients[6], gradients[7], gradients[8], gradients[9], gradients[10], gradients[11], gradients[12], gradients[13], gradients[14], gradients[15], gradients[16])
```

```python
import math

import jax
import jax.numpy as jnp
from jax import lax
from jax.sharding import PartitionSpec as P

HEADS = 12
HEAD_DIM = 64
TAB_MAX = 64
far_below = -1e30
BF = jnp.bfloat16
F32 = jnp.float32


def outer_sum(left, right):
    return lax.dot_general(left, right, (((0,), (0,)), ((), ())), preferred_element_type=F32)


def back_dot(left, right):
    return lax.dot_general(left, right, (((1,), (1,)), ((), ())), preferred_element_type=F32)


def fwd_dot(left, right):
    return jnp.dot(left, right, preferred_element_type=F32)


def norm_parts(values):
    centred = values - jnp.mean(values, axis=-1, keepdims=True)
    spread = jnp.mean(centred * centred, axis=-1, keepdims=True)
    inv = lax.rsqrt(spread + 1e-06)
    return centred * inv, inv


def norm_grad(grad, normed, inv, gain):
    scaled = grad * gain
    return inv * (
        scaled
        - jnp.mean(scaled, axis=-1, keepdims=True)
        - normed * jnp.mean(scaled * normed, axis=-1, keepdims=True)
    )


def local(
    tokens, seg_ids, turn_ids, prev_ids, answer_table, query_weight, query_bias,
    key_weight, value_weight, value_bias, out_weight, out_bias, norm_gain, norm_shift,
    up_weight, up_bias, down_weight, down_bias, final_gain, final_shift, cotangent,
):
    rows, width = tokens.shape
    blocks = lax.axis_size("blk")
    grps = lax.axis_size("grp")
    tab = TAB_MAX
    scale = HEAD_DIM ** (-0.5)
    f = lambda v: v.astype(F32)
    is_one = (prev_ids == 1)[:, None]
    answers = f(answer_table)
    resid_in = f(tokens) + jnp.where(is_one, answers[1][None], answers[0][None])
    layer_input = resid_in.astype(BF)
    flags = jnp.concatenate(
        [(seg_ids[:tab] == 0).astype(BF), jnp.zeros((128 - tab,), BF), prev_ids[:tab].astype(BF),
         jnp.zeros((width - 128 - tab,), BF)]
    )[None]
    payload = jnp.concatenate([layer_input[:tab], flags, jnp.zeros((7, width), BF)], axis=0)
    gathered = lax.all_gather(payload, "blk", axis=0, tiled=False)
    table_input = gathered[:, :tab].reshape(blocks * tab, width)
    table_open = gathered[:, tab, :tab].reshape(blocks * tab) > 0.5
    table_prev = gathered[:, tab, 128 : 128 + tab].reshape(blocks * tab)

    qkv_in = jnp.concatenate([table_input, layer_input], axis=0)
    queries = (fwd_dot(layer_input, query_weight) + f(query_bias)).astype(BF)
    keys = fwd_dot(qkv_in, key_weight).astype(BF)
    values = (fwd_dot(qkv_in, value_weight) + f(value_bias)).astype(BF)
    n_keys = keys.shape[0]
    own_open = (turn_ids[:, None] == turn_ids[None, :]) & (seg_ids != 0)[None, :]
    allowed = jnp.concatenate(
        [jnp.broadcast_to(table_open[None], (rows, blocks * tab)), own_open], axis=1
    )[None]
    qh = queries.reshape(rows, HEADS, HEAD_DIM)
    kh = keys.reshape(n_keys, HEADS, HEAD_DIM)
    vh = values.reshape(n_keys, HEADS, HEAD_DIM)
    scores = jnp.einsum("qhd,khd->hqk", qh, kh, preferred_element_type=F32) * scale
    scores = jnp.where(allowed, scores, far_below)
    top = jnp.max(scores, axis=-1, keepdims=True)
    weights = jnp.where(allowed, jnp.exp(scores - top), 0.0)
    prob_full = weights / jnp.sum(weights, axis=-1, keepdims=True)
    prob_low = prob_full.astype(BF)
    context = jnp.einsum("hqk,khd->qhd", prob_low, vh, preferred_element_type=F32)
    context_low = context.reshape(rows, width).astype(BF)

    first_in = resid_in + fwd_dot(context_low, out_weight) + f(out_bias)
    normed1, inv1 = norm_parts(first_in)
    middle = normed1 * f(norm_gain) + f(norm_shift)
    middle_low = middle.astype(BF)
    pre_act = fwd_dot(middle_low, up_weight) + f(up_bias)
    cdf = 0.5 * (1.0 + lax.erf(pre_act * (0.5**0.5)))
    act_low = (pre_act * cdf).astype(BF)
    gelu_slope = cdf + pre_act * jnp.exp(-0.5 * pre_act * pre_act) * (1.0 / math.sqrt(2 * math.pi))
    second_in = middle + fwd_dot(act_low, down_weight) + f(down_bias)
    normed2, inv2 = norm_parts(second_in)
    mixed = (normed2 * f(final_gain) + f(final_shift)).astype(BF)
    cot = f(cotangent)
    grad_final_sum = norm_grad(cot, normed2, inv2, f(final_gain))
    grad_ffn = grad_final_sum.astype(BF)
    grad_down_weight = outer_sum(act_low, grad_ffn).astype(BF)
    grad_pre = (back_dot(grad_ffn, down_weight) * gelu_slope).astype(BF)
    grad_up_weight = outer_sum(middle_low, grad_pre).astype(BF)

    def share(value):
        part = lax.psum_scatter(value, ("blk", "grp"), scatter_dimension=0, tiled=True)
        return f(lax.all_gather(part, "grp", axis=0, tiled=True))

    out_down = share(grad_down_weight)
    out_up = share(grad_up_weight)

    grad_middle = grad_final_sum + back_dot(grad_pre, up_weight)
    grad_mid_sum = norm_grad(grad_middle, normed1, inv1, f(norm_gain))
    grad_attn = grad_mid_sum.astype(BF)
    grad_out_weight = outer_sum(context_low, grad_attn).astype(BF)
    grad_context = back_dot(grad_attn, out_weight).astype(BF).reshape(rows, HEADS, HEAD_DIM)
    row_dot = jnp.einsum("qhd,qhd->hq", f(grad_context), context)
    grad_probs = jnp.einsum("qhd,khd->hqk", grad_context, vh, preferred_element_type=F32)
    grad_scores = (prob_full * (grad_probs - row_dot[..., None])).astype(BF)
    grad_queries = (
        (jnp.einsum("hqk,khd->qhd", grad_scores, kh, preferred_element_type=F32) * scale)
        .reshape(rows, width)
        .astype(BF)
    )
    grad_keys = (
        (jnp.einsum("hqk,qhd->khd", grad_scores, qh, preferred_element_type=F32) * scale)
        .reshape(n_keys, width)
        .astype(BF)
    )
    grad_values = (
        jnp.einsum("hqk,qhd->khd", prob_low, grad_context, preferred_element_type=F32)
        .reshape(n_keys, width)
        .astype(BF)
    )
    grad_kv_in = back_dot(grad_keys, key_weight) + back_dot(grad_values, value_weight)
    grad_table = grad_kv_in[: blocks * tab]
    table_share = lax.psum_scatter(grad_table.astype(BF), "blk", scatter_dimension=0, tiled=True)
    grad_query_weight = outer_sum(layer_input, grad_queries).astype(BF)
    grad_key_weight = outer_sum(qkv_in, grad_keys).astype(BF)
    grad_value_weight = outer_sum(qkv_in, grad_values).astype(BF)
    n_out = width // blocks
    stacked = jnp.stack(
        [grad_query_weight, grad_key_weight, grad_value_weight, grad_out_weight], axis=0
    ).reshape(4, blocks, grps, n_out // grps, width)
    stacked = jnp.transpose(stacked, (1, 2, 0, 3, 4)).reshape(blocks * grps * 4, n_out // grps, width)
    square = lax.psum_scatter(stacked, ("blk", "grp"), scatter_dimension=0, tiled=True)
    square = lax.all_gather(square, "grp", axis=1, tiled=True)

    grad_input_local = grad_mid_sum + back_dot(grad_queries, query_weight) + grad_kv_in[blocks * tab :]
    all_prev = jnp.concatenate([table_prev, prev_ids.astype(BF)])
    all_grads = jnp.concatenate([grad_table, grad_input_local], axis=0)
    total_sum = jnp.sum(all_grads, axis=0)
    one_sum = jnp.sum(jnp.where(all_prev[:, None] > 0.5, all_grads, 0.0), axis=0)
    column_sum = lambda v: jnp.sum(f(v), axis=0)
    vectors = jnp.stack(
        [
            total_sum - one_sum,
            one_sum,
            column_sum(grad_queries),
            column_sum(grad_values),
            column_sum(grad_attn),
            jnp.sum(grad_middle * normed1, axis=0),
            jnp.sum(grad_middle, axis=0),
            column_sum(grad_ffn),
            jnp.sum(cot * normed2, axis=0),
            jnp.sum(cot, axis=0),
        ]
        + list(column_sum(grad_pre).reshape(-1, width)),
        axis=0,
    )
    vectors = lax.psum(vectors, ("blk", "grp"))
    own = lax.axis_index("blk")
    mine = lax.dynamic_slice_in_dim(vectors[:10], own * n_out, n_out, 1)
    ff_out = up_weight.shape[1] // blocks
    up_bias_out = lax.dynamic_slice_in_dim(vectors[10:].reshape(-1), own * ff_out, ff_out, 0)
    grad_input = grad_input_local.at[:tab].add(f(table_share))
    return (
        mixed,
        grad_input,
        mine[:2],
        f(square[0]),
        mine[2],
        f(square[1]),
        f(square[2]),
        mine[3],
        f(square[3]),
        mine[4],
        mine[5],
        mine[6],
        out_up,
        up_bias_out,
        out_down,
        mine[7],
        mine[8],
        mine[9],
    )


def solution(mesh):
    both = ("grp", "blk")
    placed = (P(both, None), P(both), P(both), P(both)) + (P(),) * 16 + (P(both, None),)
    vec, mat = P("blk"), P("blk", None)
    return jax.shard_map(
        local,
        mesh=mesh,
        in_specs=placed,
        out_specs=(
            P(both, None), P(both, None), P(None, "blk"), mat, vec, mat, mat, vec, mat, vec,
            vec, vec, mat, vec, mat, vec, vec, vec,
        ),
        check_vma=False,
    )
```

```python
import math

import jax
import jax.numpy as jnp
from jax import lax
from jax.experimental import pallas as pl
from jax.experimental.pallas import tpu as pltpu
from jax.sharding import PartitionSpec as P

HEADS = 12
HEAD_DIM = 64
TAB_MAX = 64
LANES = 256
far_below = -1e30
BF = jnp.bfloat16
F32 = jnp.float32
MIB = 1 << 20


def outer_sum(left, right):
    return lax.dot_general(left, right, (((0,), (0,)), ((), ())), preferred_element_type=F32)


def back_dot(left, right):
    return lax.dot_general(left, right, (((1,), (1,)), ((), ())), preferred_element_type=F32)


def fwd_dot(left, right):
    return jnp.dot(left, right, preferred_element_type=F32)


def norm_parts(values):
    centred = values - jnp.mean(values, axis=-1, keepdims=True)
    spread = jnp.mean(centred * centred, axis=-1, keepdims=True)
    inv = lax.rsqrt(spread + 1e-06)
    return centred * inv, inv


def norm_grad(grad, normed, inv, gain):
    scaled = grad * gain
    return inv * (
        scaled
        - jnp.mean(scaled, axis=-1, keepdims=True)
        - normed * jnp.mean(scaled * normed, axis=-1, keepdims=True)
    )


def head_lanes(shape, index):
    lane = lax.broadcasted_iota(jnp.int32, shape, len(shape) - 1)
    return (lane >= index * HEAD_DIM) & (lane < (index + 1) * HEAD_DIM)


def attend_kernel(
    table_ref, key_w_ref, value_w_ref, value_b_ref, q_ref, own_k_ref, own_v_ref, bias_ref,
    keys_ref, values_ref, prob_ref, context_ref,
):
    n_table = table_ref.shape[0]
    table = table_ref[...]
    keys_ref[:n_table] = fwd_dot(table, key_w_ref[...]).astype(BF)
    values_ref[:n_table] = (fwd_dot(table, value_w_ref[...]) + value_b_ref[...]).astype(BF)
    keys_ref[n_table:] = own_k_ref[...]
    values_ref[n_table:] = own_v_ref[...]
    queries = q_ref[...]
    context = jnp.zeros(context_ref.shape, F32)
    for h in range(LANES // HEAD_DIM):
        mask = head_lanes(queries.shape, h)
        picked = jnp.where(mask, queries, jnp.zeros_like(queries))
        scores = back_dot(picked, keys_ref[...]) + bias_ref[...]
        top = jnp.max(scores, axis=-1, keepdims=True)
        weights = jnp.exp(scores - top)
        prob = (weights * (1.0 / jnp.sum(weights, axis=-1, keepdims=True))).astype(BF)
        prob_ref[h] = prob
        context = jnp.where(mask, fwd_dot(prob, values_ref[...]), context)
    context_ref[...] = context


def attend(table, key_w, value_w, value_b, queries, own_k, own_v, bias):
    rows, width = queries.shape
    n_table = table.shape[0]
    n_keys = n_table + rows
    steps = width // LANES
    per = LANES // HEAD_DIM
    whole = lambda shape: pl.BlockSpec(shape, lambda i: (0, 0))
    lanes = lambda n: pl.BlockSpec((n, LANES), lambda i: (0, i))
    return pl.pallas_call(
        attend_kernel,
        grid=(steps,),
        in_specs=[
            whole((n_table, width)), lanes(width), lanes(width), lanes(1), lanes(rows), lanes(rows),
            lanes(rows), whole((rows, n_keys)),
        ],
        out_specs=[
            lanes(n_keys), lanes(n_keys), pl.BlockSpec((per, rows, n_keys), lambda i: (i, 0, 0)), lanes(rows),
        ],
        out_shape=[
            jax.ShapeDtypeStruct((n_keys, width), BF),
            jax.ShapeDtypeStruct((n_keys, width), BF),
            jax.ShapeDtypeStruct((HEADS, rows, n_keys), BF),
            jax.ShapeDtypeStruct((rows, width), F32),
        ],
        compiler_params=pltpu.CompilerParams(vmem_limit_bytes=56 * MIB),
        cost_estimate=pl.CostEstimate(
            flops=4 * width * (n_table * width + rows * n_keys), bytes_accessed=10 * MIB,
            transcendentals=HEADS * rows * n_keys,
        ),
    )(table, key_w, value_w, value_b, queries, own_k, own_v, bias)


def middle_kernel(
    resid_ref, context_ref, cot_ref, out_w_ref, up_w_ref, down_w_ref, vec_ref, up_b_ref,
    mixed_ref, context_low_ref, middle_low_ref, act_ref, grad_ffn_ref, grad_pre_ref, grad_attn_ref,
    grad_context_ref, grad_mid_ref, sums_ref, up_sum_ref, slope_ref, total_ref,
):
    hidden = up_w_ref.shape[1]
    tile = 512
    steps = hidden // tile
    out_b, norm_g, norm_s, down_b, final_g, final_s = (vec_ref[i : i + 1] for i in range(6))
    column = lambda v: jnp.sum(v, axis=0, keepdims=True)
    context_low = context_ref[...].astype(BF)
    context_low_ref[...] = context_low
    normed1, inv1 = norm_parts(resid_ref[...] + fwd_dot(context_low, out_w_ref[...]) + out_b)
    middle = normed1 * norm_g + norm_s
    middle_low_ref[...] = middle.astype(BF)
    total_ref[...] = middle + down_b

    def forward(i, carry):
        at = pl.ds(pl.multiple_of(i * tile, tile), tile)
        pre = fwd_dot(middle_low_ref[...], up_w_ref[:, at]) + up_b_ref[:, at]
        cdf = 0.5 * (1.0 + lax.erf(pre * (0.5**0.5)))
        act = (pre * cdf).astype(BF)
        act_ref[:, at] = act
        slope_ref[:, at] = cdf + pre * jnp.exp(-0.5 * pre * pre) * (1.0 / math.sqrt(2 * math.pi))
        total_ref[...] += fwd_dot(act, down_w_ref[at, :])
        return carry

    lax.fori_loop(0, steps, forward, 0)
    normed2, inv2 = norm_parts(total_ref[...])
    mixed_ref[...] = (normed2 * final_g + final_s).astype(BF)
    cot = cot_ref[...].astype(F32)
    grad_final = norm_grad(cot, normed2, inv2, final_g)
    grad_ffn = grad_final.astype(BF)
    grad_ffn_ref[...] = grad_ffn
    total_ref[...] = grad_final

    def backward(i, carry):
        at = pl.ds(pl.multiple_of(i * tile, tile), tile)
        grad_pre = (back_dot(grad_ffn_ref[...], down_w_ref[at, :]) * slope_ref[:, at]).astype(BF)
        grad_pre_ref[:, at] = grad_pre
        up_sum_ref[:, at] = column(grad_pre.astype(F32))
        total_ref[...] += back_dot(grad_pre, up_w_ref[:, at])
        return carry

    lax.fori_loop(0, steps, backward, 0)
    grad_middle = total_ref[...]
    grad_mid = norm_grad(grad_middle, normed1, inv1, norm_g)
    grad_mid_ref[...] = grad_mid
    grad_attn = grad_mid.astype(BF)
    grad_attn_ref[...] = grad_attn
    grad_context_ref[...] = back_dot(grad_attn, out_w_ref[...]).astype(BF)
    sums_ref[0:1] = column(grad_attn.astype(F32))
    sums_ref[1:2] = column(grad_middle * normed1)
    sums_ref[2:3] = column(grad_middle)
    sums_ref[3:4] = column(grad_ffn.astype(F32))
    sums_ref[4:5] = column(cot * normed2)
    sums_ref[5:6] = column(cot)
    sums_ref[6:8] = jnp.zeros((2, sums_ref.shape[1]), F32)


def middle_part(resid, context, cot, out_w, up_w, down_w, vecs, up_b):
    rows, width = resid.shape
    hidden = up_w.shape[1]
    vmem = pl.BlockSpec(memory_space=pltpu.VMEM)
    shape = lambda n, t: jax.ShapeDtypeStruct((rows, n), t)
    return pl.pallas_call(
        middle_kernel,
        in_specs=[vmem] * 8,
        out_specs=[vmem] * 11,
        out_shape=[
            shape(width, BF), shape(width, BF), shape(width, BF), shape(hidden, BF), shape(width, BF),
            shape(hidden, BF), shape(width, BF), shape(width, BF), shape(width, F32),
            jax.ShapeDtypeStruct((8, width), F32), jax.ShapeDtypeStruct((1, hidden), F32),
        ],
        scratch_shapes=[pltpu.VMEM((rows, hidden), F32), pltpu.VMEM((rows, width), F32)],
        compiler_params=pltpu.CompilerParams(vmem_limit_bytes=48 * MIB),
        cost_estimate=pl.CostEstimate(
            flops=4 * rows * width * (2 * hidden + width), bytes_accessed=24 * MIB, transcendentals=2 * rows * hidden
        ),
    )(resid, context, cot, out_w, up_w, down_w, vecs, up_b)


def attend_back_kernel(
    q_ref, keys_ref, values_ref, prob_ref, context_ref, grad_ref, *refs
):
    grad_q_ref, grad_k_ref, grad_v_ref = refs[-3:]
    grad = grad_ref[...]
    grad_f = grad.astype(F32)
    product = grad_f * context_ref[...]
    grad_t = grad_f.T.astype(BF)
    q_t = q_ref[...].astype(F32).T.astype(BF)
    grad_q = jnp.zeros(grad.shape, F32)
    for h in range(LANES // HEAD_DIM):
        mask = head_lanes(grad.shape, h)
        at = slice(h * HEAD_DIM, (h + 1) * HEAD_DIM)
        row_dot = jnp.sum(jnp.where(mask, product, 0.0), axis=-1, keepdims=True)
        grad_prob = back_dot(jnp.where(mask, grad, jnp.zeros_like(grad)), values_ref[...])
        prob = prob_ref[h]
        grad_score = (prob.astype(F32) * (grad_prob - row_dot)).astype(BF)
        grad_v_ref[at] = fwd_dot(grad_t[at], prob).astype(BF)
        grad_k_ref[at] = fwd_dot(q_t[at], grad_score).astype(BF)
        grad_q = jnp.where(mask, fwd_dot(grad_score, keys_ref[...]), grad_q)
    grad_q_ref[...] = (grad_q * HEAD_DIM**-0.5).astype(BF)


def attend_back(queries, keys, values, prob, context, grad_context, after):
    rows, width = queries.shape
    n_keys = keys.shape[0]
    per = LANES // HEAD_DIM
    lanes = lambda n: pl.BlockSpec((n, LANES), lambda i: (0, i))
    return pl.pallas_call(
        attend_back_kernel,
        grid=(width // LANES,),
        in_specs=[
            lanes(rows), lanes(n_keys), lanes(n_keys), pl.BlockSpec((per, rows, n_keys), lambda i: (i, 0, 0)),
            lanes(rows), lanes(rows),
        ]
        + [pl.BlockSpec(memory_space=pl.ANY)] * len(after),
        out_specs=[lanes(rows)] + [pl.BlockSpec((LANES, n_keys), lambda i: (i, 0))] * 2,
        out_shape=[
            jax.ShapeDtypeStruct((rows, width), BF),
            jax.ShapeDtypeStruct((width, n_keys), BF),
            jax.ShapeDtypeStruct((width, n_keys), BF),
        ],
        compiler_params=pltpu.CompilerParams(vmem_limit_bytes=48 * MIB),
        cost_estimate=pl.CostEstimate(
            flops=8 * rows * n_keys * width, bytes_accessed=12 * MIB, transcendentals=0
        ),
    )(queries, keys, values, prob, context, grad_context, *after)


def local(
    tokens, seg_ids, turn_ids, prev_ids, answer_table, query_weight, query_bias,
    key_weight, value_weight, value_bias, out_weight, out_bias, norm_gain, norm_shift,
    up_weight, up_bias, down_weight, down_bias, final_gain, final_shift, cotangent,
):
    rows, width = tokens.shape
    blocks = lax.axis_size("blk")
    grps = lax.axis_size("grp")
    tab = TAB_MAX
    scale = HEAD_DIM ** (-0.5)
    f = lambda v: v.astype(F32)
    is_one = (prev_ids == 1)[:, None]
    answers = f(answer_table)
    resid_in = f(tokens) + jnp.where(is_one, answers[1][None], answers[0][None])
    layer_input = resid_in.astype(BF)
    flags = jnp.concatenate(
        [(seg_ids[:tab] == 0).astype(BF), jnp.zeros((128 - tab,), BF), prev_ids[:tab].astype(BF),
         jnp.zeros((width - 128 - tab,), BF)]
    )[None]
    payload = jnp.concatenate([layer_input[:tab], flags, jnp.zeros((15, width), BF)], axis=0)
    gathered = lax.all_gather(payload, "blk", axis=0, tiled=False)
    table_input = gathered[:, :tab].reshape(blocks * tab, width)
    table_open = gathered[:, tab, :tab].reshape(blocks * tab) > 0.5
    table_prev = gathered[:, tab, 128 : 128 + tab].reshape(blocks * tab)

    qkv_in = jnp.concatenate([table_input, layer_input], axis=0)
    queries = ((fwd_dot(layer_input, query_weight) + f(query_bias)).astype(BF) * scale).astype(BF)
    own_keys = fwd_dot(layer_input, key_weight).astype(BF)
    own_values = (fwd_dot(layer_input, value_weight) + f(value_bias)).astype(BF)
    own_open = (turn_ids[:, None] == turn_ids[None, :]) & (seg_ids != 0)[None, :]
    bias = jnp.concatenate(
        [
            jnp.broadcast_to(jnp.where(table_open, 0.0, far_below)[None], (rows, blocks * tab)),
            jnp.where(own_open, 0.0, far_below),
        ],
        axis=1,
    )
    keys, values, prob, context = attend(
        table_input, key_weight, value_weight, f(value_bias)[None], queries, own_keys, own_values, bias
    )
    n_keys = keys.shape[0]
    vecs = jnp.stack(
        [f(v) for v in (out_bias, norm_gain, norm_shift, down_bias, final_gain, final_shift)] + [jnp.zeros((width,), F32)] * 2
    )
    (
        mixed, context_low, middle_low, act_low, grad_ffn, grad_pre, grad_attn, grad_context, grad_mid_sum,
        sums, up_sum,
    ) = middle_part(
        resid_in, context, cotangent, out_weight, up_weight, down_weight, vecs, f(up_bias)[None]
    )

    core_bit = lax.axis_index("grp") & 1
    x_bit = lax.axis_index("grp") >> 1
    own = lax.axis_index("blk")
    y_bit, z_own = own & 1, own >> 1
    planes = blocks // 2

    def swap_grp(value, mask):
        return lax.ppermute(value, "grp", [(i, i ^ mask) for i in range(grps)])

    def swap_blk(value, mask):
        return lax.ppermute(value, "blk", [(i, i ^ mask) for i in range(blocks)])

    def take(value, index, axis):
        return lax.dynamic_index_in_dim(value, index, axis, keepdims=False)

    def half(value, index):
        size = value.shape[1] // 2
        return lax.dynamic_slice_in_dim(value, index * size, size, 1)

    def add(first, second):
        return (f(first) + f(second)).astype(BF)

    def core_stage(lhs, rhs):
        sent = swap_grp(outer_sum(lhs, half(rhs, 1 - core_bit)).astype(BF), 1)
        return (outer_sum(lhs, half(rhs, core_bit)) + f(sent)).astype(BF)

    def y_split(value):
        return take(value, y_bit, 1), take(value, 1 - y_bit, 1)

    def y_stage(value):
        kept, sent = y_split(value)
        return add(kept, swap_blk(sent, 1))

    def z_stage(value):
        total = f(take(value, z_own, 0))
        for k in range(1, planes):
            total = total + f(swap_blk(take(value, z_own ^ k, 0), 2 * k))
        return total.astype(BF)

    def x_split(value, axis):
        return take(value, x_bit, axis), take(value, 1 - x_bit, axis)

    def join(value, other, bit, axis):
        first = jnp.where(bit == 0, value, other)
        second = jnp.where(bit == 0, other, value)
        return jnp.concatenate([first, second], axis=axis)

    n_out = width // blocks
    ff_out = up_weight.shape[1] // blocks
    half_width = width // 2

    down_part = core_stage(act_low, grad_ffn).reshape(planes, 2, ff_out, half_width)
    up_part = core_stage(middle_low, grad_pre).reshape(planes, 2, 2, n_out // 2, 2 * width)
    down_kept, down_sent = y_split(down_part)
    up_kept, up_sent = x_split(up_part, 2)
    grad_queries, grad_keys_t, grad_values_t = attend_back(
        queries, keys, values, prob, context, grad_context, (down_sent, up_sent)
    )
    down_part = add(down_kept, swap_blk(down_sent, 1)).reshape(planes, 2, ff_out // 2, half_width)
    down_kept, down_sent = x_split(down_part, 1)
    down_part = z_stage(add(down_kept, swap_grp(down_sent, 2)))
    down_part = join(down_part, swap_grp(down_part, 2), x_bit, 0)
    up_part = add(up_kept, swap_grp(up_sent, 2))
    up_part = z_stage(y_stage(up_part))
    up_part = join(up_part, swap_grp(up_part, 2), x_bit, 0)
    out_down = f(join(down_part, swap_grp(down_part, 1), core_bit, 1))
    out_up = f(join(up_part, swap_grp(up_part, 1), core_bit, 1))

    half_rows = lambda value, index: lax.dynamic_slice_in_dim(value, index * half_width, half_width, 0)
    mix = lambda left, right, dims: lax.dot_general(left, right, (dims, ((), ())), preferred_element_type=F32)
    grad_kv_in = mix(grad_keys_t, key_weight, ((0,), (1,))) + mix(grad_values_t, value_weight, ((0,), (1,)))
    grad_table = grad_kv_in[: blocks * tab]
    grad_input_local = grad_mid_sum + back_dot(grad_queries, query_weight) + grad_kv_in[blocks * tab :]
    all_prev = jnp.concatenate([table_prev, prev_ids.astype(BF)])
    all_grads = jnp.concatenate([grad_table, grad_input_local], axis=0)
    total_sum = jnp.sum(all_grads, axis=0, keepdims=True)
    one_sum = jnp.sum(jnp.where(all_prev[:, None] > 0.5, all_grads, 0.0), axis=0, keepdims=True)
    vectors = jnp.concatenate(
        [
            total_sum - one_sum,
            one_sum,
            jnp.sum(f(grad_queries), axis=0, keepdims=True),
            jnp.sum(f(grad_values_t), axis=1)[None],
            sums[:6],
            up_sum.reshape(-1, width),
            jnp.zeros((2, width), F32),
        ],
        axis=0,
    )
    n_vec = vectors.shape[0]

    def pack(value):
        high = value.astype(BF)
        return jnp.concatenate([high, (value - f(high)).astype(BF)], axis=0)

    def unpack(value):
        return f(value[:n_vec]) + f(value[n_vec:])

    def pair_half(index):
        return jnp.concatenate(
            [outer_sum(layer_input, half(grad_queries, index)), mix(qkv_in, half_rows(grad_keys_t, index), ((0,), (1,)))],
            axis=1,
        )

    def pair_half_two(index):
        return jnp.concatenate(
            [mix(qkv_in, half_rows(grad_values_t, index), ((0,), (1,))), outer_sum(context_low, half(grad_attn, index))],
            axis=1,
        )

    sent = swap_grp(jnp.concatenate([pair_half(1 - core_bit).astype(BF), pack(vectors)], axis=0), 1)
    first = (pair_half(core_bit) + f(sent[:width])).astype(BF)
    vectors = vectors + unpack(sent[width:])
    sent = swap_grp(pair_half_two(1 - core_bit).astype(BF), 1)
    second = (pair_half_two(core_bit) + f(sent)).astype(BF)

    first = first.reshape(planes, 2, 2, n_out // 2, width)
    second = jnp.concatenate(
        [second.reshape(planes, 2, n_out, width), grad_table.astype(BF).reshape(planes, 2, tab, width)], axis=2
    )
    rows_of = planes * n_out
    sent = swap_grp(
        jnp.concatenate([take(first, 1 - x_bit, 2).reshape(rows_of, width), pack(vectors)], axis=0), 2
    )
    first = add(take(first, x_bit, 2).reshape(rows_of, width), sent[:rows_of]).reshape(
        planes, 2, n_out // 2, width
    )
    vectors = vectors + unpack(sent[rows_of:])
    second = y_stage(second)
    rows_of = planes * n_out // 2
    sent = swap_blk(
        jnp.concatenate([take(first, 1 - y_bit, 1).reshape(rows_of, width), pack(vectors)], axis=0), 1
    )
    first = add(take(first, y_bit, 1).reshape(rows_of, width), sent[:rows_of]).reshape(
        planes, n_out // 2, width
    )
    vectors = vectors + unpack(sent[rows_of:])
    table_kept = second[:, n_out:]
    second = second[:, :n_out].reshape(planes, 2, n_out // 2, width)
    second_kept, second_sent = x_split(second, 1)
    second = add(second_kept, swap_grp(second_sent, 2))
    second = z_stage(jnp.concatenate([second, table_kept], axis=1))
    rows_of = n_out // 2
    total = f(take(first, z_own, 0))
    packed = pack(vectors)
    for k in range(1, planes):
        sent = swap_blk(jnp.concatenate([take(first, z_own ^ k, 0), packed], axis=0), 2 * k)
        total = total + f(sent[:rows_of])
        vectors = vectors + unpack(sent[rows_of:])
    first = total.astype(BF)
    table_share = second[rows_of:]
    both = jnp.concatenate([first, second[:rows_of]], axis=1)
    both = join(both, swap_grp(both, 2), x_bit, 0)
    other = swap_grp(both, 1)
    square = []
    for index in range(4):
        at = (slice(None), slice(index * half_width, (index + 1) * half_width))
        square.append(join(both[at], other[at], core_bit, 1))
    mine = lax.dynamic_slice_in_dim(vectors[:10], own * n_out, n_out, 1)
    up_bias_out = lax.dynamic_slice_in_dim(vectors[10:14].reshape(-1), own * ff_out, ff_out, 0)
    grad_input = grad_input_local.at[:tab].add(f(table_share))
    return (
        mixed,
        grad_input,
        mine[:2],
        f(square[0]),
        mine[2],
        f(square[1]),
        f(square[2]),
        mine[3],
        f(square[3]),
        mine[4],
        mine[5],
        mine[6],
        out_up,
        up_bias_out,
        out_down,
        mine[7],
        mine[8],
        mine[9],
    )


def solution(mesh):
    both = ("grp", "blk")
    placed = (P(both, None), P(both), P(both), P(both)) + (P(),) * 16 + (P(both, None),)
    vec, mat = P("blk"), P("blk", None)
    return jax.shard_map(
        local,
        mesh=mesh,
        in_specs=placed,
        out_specs=(
            P(both, None), P(both, None), P(None, "blk"), mat, vec, mat, mat, vec, mat, vec,
            vec, vec, mat, vec, mat, vec, vec, vec,
        ),
        check_vma=False,
    )
```

```python
import math

import jax
import jax.numpy as jnp
from jax import lax
from jax.experimental import pallas as pl
from jax.experimental.pallas import tpu as pltpu
from jax.sharding import PartitionSpec as P

HEADS = 12
HEAD_DIM = 64
TAB_MAX = 64
LANES = 256
far_below = -1e30
BF = jnp.bfloat16
F32 = jnp.float32
MIB = 1 << 20


def outer_sum(left, right):
    return lax.dot_general(left, right, (((0,), (0,)), ((), ())), preferred_element_type=F32)


def back_dot(left, right):
    return lax.dot_general(left, right, (((1,), (1,)), ((), ())), preferred_element_type=F32)


def fwd_dot(left, right):
    return jnp.dot(left, right, preferred_element_type=F32)


def norm_parts(values):
    centred = values - jnp.mean(values, axis=-1, keepdims=True)
    spread = jnp.mean(centred * centred, axis=-1, keepdims=True)
    inv = lax.rsqrt(spread + 1e-06)
    return centred * inv, inv


def norm_grad(grad, normed, inv, gain):
    scaled = grad * gain
    return inv * (
        scaled
        - jnp.mean(scaled, axis=-1, keepdims=True)
        - normed * jnp.mean(scaled * normed, axis=-1, keepdims=True)
    )


def head_lanes(shape, index):
    lane = lax.broadcasted_iota(jnp.int32, shape, len(shape) - 1)
    return (lane >= index * HEAD_DIM) & (lane < (index + 1) * HEAD_DIM)


def column_of(row):
    return jnp.broadcast_to(row, (128, row.shape[1])).T[:, :1]


def entry_kernel(tokens_ref, seg_ref, prev_ref, answer_ref, payload_ref, input_ref):
    tab = TAB_MAX
    prev = prev_ref[...].astype(F32)[None]
    low = residual(tokens_ref, prev, answer_ref).astype(BF)
    input_ref[...] = low
    payload_ref[:tab] = low[:tab]
    payload_ref[tab:] = jnp.zeros((16, low.shape[1]), BF)
    lane = lax.broadcasted_iota(jnp.int32, (1, 128), 1)

    def twice(row):
        row = row[:, :128]
        return jnp.where(lane < tab, row, pltpu.roll(row, tab, 1))

    is_open = twice(jnp.where(seg_ref[...] == 0, 1.0, 0.0)[None])
    both = jnp.concatenate([is_open, twice(prev)], axis=1)
    payload_ref[tab:, :256] = jnp.broadcast_to(both, (16, 256)).astype(BF)


def residual(tokens_ref, prev, answer_ref):
    answers = answer_ref[...].astype(F32)
    return tokens_ref[...].astype(F32) + jnp.where(column_of(prev) == 1.0, answers[1:2], answers[0:1])


def entry(tokens, seg, prev, answers):
    rows, width = tokens.shape
    vmem = pl.BlockSpec(memory_space=pltpu.VMEM)
    return pl.pallas_call(
        entry_kernel,
        in_specs=[vmem] * 4,
        out_specs=[vmem] * 2,
        out_shape=[jax.ShapeDtypeStruct((TAB_MAX + 16, width), BF), jax.ShapeDtypeStruct((rows, width), BF)],
        compiler_params=pltpu.CompilerParams(vmem_limit_bytes=12 * MIB),
    )(tokens, seg, prev, answers)


def own_kernel(
    input_ref, query_w_ref, key_w_ref, value_w_ref, query_b_ref, value_b_ref, seg_ref, turn_ref,
    q_ref, k_ref, v_ref, bias_ref, value_row_ref,
):
    low = input_ref[...]
    query = fwd_dot(low, query_w_ref[...]) + query_b_ref[...].astype(F32)[None]
    q_ref[...] = (query.astype(BF).astype(F32) * HEAD_DIM**-0.5).astype(BF)
    k_ref[...] = fwd_dot(low, key_w_ref[...]).astype(BF)
    value_b = value_b_ref[...].astype(F32)[None]
    value_row_ref[...] = value_b
    v_ref[...] = (fwd_dot(low, value_w_ref[...]) + value_b).astype(BF)
    turn = turn_ref[...].astype(F32)[None]
    seg = seg_ref[...].astype(F32)[None]
    same = (column_of(turn) == turn) & (seg != 0.0)
    bias_ref[...] = jnp.where(same, 0.0, far_below)


def own_part(layer_input, query_w, key_w, value_w, query_b, value_b, seg, turn):
    rows, width = layer_input.shape
    vmem = pl.BlockSpec(memory_space=pltpu.VMEM)
    return pl.pallas_call(
        own_kernel,
        in_specs=[vmem] * 8,
        out_specs=[vmem] * 5,
        out_shape=[jax.ShapeDtypeStruct((rows, width), BF)] * 3
        + [jax.ShapeDtypeStruct((rows, rows), F32), jax.ShapeDtypeStruct((1, width), F32)],
        compiler_params=pltpu.CompilerParams(vmem_limit_bytes=20 * MIB),
        cost_estimate=pl.CostEstimate(flops=900_000_000, bytes_accessed=5 * MIB, transcendentals=0),
    )(layer_input, query_w, key_w, value_w, query_b, value_b, seg, turn)


def attend_kernel(
    input_ref, key_w_ref, value_w_ref, value_b_ref, q_ref, own_k_ref, own_v_ref, own_bias_ref, *refs
):
    *slots, keys_ref, values_ref, prob_ref, context_ref, x_t_ref, prev_ref, table_ref, bias_ref = refs
    n_table = table_ref.shape[0]
    tab = TAB_MAX

    @pl.when(pl.program_id(0) == 0)
    def _():
        lane = lax.broadcasted_iota(jnp.int32, (1, 128), 1)
        for i, slot in enumerate(slots):
            table_ref[i * tab : (i + 1) * tab] = slot[:tab]
        for i in range(0, len(slots), 2):
            marks = jnp.where(
                lax.broadcasted_iota(jnp.int32, (16, 256), 1) % 128 < tab,
                slots[i][tab:, :256].astype(F32), slots[i + 1][tab:, :256].astype(F32),
            )
            at = slice(i * tab, (i + 2) * tab)
            closed = jnp.where(marks[:1, :128] > 0.5, 0.0, far_below)
            bias_ref[:, at] = jnp.broadcast_to(closed, (bias_ref.shape[0], 128))
            prev_ref[:, at] = marks[:8, 128:]
        bias_ref[:, n_table:] = own_bias_ref[...]
        x_t_ref[:, :n_table] = table_ref[...].T
        x_t_ref[:, n_table:] = input_ref[...].T

    table = table_ref[...]
    keys_ref[:n_table] = fwd_dot(table, key_w_ref[...]).astype(BF)
    values_ref[:n_table] = (fwd_dot(table, value_w_ref[...]) + value_b_ref[...]).astype(BF)
    keys_ref[n_table:] = own_k_ref[...]
    values_ref[n_table:] = own_v_ref[...]
    queries = q_ref[...]
    context = jnp.zeros(context_ref.shape, F32)
    for h in range(queries.shape[1] // HEAD_DIM):
        mask = head_lanes(queries.shape, h)
        picked = jnp.where(mask, queries, jnp.zeros_like(queries))
        scores = back_dot(picked, keys_ref[...]) + bias_ref[...]
        top = jnp.max(scores, axis=-1, keepdims=True)
        weights = jnp.exp(scores - top)
        prob = (weights * (1.0 / jnp.sum(weights, axis=-1, keepdims=True))).astype(BF)
        prob_ref[h] = prob
        context = jnp.where(mask, fwd_dot(prob, values_ref[...]), context)
    context_ref[...] = context


def vmem_limit(n_keys, small):
    return (small if n_keys <= 1024 else 60) * MIB


def attend(slots, layer_input, key_w, value_w, value_b, queries, own_k, own_v, own_bias):
    rows, width = queries.shape
    n_table = len(slots) * TAB_MAX
    n_keys = n_table + rows
    group = LANES if n_keys <= 1024 else LANES // 2
    per = group // HEAD_DIM
    steady = {} if n_keys <= 1024 else {"pipeline_mode": pl.Buffered(1)}
    whole = lambda shape: pl.BlockSpec(shape, lambda i: (0, 0), **steady)
    lanes = lambda n: pl.BlockSpec((n, group), lambda i: (0, i))
    return pl.pallas_call(
        attend_kernel,
        grid=(width // group,),
        in_specs=[
            whole((rows, width)), lanes(width), lanes(width), lanes(1), lanes(rows), lanes(rows), lanes(rows),
            whole((rows, rows)),
        ]
        + [whole(slot.shape) for slot in slots],
        out_specs=[
            lanes(n_keys), lanes(n_keys), pl.BlockSpec((per, rows, n_keys), lambda i: (i, 0, 0)), lanes(rows),
            whole((width, n_keys)), whole((8, n_table)),
        ],
        out_shape=[
            jax.ShapeDtypeStruct((n_keys, width), BF),
            jax.ShapeDtypeStruct((n_keys, width), BF),
            jax.ShapeDtypeStruct((HEADS, rows, n_keys), BF),
            jax.ShapeDtypeStruct((rows, width), F32),
            jax.ShapeDtypeStruct((width, n_keys), BF),
            jax.ShapeDtypeStruct((8, n_table), F32),
        ],
        scratch_shapes=[pltpu.VMEM((n_table, width), BF), pltpu.VMEM((rows, n_keys), F32)],
        compiler_params=pltpu.CompilerParams(vmem_limit_bytes=vmem_limit(n_keys, 56)),
        cost_estimate=pl.CostEstimate(flops=100_000_000, bytes_accessed=1 * MIB, transcendentals=0),
    )(layer_input, key_w, value_w, value_b, queries, own_k, own_v, own_bias, *slots)


def middle_kernel(
    tokens_ref, prev_ref, answer_ref, context_ref, cot_ref, out_w_any, up_w_any, down_w_any, up_b_1d_ref, *refs
):
    biases, refs = refs[:6], refs[6:]
    mixed_ref, context_t_ref, middle_t_ref, act_t_ref, grad_ffn_ref, grad_pre_ref, grad_attn_ref = refs[:7]
    grad_context_ref, grad_mid_ref, sums_ref, up_sum_ref, slope_ref, total_ref, middle_low_ref = refs[7:14]
    out_w_ref, up_w_ref, down_w_ref, up_b_ref, sems = refs[14:]
    copies = [
        pltpu.make_async_copy(source, target, sems.at[i])
        for i, (source, target) in enumerate(
            ((out_w_any, out_w_ref), (up_w_any, up_w_ref), (down_w_any, down_w_ref))
        )
    ]
    for copy in copies:
        copy.start()
    hidden = up_w_ref.shape[1]
    tile = 512
    steps = hidden // tile
    out_b, norm_g, norm_s, down_b, final_g, final_s = (ref[...].astype(F32)[None] for ref in biases)
    up_b_ref[...] = up_b_1d_ref[...].astype(F32)[None]
    resid = residual(tokens_ref, prev_ref[...].astype(F32)[None], answer_ref)
    column = lambda v: jnp.sum(v, axis=0, keepdims=True)
    context_low = context_ref[...].astype(BF)
    context_t_ref[...] = context_low.T
    copies[0].wait()
    normed1, inv1 = norm_parts(resid + fwd_dot(context_low, out_w_ref[...]) + out_b)
    middle = normed1 * norm_g + norm_s
    middle_low = middle.astype(BF)
    middle_low_ref[...] = middle_low
    middle_t_ref[...] = middle_low.T
    total_ref[...] = middle + down_b
    copies[1].wait()
    copies[2].wait()

    def forward(i, carry):
        at = pl.ds(pl.multiple_of(i * tile, tile), tile)
        pre = fwd_dot(middle_low_ref[...], up_w_ref[:, at]) + up_b_ref[:, at]
        cdf = 0.5 * (1.0 + lax.erf(pre * (0.5**0.5)))
        act = (pre * cdf).astype(BF)
        act_t_ref[at, :] = act.T
        slope_ref[:, at] = cdf + pre * jnp.exp(-0.5 * pre * pre) * (1.0 / math.sqrt(2 * math.pi))
        total_ref[...] += fwd_dot(act, down_w_ref[at, :])
        return carry

    lax.fori_loop(0, steps, forward, 0)
    normed2, inv2 = norm_parts(total_ref[...])
    mixed_ref[...] = (normed2 * final_g + final_s).astype(BF)
    cot = cot_ref[...].astype(F32)
    grad_final = norm_grad(cot, normed2, inv2, final_g)
    grad_ffn = grad_final.astype(BF)
    grad_ffn_ref[...] = grad_ffn
    total_ref[...] = grad_final

    def backward(i, carry):
        at = pl.ds(pl.multiple_of(i * tile, tile), tile)
        grad_pre = (back_dot(grad_ffn_ref[...], down_w_ref[at, :]) * slope_ref[:, at]).astype(BF)
        grad_pre_ref[:, at] = grad_pre
        up_sum_ref[:, at] = column(grad_pre.astype(F32))
        total_ref[...] += back_dot(grad_pre, up_w_ref[:, at])
        return carry

    lax.fori_loop(0, steps, backward, 0)
    grad_middle = total_ref[...]
    grad_mid = norm_grad(grad_middle, normed1, inv1, norm_g)
    grad_mid_ref[...] = grad_mid
    grad_attn = grad_mid.astype(BF)
    grad_attn_ref[...] = grad_attn
    grad_context_ref[...] = back_dot(grad_attn, out_w_ref[...]).astype(BF)
    sums_ref[0:1] = column(grad_attn.astype(F32))
    sums_ref[1:2] = column(grad_middle * normed1)
    sums_ref[2:3] = column(grad_middle)
    sums_ref[3:4] = column(grad_ffn.astype(F32))
    sums_ref[4:5] = column(cot * normed2)
    sums_ref[5:6] = column(cot)
    sums_ref[6:8] = jnp.zeros((2, sums_ref.shape[1]), F32)


def middle_part(tokens, prev, answers, context, cot, out_w, up_w, down_w, up_b, *biases):
    rows, width = tokens.shape
    hidden = up_w.shape[1]
    vmem = pl.BlockSpec(memory_space=pltpu.VMEM)
    shape = lambda n, t: jax.ShapeDtypeStruct((rows, n), t)
    turned = lambda n: jax.ShapeDtypeStruct((n, rows), BF)
    return pl.pallas_call(
        middle_kernel,
        in_specs=[vmem] * 5 + [pl.BlockSpec(memory_space=pl.ANY)] * 3 + [vmem] * 7,
        out_specs=[vmem] * 11,
        out_shape=[
            shape(width, BF), turned(width), turned(width), turned(hidden), shape(width, BF),
            shape(hidden, BF), shape(width, BF), shape(width, BF), shape(width, F32),
            jax.ShapeDtypeStruct((8, width), F32), jax.ShapeDtypeStruct((1, hidden), F32),
        ],
        scratch_shapes=[
            pltpu.VMEM((rows, hidden), F32), pltpu.VMEM((rows, width), F32), pltpu.VMEM((rows, width), BF),
            pltpu.VMEM(out_w.shape, BF), pltpu.VMEM(up_w.shape, BF), pltpu.VMEM(down_w.shape, BF),
            pltpu.VMEM((1, hidden), F32), pltpu.SemaphoreType.DMA((3,)),
        ],
        compiler_params=pltpu.CompilerParams(vmem_limit_bytes=56 * MIB),
        cost_estimate=pl.CostEstimate(
            flops=4 * rows * width * (2 * hidden + width), bytes_accessed=24 * MIB, transcendentals=2 * rows * hidden
        ),
    )(tokens, prev, answers, context, cot, out_w, up_w, down_w, up_b, *biases)


def attend_back_kernel(
    q_ref, keys_ref, values_ref, prob_ref, context_ref, grad_ref, *refs
):
    grad_q_ref, grad_k_ref, grad_v_ref = refs[-3:]
    grad = grad_ref[...]
    grad_f = grad.astype(F32)
    product = grad_f * context_ref[...]
    grad_t = grad_f.T.astype(BF)
    q_t = q_ref[...].astype(F32).T.astype(BF)
    grad_q = jnp.zeros(grad.shape, F32)
    for h in range(grad.shape[1] // HEAD_DIM):
        mask = head_lanes(grad.shape, h)
        at = slice(h * HEAD_DIM, (h + 1) * HEAD_DIM)
        row_dot = jnp.sum(jnp.where(mask, product, 0.0), axis=-1, keepdims=True)
        grad_prob = back_dot(jnp.where(mask, grad, jnp.zeros_like(grad)), values_ref[...])
        prob = prob_ref[h]
        grad_score = (prob.astype(F32) * (grad_prob - row_dot)).astype(BF)
        grad_v_ref[at] = fwd_dot(grad_t[at], prob).astype(BF)
        grad_k_ref[at] = fwd_dot(q_t[at], grad_score).astype(BF)
        grad_q = jnp.where(mask, fwd_dot(grad_score, keys_ref[...]), grad_q)
    grad_q_ref[...] = (grad_q * HEAD_DIM**-0.5).astype(BF)


def attend_back(queries, keys, values, prob, context, grad_context, after):
    rows, width = queries.shape
    n_keys = keys.shape[0]
    group = LANES if n_keys <= 1024 else LANES // 2
    per = group // HEAD_DIM
    lanes = lambda n: pl.BlockSpec((n, group), lambda i: (0, i))
    return pl.pallas_call(
        attend_back_kernel,
        grid=(width // group,),
        in_specs=[
            lanes(rows), lanes(n_keys), lanes(n_keys), pl.BlockSpec((per, rows, n_keys), lambda i: (i, 0, 0)),
            lanes(rows), lanes(rows),
        ]
        + [pl.BlockSpec(memory_space=pl.ANY)] * len(after),
        out_specs=[lanes(rows)] + [pl.BlockSpec((group, n_keys), lambda i: (i, 0))] * 2,
        out_shape=[
            jax.ShapeDtypeStruct((rows, width), BF),
            jax.ShapeDtypeStruct((width, n_keys), BF),
            jax.ShapeDtypeStruct((width, n_keys), BF),
        ],
        compiler_params=pltpu.CompilerParams(vmem_limit_bytes=vmem_limit(n_keys, 20)),
        cost_estimate=pl.CostEstimate(flops=100_000_000, bytes_accessed=1 * MIB, transcendentals=0),
    )(queries, keys, values, prob, context, grad_context, *after)


def core_lanes(pos_ref, own, size):
    core = pos_ref[0] if own else 1 - pos_ref[0]
    return pl.ds(pl.multiple_of(core * size, 128), size)


def down_values(own, pos_ref, act_t_ref, context_t_ref, grad_ffn_ref, grad_attn_ref, blocks, store):
    half = grad_ffn_ref.shape[1] // 2
    at = core_lanes(pos_ref, own, half)
    grad_ffn = grad_ffn_ref[:, at]
    size = act_t_ref.shape[0] // blocks
    for b in range(blocks):
        store(b, 0, fwd_dot(act_t_ref[b * size : (b + 1) * size], grad_ffn))
    out = fwd_dot(context_t_ref[...], grad_attn_ref[:, at])
    small = out.shape[0] // blocks
    for b in range(blocks):
        store(b, size, out[b * small : (b + 1) * small])


def up_values(own, pos_ref, middle_t_ref, grad_pre_ref, blocks, store):
    half = grad_pre_ref.shape[1] // 2
    piece = middle_t_ref.shape[0] // 2
    small = middle_t_ref.shape[0] // blocks
    core = pos_ref[0] if own else 1 - pos_ref[0]
    for p in range(half // piece):
        at = pl.ds(pl.multiple_of(core * half + p * piece, 128), piece)
        value = fwd_dot(middle_t_ref[...], grad_pre_ref[:, at])
        for b in range(blocks):
            store(b, p * small, value[b * small : (b + 1) * small])


def qkv_values(own, pos_ref, x_t_ref, grad_q_ref, grad_k_ref, grad_v_ref, blocks, store):
    half = grad_q_ref.shape[1] // 2
    n_table = x_t_ref.shape[1] - grad_q_ref.shape[0]
    small = x_t_ref.shape[0] // blocks
    at = core_lanes(pos_ref, own, half)
    core = pos_ref[0] if own else 1 - pos_ref[0]
    rows = pl.ds(pl.multiple_of(core * half, 128), half)
    values = (
        fwd_dot(x_t_ref[:, n_table:], grad_q_ref[:, at]),
        back_dot(x_t_ref[...], grad_k_ref[rows, :]),
        back_dot(x_t_ref[...], grad_v_ref[rows, :]),
    )
    for i, value in enumerate(values):
        for b in range(blocks):
            store(b, i * small, value[b * small : (b + 1) * small])


def send_kernel(make, n_in, blocks, *refs):
    pos_ref, out_ref = refs[0], refs[-1]

    def store(b, first, value):
        out_ref[b, first : first + value.shape[0]] = value.astype(BF)

    make(False, pos_ref, *refs[1 : 1 + n_in], blocks, store)


def pick(bit, first, second):
    return jnp.where(bit == 0, first, second)


def keep_down_kernel(
    blocks, pos_ref, act_t_ref, context_t_ref, grad_ffn_ref, grad_attn_ref, got_ref,
    kept_ref, sent_ref, z_kept_ref, z_sent_ref,
):
    small = context_t_ref.shape[0] // blocks
    held = {}

    def z_store(b, first, value):
        y, low_z, high_z = b % 2, b // 2 % 2, b // 4
        if low_z == 0:
            held[b, first] = value
        else:
            rows = slice((high_z * 2 + y) * 2 * small + first, (high_z * 2 + y) * 2 * small + first + small)
            pair = (held[b - 2, first], value)
            z_kept_ref[rows] = pick(pos_ref[3], *pair)
            z_sent_ref[rows] = pick(pos_ref[3], *pair[::-1])

    def store(b, first, value):
        value = (value + got_ref[b, first : first + value.shape[0]].astype(F32)).astype(BF)
        if first == 0:
            part = (value.shape[0] - small) // 2
            low, high = value[small : small + part], value[small + part :]
            rows = slice(b * part, (b + 1) * part)
            kept_ref[rows] = pick(pos_ref[1], low, high)
            sent_ref[rows] = pick(pos_ref[1], high, low)
            z_store(b, 0, value[:small])
        else:
            z_store(b, small, value)

    down_values(True, pos_ref, act_t_ref, context_t_ref, grad_ffn_ref, grad_attn_ref, blocks, store)


def keep_up_kernel(blocks, pos_ref, middle_t_ref, grad_pre_ref, got_ref, *outs):
    kept_ref, sent_ref = outs[:2]
    size = grad_pre_ref.shape[1] // blocks
    held = {}

    def store(b, first, value):
        rows = slice(first, first + value.shape[0])
        value = (value + got_ref[b, rows].astype(F32)).astype(BF)
        if b % 2 == 0:
            held[0] = value
        else:
            rows = slice(b // 2 * size + first, b // 2 * size + first + value.shape[0])
            kept_ref[rows] = pick(pos_ref[2], held[0], value)
            sent_ref[rows] = pick(pos_ref[2], value, held[0])

    up_values(True, pos_ref, middle_t_ref, grad_pre_ref, blocks, store)


def pack(value):
    high = value.astype(BF)
    return jnp.concatenate([high, (value - high.astype(F32)).astype(BF)], axis=0)


def unpack(value):
    half = value.shape[0] // 2
    return value[:half].astype(F32) + value[half:].astype(F32)


def keep_qkv_kernel(
    blocks, pos_ref, x_t_ref, grad_q_ref, grad_k_ref, grad_v_ref, got_ref, table_ref, vec_ref, vec_got_ref, *outs
):
    first_kept_ref, first_sent_ref, kept_ref, sent_ref, vec_out_ref = outs
    small = x_t_ref.shape[0] // blocks
    planes = blocks // 2
    held = {}

    def store(b, first, value):
        value = (value + got_ref[b, first : first + small].astype(F32)).astype(BF)
        held[b, first] = value
        if first == small:
            query = held.pop((b, 0))
            rows = slice(b * small, (b + 1) * small)
            first_kept_ref[rows] = pick(pos_ref[1], query, value)
            first_sent_ref[rows] = pick(pos_ref[1], value, query)
        if first == 2 * small and b % 2 == 1:
            rows = slice(b // 2 * small, (b // 2 + 1) * small)
            kept_ref[rows] = pick(pos_ref[2], held[b - 1, first], value)
            sent_ref[rows] = pick(pos_ref[2], value, held[b - 1, first])

    qkv_values(True, pos_ref, x_t_ref, grad_q_ref, grad_k_ref, grad_v_ref, blocks, store)
    vec = vec_ref[...] + unpack(vec_got_ref[...])
    vec_out_ref[...] = vec
    first_sent_ref[blocks * small :] = pack(vec)
    sent_ref[planes * small :] = table_ref[...]


def inputs_kernel(
    blocks, grad_q_ref, grad_k_ref, grad_v_ref, query_w_ref, key_w_ref, value_w_ref, grad_mid_ref, prev_ref,
    table_prev_ref, sums_ref, up_sum_ref, *refs
):
    table_kept_ref, table_sent_ref, grad_ref, vec_ref, packed_ref = refs[-5:]
    tab = TAB_MAX
    n_table = blocks * tab
    rows, width = grad_q_ref.shape
    half = width // 2
    own = fwd_dot(key_w_ref[...], grad_k_ref[:, n_table:]) + fwd_dot(value_w_ref[...], grad_v_ref[:, n_table:])
    grad = grad_mid_ref[...] + back_dot(grad_q_ref[...], query_w_ref[...]) + own.T
    grad_ref[...] = grad
    is_one = column_of(prev_ref[...].astype(F32)[None]) == 1.0
    one_sum = jnp.sum(jnp.where(is_one, grad, 0.0), axis=0, keepdims=True)
    zero_sum = jnp.sum(jnp.where(is_one, 0.0, grad), axis=0, keepdims=True)
    step = min(n_table, 512)
    row = lax.broadcasted_iota(jnp.int32, (8, step), 0)
    for first in range(0, n_table, step):
        at = slice(first, first + step)
        part = (fwd_dot(key_w_ref[...], grad_k_ref[:, at]) + fwd_dot(value_w_ref[...], grad_v_ref[:, at])).astype(BF)
        marks = table_prev_ref[:, at]
        marks = jnp.where(row == 0, marks, 1.0 - marks).astype(BF)
        table_sums = back_dot(marks, part)
        one_sum += table_sums[0:1]
        zero_sum += table_sums[1:2]
        for j in range(step // 128):
            pair = part[:, j * 128 : (j + 1) * 128].T
            slot = first // 128 + j
            for k, ref in enumerate((table_kept_ref, table_sent_ref)):
                for side in range(2):
                    ref[(slot * 2 + side) * tab : (slot * 2 + side + 1) * tab] = pair[
                        k * tab : (k + 1) * tab, side * half : (side + 1) * half
                    ]
    ones = jnp.ones((8, grad_v_ref.shape[1]), BF)
    lines = [
        zero_sum,
        one_sum,
        jnp.sum(grad_q_ref[...].astype(F32), axis=0, keepdims=True),
        back_dot(ones, grad_v_ref[...])[0:1],
    ]
    lines += [sums_ref[i : i + 1] for i in range(6)]
    lines += [up_sum_ref[:, i * width : (i + 1) * width] for i in range(up_sum_ref.shape[1] // width)]
    vec_ref[...] = jnp.zeros(vec_ref.shape, F32)
    for i, line in enumerate(lines):
        for side in range(2):
            vec_ref[side * 16 + i : side * 16 + i + 1] = line[:, side * half : (side + 1) * half]
    packed_ref[...] = pack(vec_ref[...])


def input_grads(blocks, grad_q, grad_k, grad_v, query_w, key_w, value_w, grad_mid, prev, table_prev, sums, up_sum, after):
    rows, width = grad_q.shape
    n_half = blocks * TAB_MAX
    vmem = pl.BlockSpec(memory_space=pltpu.VMEM)
    args = (grad_q, grad_k, grad_v, query_w, key_w, value_w, grad_mid, prev, table_prev, sums, up_sum)
    return pl.pallas_call(
        lambda *refs: inputs_kernel(blocks, *refs),
        in_specs=[vmem] * len(args) + [pl.BlockSpec(memory_space=pl.ANY)] * len(after),
        out_specs=[vmem] * 5,
        out_shape=[
            jax.ShapeDtypeStruct((n_half, width // 2), BF),
            jax.ShapeDtypeStruct((n_half, width // 2), BF),
            jax.ShapeDtypeStruct((rows, width), F32),
            jax.ShapeDtypeStruct((32, width // 2), F32),
            jax.ShapeDtypeStruct((64, width // 2), BF),
        ],
        compiler_params=pltpu.CompilerParams(vmem_limit_bytes=(20 if blocks <= 8 else 56) * MIB),
        cost_estimate=pl.CostEstimate(flops=100_000_000, bytes_accessed=1 * MIB, transcendentals=0),
    )(*args, *after)


def combine(pos, items, after=()):
    width = items[0][1].shape[1]
    gots, shapes, heights, places = [], [], {}, []
    for kind, kept, got, first, outer, inner, bit, message in items:
        if not any(got is g for g in gots):
            gots.append(got)
        rows = kept.shape[0] if kind != "part" else outer * inner
        shapes.append(jax.ShapeDtypeStruct((rows, width), kept.dtype))
        if message is not None:
            places.append(heights.get(message, 0))
            heights[message] = places[-1] + (2 * rows if kind == "vec" else rows)
        else:
            places.append(None)
    sizes = [heights[m] for m in sorted(heights)]
    shapes += [jax.ShapeDtypeStruct((n, width), BF) for n in sizes]
    which = [next(i for i, g in enumerate(gots) if g is item[2]) for item in items]

    def body(pos_ref, *refs):
        kept_refs, refs = refs[: len(items)], refs[len(items) :]
        got_refs, refs = refs[: len(gots)], refs[len(gots) + len(after) :]
        out_refs, sent_refs = refs[: len(items)], refs[len(items) :]
        for i, (kind, _, _, first, outer, inner, bit, message) in enumerate(items):
            kept_ref, got_ref, out_ref = kept_refs[i], got_refs[which[i]], out_refs[i]
            n = kept_ref.shape[0]
            if kind == "vec":
                total = kept_ref[...] + unpack(got_ref[first : first + 2 * n])
                out_ref[...] = total
                if message is not None:
                    sent_refs[message][places[i] : places[i] + 2 * n] = pack(total)
            elif kind == "sum":
                total = kept_ref[...].astype(F32) + got_ref[first : first + n].astype(F32)
                out_ref[...] = total.astype(BF)
            else:
                for o in range(outer):
                    halves = []
                    for side in range(2):
                        at = (2 * o + side) * inner
                        total = kept_ref[at : at + inner].astype(F32)
                        total = total + got_ref[first + at : first + at + inner].astype(F32)
                        halves.append(total.astype(BF))
                    rows = slice(places[i] + o * inner, places[i] + (o + 1) * inner)
                    if bit is None:
                        out_ref[o * inner : (o + 1) * inner], sent_refs[message][rows] = halves
                    else:
                        out_ref[o * inner : (o + 1) * inner] = pick(pos_ref[bit], *halves)
                        sent_refs[message][rows] = pick(pos_ref[bit], *halves[::-1])

    vmem = pl.BlockSpec(memory_space=pltpu.VMEM)
    results = pl.pallas_call(
        body,
        in_specs=[pl.BlockSpec(memory_space=pltpu.SMEM)]
        + [vmem] * (len(items) + len(gots))
        + [pl.BlockSpec(memory_space=pl.ANY)] * len(after),
        out_specs=[vmem] * len(shapes),
        out_shape=shapes,
        compiler_params=pltpu.CompilerParams(vmem_limit_bytes=16 * MIB),
        cost_estimate=pl.CostEstimate(flops=1_000_000, bytes_accessed=1 * MIB, transcendentals=0),
    )(pos, *[item[1] for item in items], *gots, *after)
    return results[: len(items)], results[len(items) :]


def packet_call(kernel, shapes, pos, args, after=(), scratch=(), wide=()):
    smem, vmem = pl.BlockSpec(memory_space=pltpu.SMEM), pl.BlockSpec(memory_space=pltpu.VMEM)
    outs = [jax.ShapeDtypeStruct(shape, BF) for shape in shapes]
    outs += [jax.ShapeDtypeStruct(shape, F32) for shape in wide]

    def body(*refs):
        n = 1 + len(args)
        kernel(*refs[:n], *refs[n + len(after) :])

    return pl.pallas_call(
        body,
        in_specs=[smem] + [vmem] * len(args) + [pl.BlockSpec(memory_space=pl.ANY)] * len(after),
        out_specs=[vmem] * len(outs),
        out_shape=outs,
        scratch_shapes=list(scratch),
        compiler_params=pltpu.CompilerParams(vmem_limit_bytes=20 * MIB),
        cost_estimate=pl.CostEstimate(flops=100_000_000, bytes_accessed=1 * MIB, transcendentals=0),
    )(pos, *args, *after)


def local(
    tokens, seg_ids, turn_ids, prev_ids, answer_table, query_weight, query_bias,
    key_weight, value_weight, value_bias, out_weight, out_bias, norm_gain, norm_shift,
    up_weight, up_bias, down_weight, down_bias, final_gain, final_shift, cotangent,
):
    rows, width = tokens.shape
    blocks = lax.axis_size("blk")
    grps = lax.axis_size("grp")
    tab = TAB_MAX
    scale = HEAD_DIM ** (-0.5)
    f = lambda v: v.astype(F32)
    core_bit = lax.axis_index("grp") & 1
    x_bit = lax.axis_index("grp") >> 1
    own = lax.axis_index("blk")
    planes = blocks // 2
    n_out = width // blocks
    ff_out = up_weight.shape[1] // blocks
    half_width = width // 2
    n_table = blocks * tab
    pos = jnp.stack([core_bit, x_bit, own & 1, (own >> 1) & 1, own >> 2]).astype(jnp.int32)

    def swap_grp(value, mask):
        return lax.ppermute(value, "grp", [(i, i ^ mask) for i in range(grps)])

    def swap_blk(value, mask):
        return lax.ppermute(value, "blk", [(i, i ^ mask) for i in range(blocks)])

    payload, layer_input = entry(tokens, seg_ids, prev_ids, answer_table)
    slots = [payload] + [None] * (blocks - 1)
    for k in range(1, planes):
        slots[2 * k] = swap_blk(payload, 2 * k)
    slots[1] = swap_blk(payload, 1)
    for k in range(1, planes):
        slots[2 * k + 1] = swap_blk(slots[2 * k], 1)
    queries, own_keys, own_values, own_bias, value_row = own_part(
        layer_input, query_weight, key_weight, value_weight, query_bias, value_bias, seg_ids, turn_ids
    )
    keys, values, prob, context, x_t, table_prev = attend(
        slots, layer_input, key_weight, value_weight, value_row, queries, own_keys, own_values, own_bias
    )
    (
        mixed, context_t, middle_t, act_t, grad_ffn, grad_pre, grad_attn, grad_context, grad_mid_sum,
        sums, up_sum,
    ) = middle_part(
        tokens, prev_ids, answer_table, context, cotangent, out_weight, up_weight, down_weight, up_bias,
        out_bias, norm_gain, norm_shift, down_bias, final_gain, final_shift,
    )
    down_args = (act_t, context_t, grad_ffn, grad_attn)
    up_args = (middle_t, grad_pre)
    part = (ff_out - n_out) // 2
    back_args = (queries, keys, values, prob, context, grad_context)
    input_args = (query_weight, key_weight, value_weight, grad_mid_sum, prev_ids, table_prev, sums, up_sum)

    if blocks == 8 and n_out % 32 == 0:
        flat = lambda rows: (rows, half_width)
        (sent,) = packet_call(
            lambda *refs: send_kernel(down_values, 4, blocks, *refs),
            [(blocks, ff_out + n_out, half_width)], pos, down_args,
        )
        down_got = swap_grp(sent, 1)
        (sent,) = packet_call(
            lambda *refs: send_kernel(up_values, 2, blocks, *refs),
            [(blocks, ff_out, half_width)], pos, up_args, after=(sent,),
        )
        up_got = swap_grp(sent, 1)
        down_kept, down_sent, z_kept, z_sent = packet_call(
            lambda *refs: keep_down_kernel(blocks, *refs),
            [flat(blocks * part)] * 2 + [flat(8 * n_out)] * 2, pos, down_args + (down_got,), after=(sent,),
        )
        down_got = swap_grp(down_sent, 2)
        z_got = swap_blk(z_sent, 2)
        up_kept, up_sent = packet_call(
            lambda *refs: keep_up_kernel(blocks, *refs),
            [flat(planes * ff_out)] * 2, pos, up_args + (up_got,), after=(down_sent,),
        )
        up_got = swap_blk(up_sent, 1)
        grad_queries, grad_keys_t, grad_values_t = attend_back(*back_args, (down_sent, up_sent, z_sent))
        qkv_args = (x_t, grad_queries, grad_keys_t, grad_values_t)
        (qkv_sent,) = packet_call(
            lambda *refs: send_kernel(qkv_values, 4, blocks, *refs),
            [(blocks, 3 * n_out, half_width)], pos, qkv_args,
        )
        qkv_got = swap_grp(qkv_sent, 1)
        table_kept, table_sent, grad_input_local, vectors, packed = input_grads(
            blocks, grad_queries, grad_keys_t, grad_values_t, *input_args, (qkv_sent,)
        )
        vec_got = swap_grp(packed, 1)
        (z_kept,), (z_sent,) = combine(pos, [("part", z_kept, z_got, 0, 1, 4 * n_out, 4, 0)], after=(table_sent,))
        z_got = swap_blk(z_sent, 4)
        n_first, n_value, n_rows = blocks * n_out, planes * n_out, blocks * tab
        first_kept, first_sent, value_kept, value_sent, vectors = packet_call(
            lambda *refs: keep_qkv_kernel(blocks, *refs),
            [flat(n_first), flat(n_first + 64), flat(n_value), flat(n_value + n_rows)],
            pos, qkv_args + (qkv_got, table_sent, vectors, vec_got), wide=[flat(32)], after=(z_sent,),
        )
        first_got = swap_grp(first_sent, 2)
        value_got = swap_blk(value_sent, 1)
        (down_kept,), (down_sent,) = combine(
            pos, [("part", down_kept, down_got, 0, 2, 2 * part, 3, 0)], after=(value_sent,)
        )
        down_got = swap_blk(down_sent, 2)
        (up_kept,), (up_sent,) = combine(
            pos, [("part", up_kept, up_got, 0, planes, ff_out // 2, 1, 0)], after=(down_sent,)
        )
        up_got = swap_grp(up_sent, 2)
        (first_kept, vectors), (first_sent,) = combine(
            pos,
            [
                ("part", first_kept, first_got, 0, planes, n_out, 2, 0),
                ("vec", vectors, first_got, n_first, 0, 0, None, 0),
            ],
            after=(up_sent,),
        )
        first_got = swap_blk(first_sent, 1)
        (value_kept, table_kept), (value_sent, table_sent) = combine(
            pos,
            [
                ("part", value_kept, value_got, 0, planes, n_out // 2, 1, 0),
                ("part", table_kept, value_got, n_value, 2, 2 * tab, None, 1),
            ],
            after=(first_sent,),
        )
        value_got = swap_grp(value_sent, 2)
        table_got = swap_blk(table_sent, 2)
        (down_kept, z_kept), (down_sent,) = combine(
            pos,
            [
                ("part", down_kept, down_got, 0, 2, part, 2, 0),
                ("part", z_kept, z_got, 0, 1, 2 * n_out, 2, 0),
            ],
            after=(value_sent,),
        )
        down_got = swap_blk(down_sent, 1)
        (up_kept,), (up_sent,) = combine(
            pos, [("part", up_kept, up_got, 0, 2, ff_out // 2, 3, 0)], after=(down_sent,)
        )
        up_got = swap_blk(up_sent, 2)
        (first_kept, value_kept, vectors), (first_sent,) = combine(
            pos,
            [
                ("part", first_kept, first_got, 0, 2, n_out, 3, 0),
                ("part", value_kept, value_got, 0, 2, n_out // 2, 3, 0),
                ("vec", vectors, first_got, n_value, 0, 0, None, 0),
            ],
            after=(up_sent,),
        )
        first_got = swap_blk(first_sent, 2)
        n_down = 2 * part
        (down_kept, z_kept, up_kept), (down_sent, z_sent) = combine(
            pos,
            [
                ("part", down_kept, down_got, 0, 1, part, 4, 0),
                ("part", z_kept, down_got, n_down, 1, n_out, 1, 1),
                ("part", up_kept, up_got, 0, 1, ff_out // 2, 4, 0),
            ],
            after=(first_sent,),
        )
        down_got = swap_blk(down_sent, 4)
        z_got = swap_grp(z_sent, 2)
        (first_kept, value_kept, table_kept, vectors), (first_sent,) = combine(
            pos,
            [
                ("part", first_kept, first_got, 0, 1, n_out, 4, 0),
                ("part", value_kept, first_got, 2 * n_out, 1, n_out // 2, 4, 0),
                ("part", table_kept, table_got, 0, 1, 2 * tab, None, 0),
                ("vec", vectors, first_got, 3 * n_out, 0, 0, None, 0),
            ],
            after=(down_sent,),
        )
        first_got = swap_blk(first_sent, 4)
        (down_part, up_part, z_part), _ = combine(
            pos,
            [
                ("sum", down_kept, down_got, 0, 0, 0, None, None),
                ("sum", up_kept, down_got, part, 0, 0, None, None),
                ("sum", z_kept, z_got, 0, 0, 0, None, None),
            ],
            after=(first_sent,),
        )
        n_small = n_out + n_out // 2
        (first_part, value_part, table_part, vectors), _ = combine(
            pos,
            [
                ("sum", first_kept, first_got, 0, 0, 0, None, None),
                ("sum", value_kept, first_got, n_out, 0, 0, None, None),
                ("sum", table_kept, first_got, n_small, 0, 0, None, None),
                ("vec", vectors, first_got, n_small + 2 * tab, 0, 0, None, None),
            ],
            after=(down_part,),
        )

        def whole(value):
            other = swap_grp(value, 2)
            return pick(x_bit, value, other), pick(x_bit, other, value)

        low, high = whole(jnp.concatenate([down_part, up_part, z_part], axis=0))
        at_up, at_z = part, part + ff_out // 2
        big = jnp.concatenate(
            [low[:at_up], high[:at_up], low[at_up:at_z], high[at_up:at_z], low[at_z:], high[at_z:]], axis=0
        )
        low, high = whole(jnp.concatenate([first_part, value_part], axis=0))
        square = jnp.concatenate([low[:n_out], high[:n_out], low[n_out:], high[n_out:]], axis=0)
        down_rows, up_rows, z_rows = big[: 2 * part], big[2 * at_up : 2 * at_z], big[2 * at_z :]
        table_share = f(table_part)
    else:
        lanes = lambda value, index: lax.dynamic_slice_in_dim(value, index * (value.shape[1] // 2), value.shape[1] // 2, 1)
        rows_of = lambda value, index: lax.dynamic_slice_in_dim(value, index * (value.shape[0] // 2), value.shape[0] // 2, 0)
        blocked = lambda value: value.reshape(blocks, value.shape[0] // blocks, value.shape[1])
        grad_queries, grad_keys_t, grad_values_t = attend_back(*back_args, ())
        table_kept, table_sent, grad_input_local, vectors, packed = input_grads(
            blocks, grad_queries, grad_keys_t, grad_values_t, *input_args, ()
        )

        def packet(index):
            up = blocked(fwd_dot(middle_t, lanes(grad_pre, index)))
            return jnp.concatenate(
                [
                    blocked(fwd_dot(x_t[:, n_table:], lanes(grad_queries, index))),
                    blocked(back_dot(x_t, rows_of(grad_keys_t, index))),
                    blocked(back_dot(x_t, rows_of(grad_values_t, index))),
                    blocked(fwd_dot(context_t, lanes(grad_attn, index))),
                ]
                + [up[:, :, i : i + half_width] for i in range(0, up.shape[2], half_width)]
                + [blocked(fwd_dot(act_t, lanes(grad_ffn, index)))],
                axis=1,
            )

        total = (packet(core_bit) + f(swap_grp(packet(1 - core_bit).astype(BF), 1))).astype(BF)
        total = lax.psum_scatter(total, "blk", scatter_dimension=0, tiled=False)
        total = (f(total) + f(swap_grp(total, 2))).astype(BF)
        at = 4 * n_out
        square = total[: 3 * n_out]
        up_rows = total[at : at + ff_out]
        down_all = total[at + ff_out :]
        z_rows = jnp.concatenate([down_all[:n_out], total[3 * n_out : at]], axis=0)
        down_rows = down_all[n_out:]
        table_rows = jnp.stack([blocked_half.reshape(planes, 2 * tab, half_width) for blocked_half in (table_kept, table_sent)], axis=1)
        table_rows = table_rows.reshape(blocks, 2 * tab, half_width)
        table_rows = jnp.take(table_rows, jnp.arange(blocks) ^ own, axis=0)
        table_share = f(lax.psum_scatter(table_rows, "blk", scatter_dimension=0, tiled=False))
        vectors = lax.psum(vectors, ("blk", "grp"))
        big = jnp.concatenate([down_rows, up_rows, z_rows], axis=0)

    def both_cores(value):
        other = swap_grp(value, 1)
        return f(pick(core_bit, value, other)), f(pick(core_bit, other, value))

    sides = both_cores(big)
    n_down = ff_out - n_out
    at_z = n_down + ff_out
    out_up = jnp.concatenate(
        [side[i : i + n_out] for side in sides for i in range(n_down, at_z, n_out)], axis=1
    )
    out_down = jnp.concatenate(
        [
            jnp.concatenate([side[at_z : at_z + n_out] for side in sides], axis=1),
            jnp.concatenate([side[:n_down] for side in sides], axis=1),
        ],
        axis=0,
    )
    out_out = jnp.concatenate([side[at_z + n_out :] for side in sides], axis=1)
    square = jnp.concatenate(both_cores(square), axis=1)
    table_share = jnp.concatenate([table_share[:tab], table_share[tab:]], axis=1)
    vectors = jnp.concatenate([vectors[:16], vectors[16:]], axis=1)
    mine = lax.dynamic_slice_in_dim(vectors[:10], own * n_out, n_out, 1)
    up_bias_out = lax.dynamic_slice_in_dim(vectors[10:14].reshape(-1), own * ff_out, ff_out, 0)
    grad_input = grad_input_local.at[:tab].add(table_share)
    return (
        mixed,
        grad_input,
        mine[:2],
        square[:n_out],
        mine[2],
        square[n_out : 2 * n_out],
        square[2 * n_out :],
        mine[3],
        out_out,
        mine[4],
        mine[5],
        mine[6],
        out_up,
        up_bias_out,
        out_down,
        mine[7],
        mine[8],
        mine[9],
    )


def solution(mesh):
    both = ("grp", "blk")
    placed = (P(both, None), P(both), P(both), P(both)) + (P(),) * 16 + (P(both, None),)
    vec, mat = P("blk"), P("blk", None)
    return jax.shard_map(
        local,
        mesh=mesh,
        in_specs=placed,
        out_specs=(
            P(both, None), P(both, None), P(None, "blk"), mat, vec, mat, mat, vec, mat, vec,
            vec, vec, mat, vec, mat, vec, vec, vec,
        ),
        check_vma=False,
    )
```

```python
import math

import jax
import jax.numpy as jnp
from jax import lax
from jax.experimental import pallas as pl
from jax.experimental.pallas import tpu as pltpu
from jax.sharding import PartitionSpec as P

HEADS = 12
HEAD_DIM = 64
TAB_MAX = 64
LANES = 256
far_below = -1e30
BF = jnp.bfloat16
F32 = jnp.float32
MIB = 1 << 20
LONG = pl.CostEstimate(flops=40_000_000_000, bytes_accessed=MIB, transcendentals=0)
SHORT = pl.CostEstimate(flops=100000000, bytes_accessed=MIB, transcendentals=0)
HBM = pl.BlockSpec(memory_space=pltpu.HBM)


def outer_sum(left, right):
    return lax.dot_general(left, right, (((0,), (0,)), ((), ())), preferred_element_type=F32)


def back_dot(left, right):
    return lax.dot_general(left, right, (((1,), (1,)), ((), ())), preferred_element_type=F32)


def fwd_dot(left, right):
    return jnp.dot(left, right, preferred_element_type=F32)


def norm_parts(values):
    centred = values - jnp.mean(values, axis=-1, keepdims=True)
    spread = jnp.mean(centred * centred, axis=-1, keepdims=True)
    inv = lax.rsqrt(spread + 1e-06)
    return centred * inv, inv


def norm_grad(grad, normed, inv, gain):
    scaled = grad * gain
    return inv * (
        scaled
        - jnp.mean(scaled, axis=-1, keepdims=True)
        - normed * jnp.mean(scaled * normed, axis=-1, keepdims=True)
    )


def head_lanes(shape, index):
    lane = lax.broadcasted_iota(jnp.int32, shape, len(shape) - 1)
    return (lane >= index * HEAD_DIM) & (lane < (index + 1) * HEAD_DIM)


def column_of(row):
    return jnp.broadcast_to(row, (128, row.shape[1])).T[:, :1]


def start_copies(sources, targets, sems):
    copies = [pltpu.make_async_copy(a, b, sems.at[i]) for i, (a, b) in enumerate(zip(sources, targets))]
    for copy in copies:
        copy.start()
    return copies


def entry_kernel(tokens_any, seg_any, prev_any, answer_any, payload_ref, input_ref, *scratch):
    tab = TAB_MAX
    *held, sems = scratch
    for copy in start_copies((tokens_any, seg_any, prev_any, answer_any), held, sems):
        copy.wait()
    tokens_ref, seg_ref, prev_ref, answer_ref = held
    prev = prev_ref[...].astype(F32)[None]
    low = residual(tokens_ref, prev, answer_ref).astype(BF)
    input_ref[...] = low
    payload_ref[:tab] = low[:tab]
    payload_ref[tab:] = jnp.zeros((16, low.shape[1]), BF)
    lane = lax.broadcasted_iota(jnp.int32, (1, 128), 1)

    def twice(row):
        row = row[:, :128]
        return jnp.where(lane < tab, row, pltpu.roll(row, tab, 1))

    is_open = twice(jnp.where(seg_ref[...] == 0, 1.0, 0.0)[None])
    both = jnp.concatenate([is_open, twice(prev)], axis=1)
    payload_ref[tab:, :256] = jnp.broadcast_to(both, (16, 256)).astype(BF)


def residual(tokens_ref, prev, answer_ref):
    answers = answer_ref[...].astype(F32)
    return tokens_ref[...].astype(F32) + jnp.where(column_of(prev) == 1.0, answers[1:2], answers[0:1])


def entry(tokens, seg, prev, answers):
    rows, width = tokens.shape
    vmem = pl.BlockSpec(memory_space=pltpu.VMEM)
    return pl.pallas_call(
        entry_kernel,
        in_specs=[HBM] * 4,
        out_specs=[vmem] * 2,
        out_shape=[jax.ShapeDtypeStruct((TAB_MAX + 16, width), BF), jax.ShapeDtypeStruct((rows, width), BF)],
        scratch_shapes=[pltpu.VMEM(v.shape, v.dtype) for v in (tokens, seg, prev, answers)]
        + [pltpu.SemaphoreType.DMA((4,))],
        compiler_params=pltpu.CompilerParams(vmem_limit_bytes=60 * MIB),
    )(tokens, seg, prev, answers)


def own_kernel(
    input_ref, query_w_any, key_w_any, value_w_any, query_b_any, value_b_any, seg_any, turn_any,
    q_ref, k_ref, v_ref, bias_ref, value_row_ref, *scratch
):
    *held, sems = scratch
    query_w_ref, key_w_ref, value_w_ref, query_b_ref, value_b_ref, seg_ref, turn_ref = held
    sources = (query_w_any, key_w_any, value_w_any, query_b_any, value_b_any, seg_any, turn_any)
    for copy in start_copies(sources, held, sems):
        copy.wait()
    low = input_ref[...]
    query = fwd_dot(low, query_w_ref[...]) + query_b_ref[...].astype(F32)[None]
    q_ref[...] = (query.astype(BF).astype(F32) * HEAD_DIM**-0.5).astype(BF)
    k_ref[...] = fwd_dot(low, key_w_ref[...]).astype(BF)
    value_b = value_b_ref[...].astype(F32)[None]
    value_row_ref[...] = value_b
    v_ref[...] = (fwd_dot(low, value_w_ref[...]) + value_b).astype(BF)
    turn = turn_ref[...].astype(F32)[None]
    seg = seg_ref[...].astype(F32)[None]
    same = (column_of(turn) == turn) & (seg != 0.0)
    bias_ref[...] = jnp.where(same, 0.0, far_below)


def own_part(layer_input, query_w, key_w, value_w, query_b, value_b, seg, turn):
    rows, width = layer_input.shape
    vmem = pl.BlockSpec(memory_space=pltpu.VMEM)
    return pl.pallas_call(
        own_kernel,
        in_specs=[vmem] + [HBM] * 7,
        out_specs=[vmem] * 5,
        out_shape=[jax.ShapeDtypeStruct((rows, width), BF)] * 3
        + [jax.ShapeDtypeStruct((rows, rows), F32), jax.ShapeDtypeStruct((1, width), F32)],
        scratch_shapes=[
            pltpu.VMEM(v.shape, v.dtype) for v in (query_w, key_w, value_w, query_b, value_b, seg, turn)
        ]
        + [pltpu.SemaphoreType.DMA((7,))],
        compiler_params=pltpu.CompilerParams(vmem_limit_bytes=60 * MIB),
        cost_estimate=pl.CostEstimate(flops=100000000, bytes_accessed=MIB, transcendentals=0),
    )(layer_input, query_w, key_w, value_w, query_b, value_b, seg, turn)


def attend_kernel(
    views, input_ref, key_w_ref, value_w_ref, value_b_ref, q_ref, own_k_ref, own_v_ref, own_bias_ref, *refs
):
    *parts, keys_ref, values_ref, prob_ref, context_ref, x_t_ref, prev_ref, table_ref, bias_ref = refs
    n_table = table_ref.shape[0]
    tab = TAB_MAX
    slots = [parts[part].at[first : first + tab + 16] for part, first in views]

    @pl.when(pl.program_id(0) == 0)
    def _():
        lane = lax.broadcasted_iota(jnp.int32, (1, 128), 1)
        for i, slot in enumerate(slots):
            table_ref[i * tab : (i + 1) * tab] = slot[:tab]
        for i in range(0, len(slots), 2):
            marks = jnp.where(
                lax.broadcasted_iota(jnp.int32, (16, 256), 1) % 128 < tab,
                slots[i][tab:, :256].astype(F32), slots[i + 1][tab:, :256].astype(F32),
            )
            at = slice(i * tab, (i + 2) * tab)
            closed = jnp.where(marks[:1, :128] > 0.5, 0.0, far_below)
            bias_ref[:, at] = jnp.broadcast_to(closed, (bias_ref.shape[0], 128))
            prev_ref[:, at] = marks[:8, 128:]
        bias_ref[:, n_table:] = own_bias_ref[...]
        x_t_ref[:, :n_table] = table_ref[...].T
        x_t_ref[:, n_table:] = input_ref[...].T

    table = table_ref[...]
    keys_ref[:n_table] = fwd_dot(table, key_w_ref[...]).astype(BF)
    values_ref[:n_table] = (fwd_dot(table, value_w_ref[...]) + value_b_ref[...]).astype(BF)
    keys_ref[n_table:] = own_k_ref[...]
    values_ref[n_table:] = own_v_ref[...]
    queries = q_ref[...]
    context = jnp.zeros(context_ref.shape, F32)
    for h in range(queries.shape[1] // HEAD_DIM):
        mask = head_lanes(queries.shape, h)
        picked = jnp.where(mask, queries, jnp.zeros_like(queries))
        scores = back_dot(picked, keys_ref[...]) + bias_ref[...]
        top = jnp.max(scores, axis=-1, keepdims=True)
        weights = jnp.exp(scores - top)
        prob = (weights * (1.0 / jnp.sum(weights, axis=-1, keepdims=True))).astype(BF)
        prob_ref[h] = prob
        context = jnp.where(mask, fwd_dot(prob, values_ref[...]), context)
    context_ref[...] = context


def vmem_limit(n_keys, small):
    return (small if n_keys <= 1024 else 60) * MIB


def attend(parts, views, layer_input, key_w, value_w, value_b, queries, own_k, own_v, own_bias):
    rows, width = queries.shape
    n_table = len(views) * TAB_MAX
    n_keys = n_table + rows
    group = LANES if n_keys <= 1024 else LANES // 2
    per = group // HEAD_DIM
    steady = {} if n_keys <= 1024 else {"pipeline_mode": pl.Buffered(1)}
    whole = lambda shape: pl.BlockSpec(shape, lambda i: (0, 0), **steady)
    lanes = lambda n: pl.BlockSpec((n, group), lambda i: (0, i))
    return pl.pallas_call(
        lambda *refs: attend_kernel(views, *refs),
        grid=(width // group,),
        in_specs=[
            whole((rows, width)), lanes(width), lanes(width), lanes(1), lanes(rows), lanes(rows), lanes(rows),
            whole((rows, rows)),
        ]
        + [whole(part.shape) for part in parts],
        out_specs=[
            lanes(n_keys), lanes(n_keys), pl.BlockSpec((per, rows, n_keys), lambda i: (i, 0, 0)), lanes(rows),
            whole((width, n_keys)), whole((8, n_table)),
        ],
        out_shape=[
            jax.ShapeDtypeStruct((n_keys, width), BF),
            jax.ShapeDtypeStruct((n_keys, width), BF),
            jax.ShapeDtypeStruct((HEADS, rows, n_keys), BF),
            jax.ShapeDtypeStruct((rows, width), F32),
            jax.ShapeDtypeStruct((width, n_keys), BF),
            jax.ShapeDtypeStruct((8, n_table), F32),
        ],
        scratch_shapes=[pltpu.VMEM((n_table, width), BF), pltpu.VMEM((rows, n_keys), F32)],
        compiler_params=pltpu.CompilerParams(vmem_limit_bytes=vmem_limit(n_keys, 60)),
        cost_estimate=pl.CostEstimate(flops=100000000, bytes_accessed=MIB, transcendentals=0),
    )(layer_input, key_w, value_w, value_b, queries, own_k, own_v, own_bias, *parts)


def middle_kernel(
    packets, pos_ref, tokens_ref, prev_ref, answer_ref, context_ref, cot_ref, out_w_any, up_w_any, down_w_any,
    up_b_1d_ref, *refs
):
    biases, refs = refs[:6], refs[6:]
    mixed_ref, grad_context_ref, grad_mid_ref, sums_ref, up_sum_ref = refs[:5]
    refs = refs[5:]
    if packets:
        anys, refs = refs[:5], refs[5:]
    context_t_ref, middle_t_ref, act_t_ref, grad_ffn_ref, grad_pre_ref, grad_attn_ref = refs[:6]
    slope_ref, total_ref, middle_low_ref, out_w_ref, up_w_ref, down_w_ref, up_b_ref, sems = refs[6:14]
    width, hidden = up_w_ref.shape
    tile = width
    steps = hidden // tile

    def tile_copies(i):
        at = pl.ds(pl.multiple_of(i * tile, tile), tile)
        return (
            pltpu.make_async_copy(up_w_any.at[:, at], up_w_ref.at[:, at], sems.at[2 * i + 1]),
            pltpu.make_async_copy(down_w_any.at[at, :], down_w_ref.at[at, :], sems.at[2 * i + 2]),
        )

    out_copy = pltpu.make_async_copy(out_w_any, out_w_ref, sems.at[0])
    out_copy.start()
    for i in range(steps):
        for copy in tile_copies(i):
            copy.start()
    out_b, norm_g, norm_s, down_b, final_g, final_s = (ref[...].astype(F32)[None] for ref in biases)
    up_b_ref[...] = up_b_1d_ref[...].astype(F32)[None]
    resid = residual(tokens_ref, prev_ref[...].astype(F32)[None], answer_ref)
    column = lambda v: jnp.sum(v, axis=0, keepdims=True)
    context_low = context_ref[...].astype(BF)
    context_t_ref[...] = context_low.T
    out_copy.wait()
    normed1, inv1 = norm_parts(resid + fwd_dot(context_low, out_w_ref[...]) + out_b)
    middle = normed1 * norm_g + norm_s
    middle_low = middle.astype(BF)
    middle_low_ref[...] = middle_low
    middle_t_ref[...] = middle_low.T
    total_ref[...] = middle + down_b

    def forward(i, carry):
        at = pl.ds(pl.multiple_of(i * tile, tile), tile)
        for copy in tile_copies(i):
            copy.wait()
        pre = fwd_dot(middle_low_ref[...], up_w_ref[:, at]) + up_b_ref[:, at]
        cdf = 0.5 * (1.0 + lax.erf(pre * (0.5**0.5)))
        act = (pre * cdf).astype(BF)
        act_t_ref[at, :] = act.T
        slope_ref[:, at] = cdf + pre * jnp.exp(-0.5 * pre * pre) * (1.0 / math.sqrt(2 * math.pi))
        total_ref[...] += fwd_dot(act, down_w_ref[at, :])
        return carry

    lax.fori_loop(0, steps, forward, 0)
    normed2, inv2 = norm_parts(total_ref[...])
    mixed_ref[...] = (normed2 * final_g + final_s).astype(BF)
    cot = cot_ref[...].astype(F32)
    grad_final = norm_grad(cot, normed2, inv2, final_g)
    grad_ffn = grad_final.astype(BF)
    grad_ffn_ref[...] = grad_ffn
    total_ref[...] = grad_final

    def backward(i, carry):
        at = pl.ds(pl.multiple_of(i * tile, tile), tile)
        grad_pre = (back_dot(grad_ffn_ref[...], down_w_ref[at, :]) * slope_ref[:, at]).astype(BF)
        grad_pre_ref[:, at] = grad_pre
        up_sum_ref[:, at] = column(grad_pre.astype(F32))
        total_ref[...] += back_dot(grad_pre, up_w_ref[:, at])
        return carry

    copies = []
    if packets:
        blocks = packets
        sent_ref, down_own_ref, z_own_ref, up_sent_ref, up_own_ref, out_sems = refs[14:]
        half = width // 2
        small, size = width // blocks, hidden // blocks
        first_rows = 2 * small // 3
        z_rows, rows = first_rows + small, size - first_rows
        core = pos_ref[0]
        n_down = blocks * rows

        def leave(source, target):
            copy = pltpu.make_async_copy(source, target, out_sems.at[len(copies)])
            copy.start()
            copies.append(copy)

        def lanes_of(own):
            return pl.ds(pl.multiple_of((core if own else 1 - core) * half, 128), half)

        for own, down_ref, first_z, z_ref in ((False, sent_ref, n_down, sent_ref), (True, down_own_ref, 0, z_own_ref)):
            part = grad_ffn_ref[:, lanes_of(own)]
            for b in range(blocks):
                value = fwd_dot(act_t_ref[b * size : (b + 1) * size], part).astype(BF)
                down_ref[b * rows : (b + 1) * rows] = value[first_rows:]
                z_ref[first_z + b * z_rows : first_z + b * z_rows + first_rows] = value[:first_rows]
            leave(down_ref.at[:n_down], (anys[1] if own else anys[0].at[:n_down]))
        for i in range(steps):
            t = lax.rem(2 * (1 - core) + i, steps)
            backward(t, 0)
            value = fwd_dot(middle_t_ref[...], grad_pre_ref[:, pl.ds(pl.multiple_of(t * tile, tile), tile)]).astype(BF)
            target = up_sent_ref if i < steps // 2 else up_own_ref
            for b in range(blocks):
                for q in range(2):
                    first = b * size + (2 * (i % (steps // 2)) + q) * small
                    target[first : first + small] = value[b * small : (b + 1) * small, q * half : (q + 1) * half]
            if i == steps // 2 - 1:
                leave(up_sent_ref, anys[3])
        leave(up_own_ref, anys[4])
    else:
        lax.fori_loop(0, steps, backward, 0)
    grad_middle = total_ref[...]
    grad_mid = norm_grad(grad_middle, normed1, inv1, norm_g)
    grad_mid_ref[...] = grad_mid
    grad_attn = grad_mid.astype(BF)
    grad_attn_ref[...] = grad_attn
    if packets:
        for own, first_z, z_ref in ((False, n_down, sent_ref), (True, 0, z_own_ref)):
            value = fwd_dot(context_t_ref[...], grad_attn_ref[:, lanes_of(own)]).astype(BF)
            for b in range(blocks):
                first = first_z + b * z_rows + first_rows
                z_ref[first : first + small] = value[b * small : (b + 1) * small]
            if own:
                leave(z_own_ref, anys[2])
            else:
                leave(sent_ref.at[n_down:], anys[0].at[n_down:])
    grad_context_ref[...] = back_dot(grad_attn, out_w_ref[...]).astype(BF)
    sums_ref[0:1] = column(grad_attn.astype(F32))
    sums_ref[1:2] = column(grad_middle * normed1)
    sums_ref[2:3] = column(grad_middle)
    sums_ref[3:4] = column(grad_ffn.astype(F32))
    sums_ref[4:5] = column(cot * normed2)
    sums_ref[5:6] = column(cot)
    sums_ref[6:8] = jnp.zeros((2, sums_ref.shape[1]), F32)
    for copy in copies:
        copy.wait()


def middle_part(packets, pos, tokens, prev, answers, context, cot, out_w, up_w, down_w, up_b, *biases):
    rows, width = tokens.shape
    hidden = up_w.shape[1]
    half = width // 2
    vmem, away = pl.BlockSpec(memory_space=pltpu.VMEM), pl.BlockSpec(memory_space=pl.ANY)
    shape = lambda n, t: jax.ShapeDtypeStruct((rows, n), t)
    turned = lambda n: jax.ShapeDtypeStruct((n, rows), BF)
    inner = [turned(width), turned(width), turned(hidden), shape(width, BF), shape(hidden, BF), shape(width, BF)]
    held = lambda shapes: [pltpu.VMEM(v.shape, v.dtype) for v in shapes]
    outs = [
        shape(width, BF), shape(width, BF), shape(width, F32), jax.ShapeDtypeStruct((8, width), F32),
        jax.ShapeDtypeStruct((1, hidden), F32),
    ]
    scratch = [
        pltpu.VMEM((rows, hidden), F32), pltpu.VMEM((rows, width), F32), pltpu.VMEM((rows, width), BF),
        pltpu.VMEM(out_w.shape, BF), pltpu.VMEM(up_w.shape, BF), pltpu.VMEM(down_w.shape, BF),
        pltpu.VMEM((1, hidden), F32), pltpu.SemaphoreType.DMA((1 + 2 * (hidden // width),)),
    ]
    specs = [vmem] * 5
    if packets:
        first_rows = 2 * width // 3
        z_rows, down_rows = first_rows + width, hidden - first_rows
        packed = [
            jax.ShapeDtypeStruct((n, half), BF) for n in (down_rows + z_rows, down_rows, z_rows, hidden, hidden)
        ]
        scratch = held(inner) + scratch + held(packed) + [pltpu.SemaphoreType.DMA((6,))]
        outs, specs = outs + packed, specs + [away] * 5
    else:
        outs, specs = outs + inner, specs + [vmem] * 6
    return pl.pallas_call(
        lambda *refs: middle_kernel(packets, *refs),
        in_specs=[pl.BlockSpec(memory_space=pltpu.SMEM)] + [vmem] * 5 + [HBM] * 3 + [vmem] * 7,
        out_specs=specs,
        out_shape=outs,
        scratch_shapes=scratch,
        compiler_params=pltpu.CompilerParams(vmem_limit_bytes=60 * MIB),
        cost_estimate=pl.CostEstimate(flops=100000000, bytes_accessed=MIB, transcendentals=0),
    )(pos, tokens, prev, answers, context, cot, out_w, up_w, down_w, up_b, *biases)


def attend_back_kernel(
    q_ref, keys_ref, values_ref, prob_ref, context_ref, grad_ref, *refs
):
    grad_q_ref, grad_k_ref, grad_v_ref = refs[-3:]
    grad = grad_ref[...]
    grad_f = grad.astype(F32)
    product = grad_f * context_ref[...]
    grad_t = grad_f.T.astype(BF)
    q_t = q_ref[...].astype(F32).T.astype(BF)
    grad_q = jnp.zeros(grad.shape, F32)
    for h in range(grad.shape[1] // HEAD_DIM):
        mask = head_lanes(grad.shape, h)
        at = slice(h * HEAD_DIM, (h + 1) * HEAD_DIM)
        row_dot = jnp.sum(jnp.where(mask, product, 0.0), axis=-1, keepdims=True)
        grad_prob = back_dot(jnp.where(mask, grad, jnp.zeros_like(grad)), values_ref[...])
        prob = prob_ref[h]
        grad_score = (prob.astype(F32) * (grad_prob - row_dot)).astype(BF)
        grad_v_ref[at] = fwd_dot(grad_t[at], prob).astype(BF)
        grad_k_ref[at] = fwd_dot(q_t[at], grad_score).astype(BF)
        grad_q = jnp.where(mask, fwd_dot(grad_score, keys_ref[...]), grad_q)
    grad_q_ref[...] = (grad_q * HEAD_DIM**-0.5).astype(BF)


def attend_back(queries, keys, values, prob, context, grad_context, after):
    rows, width = queries.shape
    n_keys = keys.shape[0]
    group = LANES if n_keys <= 1024 else LANES // 2
    per = group // HEAD_DIM
    lanes = lambda n: pl.BlockSpec((n, group), lambda i: (0, i))
    return pl.pallas_call(
        attend_back_kernel,
        grid=(width // group,),
        in_specs=[
            lanes(rows), lanes(n_keys), lanes(n_keys), pl.BlockSpec((per, rows, n_keys), lambda i: (i, 0, 0)),
            lanes(rows), lanes(rows),
        ]
        + [pl.BlockSpec(memory_space=pl.ANY)] * len(after),
        out_specs=[lanes(rows)] + [pl.BlockSpec((group, n_keys), lambda i: (i, 0))] * 2,
        out_shape=[
            jax.ShapeDtypeStruct((rows, width), BF),
            jax.ShapeDtypeStruct((width, n_keys), BF),
            jax.ShapeDtypeStruct((width, n_keys), BF),
        ],
        compiler_params=pltpu.CompilerParams(vmem_limit_bytes=vmem_limit(n_keys, 60)),
        cost_estimate=LONG,
    )(queries, keys, values, prob, context, grad_context, *after)


def core_lanes(pos_ref, own, size):
    core = pos_ref[0] if own else 1 - pos_ref[0]
    return pl.ds(pl.multiple_of(core * size, 128), size)


def qkv_values(own, pos_ref, x_t_ref, grad_q_ref, grad_k_ref, grad_v_ref, blocks, store):
    half = grad_q_ref.shape[1] // 2
    n_table = x_t_ref.shape[1] - grad_q_ref.shape[0]
    small = x_t_ref.shape[0] // blocks
    at = core_lanes(pos_ref, own, half)
    core = pos_ref[0] if own else 1 - pos_ref[0]
    rows = pl.ds(pl.multiple_of(core * half, 128), half)
    values = (
        fwd_dot(x_t_ref[:, n_table:], grad_q_ref[:, at]),
        back_dot(x_t_ref[...], grad_k_ref[rows, :]),
        back_dot(x_t_ref[...], grad_v_ref[rows, :]),
    )
    for i, value in enumerate(values):
        for b in range(blocks):
            store(b, i * small, value[b * small : (b + 1) * small])


def send_kernel(make, n_in, blocks, *refs):
    pos_ref, out_ref = refs[0], refs[-1]

    def store(b, first, value):
        out_ref[b, first : first + value.shape[0]] = value.astype(BF)

    make(False, pos_ref, *refs[1 : 1 + n_in], blocks, store)


def pick(bit, first, second):
    return jnp.where(bit == 0, first, second)


def keep_qkv_kernel(
    blocks, pos_ref, x_t_ref, grad_q_ref, grad_k_ref, grad_v_ref, got_ref, table_ref, vec_ref, *outs
):
    first_kept_ref, first_sent_ref, kept_ref, sent_ref = outs
    small = x_t_ref.shape[0] // blocks
    planes = blocks // 2
    held = {}

    def store(b, first, value):
        value = (value + got_ref[b, first : first + small].astype(F32)).astype(BF)
        held[b, first] = value
        if first == small:
            query = held.pop((b, 0))
            rows = slice(b * small, (b + 1) * small)
            first_kept_ref[rows] = pick(pos_ref[1], query, value)
            first_sent_ref[rows] = pick(pos_ref[1], value, query)
        if first == 2 * small and b % 2 == 1:
            rows = slice(b // 2 * small, (b // 2 + 1) * small)
            kept_ref[rows] = pick(pos_ref[2], held[b - 1, first], value)
            sent_ref[rows] = pick(pos_ref[2], value, held[b - 1, first])

    qkv_values(True, pos_ref, x_t_ref, grad_q_ref, grad_k_ref, grad_v_ref, blocks, store)
    first_sent_ref[blocks * small :] = vec_ref[...].astype(BF)
    sent_ref[planes * small :] = table_ref[...]


def inputs_kernel(
    blocks, grad_q_ref, grad_k_ref, grad_v_ref, query_w_ref, key_w_ref, value_w_ref, grad_mid_ref, prev_ref,
    table_prev_ref, sums_ref, up_sum_ref, *refs
):
    table_kept_ref, table_sent_ref, grad_ref, vec_ref = refs[-4:]
    tab = TAB_MAX
    n_table = blocks * tab
    rows, width = grad_q_ref.shape
    half = width // 2
    own = fwd_dot(key_w_ref[...], grad_k_ref[:, n_table:]) + fwd_dot(value_w_ref[...], grad_v_ref[:, n_table:])
    grad = grad_mid_ref[...] + back_dot(grad_q_ref[...], query_w_ref[...]) + own.T
    grad_ref[...] = grad
    is_one = column_of(prev_ref[...].astype(F32)[None]) == 1.0
    one_sum = jnp.sum(jnp.where(is_one, grad, 0.0), axis=0, keepdims=True)
    zero_sum = jnp.sum(jnp.where(is_one, 0.0, grad), axis=0, keepdims=True)
    step = min(n_table, 512)
    row = lax.broadcasted_iota(jnp.int32, (8, step), 0)
    for first in range(0, n_table, step):
        at = slice(first, first + step)
        part = (fwd_dot(key_w_ref[...], grad_k_ref[:, at]) + fwd_dot(value_w_ref[...], grad_v_ref[:, at])).astype(BF)
        marks = table_prev_ref[:, at]
        marks = jnp.where(row == 0, marks, 1.0 - marks).astype(BF)
        table_sums = back_dot(marks, part)
        one_sum += table_sums[0:1]
        zero_sum += table_sums[1:2]
        for j in range(step // 128):
            pair = part[:, j * 128 : (j + 1) * 128].T
            slot = first // 128 + j
            for k, ref in enumerate((table_kept_ref, table_sent_ref)):
                for side in range(2):
                    ref[(slot * 2 + side) * tab : (slot * 2 + side + 1) * tab] = pair[
                        k * tab : (k + 1) * tab, side * half : (side + 1) * half
                    ]
    ones = jnp.ones((8, grad_v_ref.shape[1]), BF)
    lines = [
        zero_sum,
        one_sum,
        jnp.sum(grad_q_ref[...].astype(F32), axis=0, keepdims=True),
        back_dot(ones, grad_v_ref[...])[0:1],
    ]
    lines += [sums_ref[i : i + 1] for i in range(6)]
    lines += [up_sum_ref[:, i * width : (i + 1) * width] for i in range(up_sum_ref.shape[1] // width)]
    vec_ref[...] = jnp.zeros(vec_ref.shape, F32)
    for i, line in enumerate(lines):
        for side in range(2):
            vec_ref[side * 16 + i : side * 16 + i + 1] = line[:, side * half : (side + 1) * half]


def input_grads(blocks, grad_q, grad_k, grad_v, query_w, key_w, value_w, grad_mid, prev, table_prev, sums, up_sum, after):
    rows, width = grad_q.shape
    n_half = blocks * TAB_MAX
    vmem = pl.BlockSpec(memory_space=pltpu.VMEM)
    args = (grad_q, grad_k, grad_v, query_w, key_w, value_w, grad_mid, prev, table_prev, sums, up_sum)
    return pl.pallas_call(
        lambda *refs: inputs_kernel(blocks, *refs),
        in_specs=[vmem] * len(args) + [pl.BlockSpec(memory_space=pl.ANY)] * len(after),
        out_specs=[vmem] * 4,
        out_shape=[
            jax.ShapeDtypeStruct((n_half, width // 2), BF),
            jax.ShapeDtypeStruct((n_half, width // 2), BF),
            jax.ShapeDtypeStruct((rows, width), F32),
            jax.ShapeDtypeStruct((32, width // 2), F32),
        ],
        compiler_params=pltpu.CompilerParams(vmem_limit_bytes=(20 if blocks <= 8 else 56) * MIB),
        cost_estimate=LONG,
    )(*args, *after)


def combine(pos, items, after=()):
    width = items[0][1].shape[1]
    gots, shapes, heights, places = [], [], {}, []
    for kind, kept, got, first, outer, inner, bit, message in items:
        if got is not None and not any(got is g for g in gots):
            gots.append(got)
        rows = kept.shape[0] if kind != "part" else outer * inner
        if kind != "copy":
            shapes.append(jax.ShapeDtypeStruct((rows, width), kept.dtype))
        if message is not None:
            places.append(heights.get(message, 0))
            heights[message] = places[-1] + rows
        else:
            places.append(None)
    sizes = [heights[m] for m in sorted(heights)]
    shapes += [jax.ShapeDtypeStruct((n, width), BF) for n in sizes]
    which = [next((i for i, g in enumerate(gots) if g is item[2]), None) for item in items]
    n_outs = sum(item[0] != "copy" for item in items)

    def body(pos_ref, *refs):
        kept_refs, refs = refs[: len(items)], refs[len(items) :]
        got_refs, refs = refs[: len(gots)], refs[len(gots) + len(after) :]
        out_refs, sent_refs = list(refs[:n_outs]), refs[n_outs:]
        for i, (kind, _, _, first, outer, inner, bit, message) in enumerate(items):
            kept_ref = kept_refs[i]
            n = kept_ref.shape[0]
            if kind == "copy":
                sent_refs[message][places[i] : places[i] + n] = kept_ref[...]
                continue
            got_ref, out_ref = got_refs[which[i]], out_refs.pop(0)
            if kind == "vec":
                total = kept_ref[...] + got_ref[first : first + n].astype(F32)
                out_ref[...] = total
                if message is not None:
                    sent_refs[message][places[i] : places[i] + n] = total.astype(BF)
            elif kind == "sum":
                total = kept_ref[...].astype(F32) + got_ref[first : first + n].astype(F32)
                out_ref[...] = total.astype(BF)
                if message is not None:
                    sent_refs[message][places[i] : places[i] + n] = total.astype(BF)
            else:
                for o in range(outer):
                    halves = []
                    for side in range(2):
                        at = (2 * o + side) * inner
                        total = kept_ref[at : at + inner].astype(F32)
                        total = total + got_ref[first + at : first + at + inner].astype(F32)
                        halves.append(total.astype(BF))
                    rows = slice(places[i] + o * inner, places[i] + (o + 1) * inner)
                    if bit is None:
                        out_ref[o * inner : (o + 1) * inner], sent_refs[message][rows] = halves
                    else:
                        out_ref[o * inner : (o + 1) * inner] = pick(pos_ref[bit], *halves)
                        sent_refs[message][rows] = pick(pos_ref[bit], *halves[::-1])

    vmem = pl.BlockSpec(memory_space=pltpu.VMEM)
    results = pl.pallas_call(
        body,
        in_specs=[pl.BlockSpec(memory_space=pltpu.SMEM)]
        + [vmem] * (len(items) + len(gots))
        + [pl.BlockSpec(memory_space=pl.ANY)] * len(after),
        out_specs=[vmem] * len(shapes),
        out_shape=shapes,
        compiler_params=pltpu.CompilerParams(vmem_limit_bytes=16 * MIB),
        cost_estimate=LONG,
    )(pos, *[item[1] for item in items], *gots, *after)
    return results[:n_outs], results[n_outs:]


def packet_call(kernel, shapes, pos, args, after=(), scratch=(), wide=(), cost=LONG):
    smem, vmem = pl.BlockSpec(memory_space=pltpu.SMEM), pl.BlockSpec(memory_space=pltpu.VMEM)
    outs = [jax.ShapeDtypeStruct(shape, BF) for shape in shapes]
    outs += [jax.ShapeDtypeStruct(shape, F32) for shape in wide]

    def body(*refs):
        n = 1 + len(args)
        kernel(*refs[:n], *refs[n + len(after) :])

    return pl.pallas_call(
        body,
        in_specs=[smem] + [vmem] * len(args) + [pl.BlockSpec(memory_space=pl.ANY)] * len(after),
        out_specs=[vmem] * len(outs),
        out_shape=outs,
        scratch_shapes=list(scratch),
        compiler_params=pltpu.CompilerParams(vmem_limit_bytes=20 * MIB),
        cost_estimate=cost,
    )(pos, *args, *after)


def local(
    tokens, seg_ids, turn_ids, prev_ids, answer_table, query_weight, query_bias,
    key_weight, value_weight, value_bias, out_weight, out_bias, norm_gain, norm_shift,
    up_weight, up_bias, down_weight, down_bias, final_gain, final_shift, cotangent,
):
    rows, width = tokens.shape
    blocks = lax.axis_size("blk")
    grps = lax.axis_size("grp")
    tab = TAB_MAX
    scale = HEAD_DIM ** (-0.5)
    f = lambda v: v.astype(F32)
    core_bit = lax.axis_index("grp") & 1
    x_bit = lax.axis_index("grp") >> 1
    own = lax.axis_index("blk")
    planes = blocks // 2
    n_out = width // blocks
    ff_out = up_weight.shape[1] // blocks
    half_width = width // 2
    n_table = blocks * tab
    pos = jnp.stack([core_bit, x_bit, own & 1, (own >> 1) & 1, own >> 2]).astype(jnp.int32)

    def swap_grp(value, mask):
        return lax.ppermute(value, "grp", [(i, i ^ mask) for i in range(grps)])

    def swap_blk(value, mask):
        return lax.ppermute(value, "blk", [(i, i ^ mask) for i in range(blocks)])

    payload, layer_input = entry(tokens, seg_ids, prev_ids, answer_table)
    slots = [payload] + [None] * (blocks - 1)
    for k in range(1, planes):
        slots[2 * k] = swap_blk(payload, 2 * k)
    slots[1] = swap_blk(payload, 1)
    for k in range(1, planes):
        slots[2 * k + 1] = swap_blk(slots[2 * k], 1)
    queries, own_keys, own_values, own_bias, value_row = own_part(
        layer_input, query_weight, key_weight, value_weight, query_bias, value_bias, seg_ids, turn_ids
    )
    views = [(i, 0) for i in range(blocks)]
    keys, values, prob, context, x_t, table_prev = attend(
        slots, views, layer_input, key_weight, value_weight, value_row, queries, own_keys, own_values, own_bias
    )
    packets = blocks if blocks == 8 and n_out % 32 == 0 else 0
    mixed, grad_context, grad_mid_sum, sums, up_sum, *made = middle_part(
        packets, pos, tokens, prev_ids, answer_table, context, cotangent, out_weight, up_weight, down_weight, up_bias,
        out_bias, norm_gain, norm_shift, down_bias, final_gain, final_shift,
    )
    first_rows = 2 * n_out // 3
    part, z_rows = (ff_out - first_rows) // 2, n_out + first_rows
    back_args = (queries, keys, values, prob, context, grad_context)
    input_args = (query_weight, key_weight, value_weight, grad_mid_sum, prev_ids, table_prev, sums, up_sum)

    if packets:
        flat = lambda rows: (rows, half_width)
        down_sent, down_kept, z_kept, up_sent, up_kept = made
        down_got = swap_grp(down_sent, 1)
        up_got = swap_grp(up_sent, 1)
        grad_queries, grad_keys_t, grad_values_t = attend_back(*back_args, ())
        (down_kept, z_kept), (down_sent, z_sent) = combine(
            pos,
            [
                ("part", down_kept, down_got, 0, blocks, part, 1, 0),
                ("part", z_kept, down_got, 2 * blocks * part, 2, 2 * z_rows, 3, 1),
            ],
            after=(grad_queries,),
        )
        down_got = swap_grp(down_sent, 2)
        z_got = swap_blk(z_sent, 2)
        (up_kept,), (up_sent,) = combine(
            pos, [("part", up_kept, up_got, 0, planes, ff_out, 2, 0)], after=(down_sent,)
        )
        up_got = swap_blk(up_sent, 1)
        qkv_args = (x_t, grad_queries, grad_keys_t, grad_values_t)
        (qkv_sent,) = packet_call(
            lambda *refs: send_kernel(qkv_values, 4, blocks, *refs),
            [(blocks, 3 * n_out, half_width)], pos, qkv_args, after=(up_sent,),
        )
        qkv_got = swap_grp(qkv_sent, 1)
        table_kept, table_sent, grad_input_local, vectors = input_grads(
            blocks, grad_queries, grad_keys_t, grad_values_t, *input_args, (qkv_sent,)
        )
        (z_kept,), (z_sent,) = combine(pos, [("part", z_kept, z_got, 0, 1, 2 * z_rows, 4, 0)], after=(table_sent,))
        z_got = swap_blk(z_sent, 4)
        n_first, n_value, n_rows = blocks * n_out, planes * n_out, blocks * tab
        first_kept, first_sent, value_kept, value_sent = packet_call(
            lambda *refs: keep_qkv_kernel(blocks, *refs),
            [flat(n_first), flat(n_first + 32), flat(n_value), flat(n_value + n_rows)],
            pos, qkv_args + (qkv_got, table_sent, vectors), after=(z_sent,),
        )
        first_got = swap_grp(first_sent, 2)
        value_got = swap_blk(value_sent, 1)
        (down_kept,), (down_sent,) = combine(
            pos, [("part", down_kept, down_got, 0, 2, 2 * part, 3, 0)], after=(value_sent,)
        )
        down_got = swap_blk(down_sent, 2)
        (up_kept,), (up_sent,) = combine(
            pos, [("part", up_kept, up_got, 0, planes, ff_out // 2, 1, 0)], after=(down_sent,)
        )
        up_got = swap_grp(up_sent, 2)
        (first_kept, vectors, z_kept), (first_sent,) = combine(
            pos,
            [
                ("part", first_kept, first_got, 0, planes, n_out, 2, 0),
                ("vec", vectors, first_got, n_first, 0, 0, None, 0),
                ("part", z_kept, z_got, 0, 1, z_rows, 2, 0),
            ],
            after=(up_sent,),
        )
        first_got = swap_blk(first_sent, 1)
        (down_kept,), (down_sent,) = combine(
            pos, [("part", down_kept, down_got, 0, 1, 2 * part, 4, 0)], after=(first_sent,)
        )
        down_got = swap_blk(down_sent, 4)
        (value_kept, table_kept), (value_sent, table_sent) = combine(
            pos,
            [
                ("part", value_kept, value_got, 0, planes, n_out // 2, 1, 0),
                ("part", table_kept, value_got, n_value, 2, 2 * tab, None, 1),
            ],
            after=(down_sent,),
        )
        value_got = swap_grp(value_sent, 2)
        table_got = swap_blk(table_sent, 2)
        (down_kept, up_kept), (down_sent, up_sent) = combine(
            pos,
            [
                ("part", down_kept, down_got, 0, 1, part, 2, 0),
                ("part", up_kept, up_got, 0, 2, ff_out // 2, 3, 1),
            ],
            after=(value_sent,),
        )
        down_got = swap_blk(down_sent, 1)
        up_got = swap_blk(up_sent, 2)
        (first_kept, value_kept, vectors, z_kept), (first_sent, z_sent) = combine(
            pos,
            [
                ("part", first_kept, first_got, 0, 2, n_out, 3, 0),
                ("part", value_kept, value_got, 0, 2, n_out // 2, 3, 0),
                ("vec", vectors, first_got, n_value, 0, 0, None, 0),
                ("part", z_kept, first_got, n_value + 32, 1, z_rows // 2, 1, 1),
            ],
            after=(up_sent,),
        )
        first_got = swap_blk(first_sent, 2)
        z_got = swap_grp(z_sent, 2)
        (up_kept,), (up_sent,) = combine(
            pos, [("part", up_kept, up_got, 0, 1, ff_out // 2, 4, 0)], after=(first_sent,)
        )
        up_got = swap_blk(up_sent, 4)
        (first_kept, value_kept, table_kept, vectors), (first_sent,) = combine(
            pos,
            [
                ("part", first_kept, first_got, 0, 1, n_out, 4, 0),
                ("part", value_kept, first_got, 2 * n_out, 1, n_out // 2, 4, 0),
                ("part", table_kept, table_got, 0, 1, 2 * tab, None, 0),
                ("vec", vectors, first_got, 3 * n_out, 0, 0, None, 0),
            ],
            after=(up_sent,),
        )
        first_got = swap_blk(first_sent, 4)
        early, (early_sent,) = combine(
            pos,
            [
                ("sum", down_kept, down_got, 0, 0, 0, None, 0),
                ("sum", z_kept, z_got, 0, 0, 0, None, 0),
            ],
            after=(first_sent,),
        )
        early_got = swap_grp(early_sent, 2)
        (up_part,), _ = combine(
            pos, [("sum", up_kept, up_got, 0, 0, 0, None, None)], after=(early_sent,)
        )
        n_small = n_out + n_out // 2
        (first_part, value_part, table_part, vectors), _ = combine(
            pos,
            [
                ("sum", first_kept, first_got, 0, 0, 0, None, None),
                ("sum", value_kept, first_got, n_out, 0, 0, None, None),
                ("sum", table_kept, first_got, n_small, 0, 0, None, None),
                ("vec", vectors, first_got, n_small + 2 * tab, 0, 0, None, None),
            ],
            after=(up_part,),
        )

        def whole(value, other):
            return pick(x_bit, value, other), pick(x_bit, other, value)

        low, high = whole(early_sent, early_got)
        early = jnp.concatenate([low[:part], high[:part], low[part:], high[part:]], axis=0)
        up_rows = jnp.concatenate(whole(up_part, swap_grp(up_part, 2)), axis=0)
        square = jnp.concatenate([first_part, value_part], axis=0)
        near_core = swap_grp(jnp.concatenate([square, vectors.astype(BF)], axis=0), 1)
        near, far = (square, swap_grp(square, 2)), (near_core[:n_small], swap_grp(square, 3))
        vectors = vectors + f(near_core[n_small:])
        sides = []
        for value, other in (near, far):
            low, high = pick(x_bit, value, other), pick(x_bit, other, value)
            sides.append(jnp.concatenate([low[:n_out], high[:n_out], low[n_out:], high[n_out:]], axis=0))
        square = (f(pick(core_bit, *sides)), f(pick(core_bit, *sides[::-1])))
        table_share = f(table_part)
    else:
        context_t, middle_t, act_t, grad_ffn, grad_pre, grad_attn = made
        lanes = lambda value, index: lax.dynamic_slice_in_dim(value, index * (value.shape[1] // 2), value.shape[1] // 2, 1)
        rows_of = lambda value, index: lax.dynamic_slice_in_dim(value, index * (value.shape[0] // 2), value.shape[0] // 2, 0)
        blocked = lambda value: value.reshape(blocks, value.shape[0] // blocks, value.shape[1])
        grad_queries, grad_keys_t, grad_values_t = attend_back(*back_args, ())
        table_kept, table_sent, grad_input_local, vectors = input_grads(
            blocks, grad_queries, grad_keys_t, grad_values_t, *input_args, ()
        )

        def packet(index):
            up = blocked(fwd_dot(middle_t, lanes(grad_pre, index)))
            return jnp.concatenate(
                [
                    blocked(fwd_dot(x_t[:, n_table:], lanes(grad_queries, index))),
                    blocked(back_dot(x_t, rows_of(grad_keys_t, index))),
                    blocked(back_dot(x_t, rows_of(grad_values_t, index))),
                    blocked(fwd_dot(context_t, lanes(grad_attn, index))),
                ]
                + [up[:, :, i : i + half_width] for i in range(0, up.shape[2], half_width)]
                + [blocked(fwd_dot(act_t, lanes(grad_ffn, index)))],
                axis=1,
            )

        total = (packet(core_bit) + f(swap_grp(packet(1 - core_bit).astype(BF), 1))).astype(BF)
        total = lax.psum_scatter(total, "blk", scatter_dimension=0, tiled=False)
        total = (f(total) + f(swap_grp(total, 2))).astype(BF)
        at = 4 * n_out
        square = total[: 3 * n_out]
        up_rows = total[at : at + ff_out]
        down_all = total[at + ff_out :]
        z_rows = jnp.concatenate([down_all[:first_rows], total[3 * n_out : at]], axis=0)
        down_rows = down_all[first_rows:]
        table_rows = jnp.stack([blocked_half.reshape(planes, 2 * tab, half_width) for blocked_half in (table_kept, table_sent)], axis=1)
        table_rows = table_rows.reshape(blocks, 2 * tab, half_width)
        table_rows = jnp.take(table_rows, jnp.arange(blocks) ^ own, axis=0)
        table_share = f(lax.psum_scatter(table_rows, "blk", scatter_dimension=0, tiled=False))
        vectors = lax.psum(vectors, ("blk", "grp"))
        early = jnp.concatenate([down_rows, z_rows], axis=0)

    def both_cores(value):
        other = swap_grp(value, 1)
        return f(pick(core_bit, value, other)), f(pick(core_bit, other, value))

    sides = both_cores(up_rows)
    out_up = jnp.concatenate([side[i : i + n_out] for side in sides for i in range(0, ff_out, n_out)], axis=1)
    sides = both_cores(early)
    at_z = ff_out - first_rows
    out_down = jnp.concatenate(
        [
            jnp.concatenate([side[at_z : at_z + first_rows] for side in sides], axis=1),
            jnp.concatenate([side[:at_z] for side in sides], axis=1),
        ],
        axis=0,
    )
    out_out = jnp.concatenate([side[at_z + first_rows :] for side in sides], axis=1)
    square = jnp.concatenate(square if packets else both_cores(square), axis=1)
    table_share = jnp.concatenate([table_share[:tab], table_share[tab:]], axis=1)
    vectors = jnp.concatenate([vectors[:16], vectors[16:]], axis=1)
    mine = lax.dynamic_slice_in_dim(vectors[:10], own * n_out, n_out, 1)
    up_bias_out = lax.dynamic_slice_in_dim(vectors[10:14].reshape(-1), own * ff_out, ff_out, 0)
    grad_input = grad_input_local.at[:tab].add(table_share)
    return (
        mixed,
        grad_input,
        mine[:2],
        square[:n_out],
        mine[2],
        square[n_out : 2 * n_out],
        square[2 * n_out :],
        mine[3],
        out_out,
        mine[4],
        mine[5],
        mine[6],
        out_up,
        up_bias_out,
        out_down,
        mine[7],
        mine[8],
        mine[9],
    )


def solution(mesh):
    both = ("grp", "blk")
    placed = (P(both, None), P(both), P(both), P(both)) + (P(),) * 16 + (P(both, None),)
    vec, mat = P("blk"), P("blk", None)
    return jax.shard_map(
        local,
        mesh=mesh,
        in_specs=placed,
        out_specs=(
            P(both, None), P(both, None), P(None, "blk"), mat, vec, mat, mat, vec, mat, vec,
            vec, vec, mat, vec, mat, vec, vec, vec,
        ),
        check_vma=False,
    )
```

```python
import math

import jax
import jax.numpy as jnp
from jax import lax
from jax.experimental import pallas as pl
from jax.experimental.pallas import tpu as pltpu
from jax.sharding import PartitionSpec as P

HEADS = 12
HEAD_DIM = 64
TAB_MAX = 64
LANES = 256
far_below = -1e30
BF = jnp.bfloat16
F32 = jnp.float32
MIB = 1 << 20
LONG = pl.CostEstimate(flops=40_000_000_000, bytes_accessed=MIB, transcendentals=0)
SHORT = pl.CostEstimate(flops=100000000, bytes_accessed=MIB, transcendentals=0)
HBM = pl.BlockSpec(memory_space=pltpu.HBM)


def outer_sum(left, right):
    return lax.dot_general(left, right, (((0,), (0,)), ((), ())), preferred_element_type=F32)


def back_dot(left, right):
    return lax.dot_general(left, right, (((1,), (1,)), ((), ())), preferred_element_type=F32)


def fwd_dot(left, right):
    return jnp.dot(left, right, preferred_element_type=F32)


def norm_parts(values):
    centred = values - jnp.mean(values, axis=-1, keepdims=True)
    spread = jnp.mean(centred * centred, axis=-1, keepdims=True)
    inv = lax.rsqrt(spread + 1e-06)
    return centred * inv, inv


def norm_grad(grad, normed, inv, gain):
    scaled = grad * gain
    return inv * (
        scaled
        - jnp.mean(scaled, axis=-1, keepdims=True)
        - normed * jnp.mean(scaled * normed, axis=-1, keepdims=True)
    )


def head_lanes(shape, index):
    lane = lax.broadcasted_iota(jnp.int32, shape, len(shape) - 1)
    return (lane >= index * HEAD_DIM) & (lane < (index + 1) * HEAD_DIM)


def column_of(row):
    return jnp.broadcast_to(row, (128, row.shape[1])).T[:, :1]


def start_copies(sources, targets, sems):
    copies = [pltpu.make_async_copy(a, b, sems.at[i]) for i, (a, b) in enumerate(zip(sources, targets))]
    for copy in copies:
        copy.start()
    return copies


def entry_kernel(tokens_any, seg_any, prev_any, answer_any, payload_ref, input_ref, *scratch):
    tab = TAB_MAX
    *held, sems = scratch
    for copy in start_copies((tokens_any, seg_any, prev_any, answer_any), held, sems):
        copy.wait()
    tokens_ref, seg_ref, prev_ref, answer_ref = held
    prev = prev_ref[...].astype(F32)[None]
    low = residual(tokens_ref, prev, answer_ref).astype(BF)
    input_ref[...] = low
    payload_ref[:tab] = low[:tab]
    payload_ref[tab:] = jnp.zeros((16, low.shape[1]), BF)
    lane = lax.broadcasted_iota(jnp.int32, (1, 128), 1)

    def twice(row):
        row = row[:, :128]
        return jnp.where(lane < tab, row, pltpu.roll(row, tab, 1))

    is_open = twice(jnp.where(seg_ref[...] == 0, 1.0, 0.0)[None])
    both = jnp.concatenate([is_open, twice(prev)], axis=1)
    payload_ref[tab:, :256] = jnp.broadcast_to(both, (16, 256)).astype(BF)


def residual(tokens_ref, prev, answer_ref):
    answers = answer_ref[...].astype(F32)
    return tokens_ref[...].astype(F32) + jnp.where(column_of(prev) == 1.0, answers[1:2], answers[0:1])


def entry(tokens, seg, prev, answers):
    rows, width = tokens.shape
    vmem = pl.BlockSpec(memory_space=pltpu.VMEM)
    return pl.pallas_call(
        entry_kernel,
        in_specs=[HBM] * 4,
        out_specs=[vmem] * 2,
        out_shape=[jax.ShapeDtypeStruct((TAB_MAX + 16, width), BF), jax.ShapeDtypeStruct((rows, width), BF)],
        scratch_shapes=[pltpu.VMEM(v.shape, v.dtype) for v in (tokens, seg, prev, answers)]
        + [pltpu.SemaphoreType.DMA((4,))],
        compiler_params=pltpu.CompilerParams(vmem_limit_bytes=60 * MIB),
    )(tokens, seg, prev, answers)


def own_kernel(
    input_ref, query_w_any, key_w_any, value_w_any, query_b_any, value_b_any, seg_any, turn_any,
    q_ref, k_ref, v_ref, bias_ref, value_row_ref, *scratch
):
    *held, sems = scratch
    query_w_ref, key_w_ref, value_w_ref, query_b_ref, value_b_ref, seg_ref, turn_ref = held
    sources = (query_w_any, key_w_any, value_w_any, query_b_any, value_b_any, seg_any, turn_any)
    for copy in start_copies(sources, held, sems):
        copy.wait()
    low = input_ref[...]
    query = fwd_dot(low, query_w_ref[...]) + query_b_ref[...].astype(F32)[None]
    q_ref[...] = (query.astype(BF).astype(F32) * HEAD_DIM**-0.5).astype(BF)
    k_ref[...] = fwd_dot(low, key_w_ref[...]).astype(BF)
    value_b = value_b_ref[...].astype(F32)[None]
    value_row_ref[...] = value_b
    v_ref[...] = (fwd_dot(low, value_w_ref[...]) + value_b).astype(BF)
    turn = turn_ref[...].astype(F32)[None]
    seg = seg_ref[...].astype(F32)[None]
    same = (column_of(turn) == turn) & (seg != 0.0)
    bias_ref[...] = jnp.where(same, 0.0, far_below)


def own_part(layer_input, query_w, key_w, value_w, query_b, value_b, seg, turn):
    rows, width = layer_input.shape
    vmem = pl.BlockSpec(memory_space=pltpu.VMEM)
    return pl.pallas_call(
        own_kernel,
        in_specs=[vmem] + [HBM] * 7,
        out_specs=[vmem] * 5,
        out_shape=[jax.ShapeDtypeStruct((rows, width), BF)] * 3
        + [jax.ShapeDtypeStruct((rows, rows), F32), jax.ShapeDtypeStruct((1, width), F32)],
        scratch_shapes=[
            pltpu.VMEM(v.shape, v.dtype) for v in (query_w, key_w, value_w, query_b, value_b, seg, turn)
        ]
        + [pltpu.SemaphoreType.DMA((7,))],
        compiler_params=pltpu.CompilerParams(vmem_limit_bytes=60 * MIB),
        cost_estimate=pl.CostEstimate(flops=100000000, bytes_accessed=MIB, transcendentals=0),
    )(layer_input, query_w, key_w, value_w, query_b, value_b, seg, turn)


def attend_kernel(
    views, input_ref, key_w_ref, value_w_ref, value_b_ref, q_ref, own_k_ref, own_v_ref, own_bias_ref, *refs
):
    *parts, keys_ref, values_ref, prob_ref, context_ref, x_t_ref, prev_ref, table_ref, bias_ref = refs
    n_table = table_ref.shape[0]
    tab = TAB_MAX
    slots = [parts[part].at[first : first + tab + 16] for part, first in views]

    @pl.when(pl.program_id(0) == 0)
    def _():
        lane = lax.broadcasted_iota(jnp.int32, (1, 128), 1)
        for i, slot in enumerate(slots):
            table_ref[i * tab : (i + 1) * tab] = slot[:tab]
        for i in range(0, len(slots), 2):
            marks = jnp.where(
                lax.broadcasted_iota(jnp.int32, (16, 256), 1) % 128 < tab,
                slots[i][tab:, :256].astype(F32), slots[i + 1][tab:, :256].astype(F32),
            )
            at = slice(i * tab, (i + 2) * tab)
            closed = jnp.where(marks[:1, :128] > 0.5, 0.0, far_below)
            bias_ref[:, at] = jnp.broadcast_to(closed, (bias_ref.shape[0], 128))
            prev_ref[:, at] = marks[:8, 128:]
        bias_ref[:, n_table:] = own_bias_ref[...]
        x_t_ref[:, :n_table] = table_ref[...].T
        x_t_ref[:, n_table:] = input_ref[...].T

    table = table_ref[...]
    keys_ref[:n_table] = fwd_dot(table, key_w_ref[...]).astype(BF)
    values_ref[:n_table] = (fwd_dot(table, value_w_ref[...]) + value_b_ref[...]).astype(BF)
    keys_ref[n_table:] = own_k_ref[...]
    values_ref[n_table:] = own_v_ref[...]
    queries = q_ref[...]
    context = jnp.zeros(context_ref.shape, F32)
    for h in range(queries.shape[1] // HEAD_DIM):
        mask = head_lanes(queries.shape, h)
        picked = jnp.where(mask, queries, jnp.zeros_like(queries))
        scores = back_dot(picked, keys_ref[...]) + bias_ref[...]
        top = jnp.max(scores, axis=-1, keepdims=True)
        weights = jnp.exp(scores - top)
        prob = (weights * (1.0 / jnp.sum(weights, axis=-1, keepdims=True))).astype(BF)
        prob_ref[h] = prob
        context = jnp.where(mask, fwd_dot(prob, values_ref[...]), context)
    context_ref[...] = context


def vmem_limit(n_keys, small):
    return (small if n_keys <= 1024 else 60) * MIB


def attend(parts, views, layer_input, key_w, value_w, value_b, queries, own_k, own_v, own_bias):
    rows, width = queries.shape
    n_table = len(views) * TAB_MAX
    n_keys = n_table + rows
    group = LANES if n_keys <= 1024 else LANES // 2
    per = group // HEAD_DIM
    steady = {} if n_keys <= 1024 else {"pipeline_mode": pl.Buffered(1)}
    whole = lambda shape: pl.BlockSpec(shape, lambda i: (0, 0), **steady)
    lanes = lambda n: pl.BlockSpec((n, group), lambda i: (0, i))
    return pl.pallas_call(
        lambda *refs: attend_kernel(views, *refs),
        grid=(width // group,),
        in_specs=[
            whole((rows, width)), lanes(width), lanes(width), lanes(1), lanes(rows), lanes(rows), lanes(rows),
            whole((rows, rows)),
        ]
        + [whole(part.shape) for part in parts],
        out_specs=[
            lanes(n_keys), lanes(n_keys), pl.BlockSpec((per, rows, n_keys), lambda i: (i, 0, 0)), lanes(rows),
            whole((width, n_keys)), whole((8, n_table)),
        ],
        out_shape=[
            jax.ShapeDtypeStruct((n_keys, width), BF),
            jax.ShapeDtypeStruct((n_keys, width), BF),
            jax.ShapeDtypeStruct((HEADS, rows, n_keys), BF),
            jax.ShapeDtypeStruct((rows, width), F32),
            jax.ShapeDtypeStruct((width, n_keys), BF),
            jax.ShapeDtypeStruct((8, n_table), F32),
        ],
        scratch_shapes=[pltpu.VMEM((n_table, width), BF), pltpu.VMEM((rows, n_keys), F32)],
        compiler_params=pltpu.CompilerParams(vmem_limit_bytes=vmem_limit(n_keys, 60)),
        cost_estimate=pl.CostEstimate(flops=100000000, bytes_accessed=MIB, transcendentals=0),
    )(layer_input, key_w, value_w, value_b, queries, own_k, own_v, own_bias, *parts)


def middle_kernel(
    packets, pos_ref, tokens_ref, prev_ref, answer_ref, context_ref, cot_ref, out_w_any, up_w_any, down_w_any,
    up_b_1d_ref, *refs
):
    biases, refs = refs[:6], refs[6:]
    mixed_ref, grad_context_ref, grad_mid_ref, sums_ref, up_sum_ref = refs[:5]
    refs = refs[5:]
    if packets:
        anys, refs = refs[:5], refs[5:]
    context_t_ref, middle_t_ref, act_t_ref, grad_ffn_ref, grad_pre_ref, grad_attn_ref = refs[:6]
    slope_ref, total_ref, middle_low_ref, out_w_ref, up_w_ref, down_w_ref, up_b_ref, sems = refs[6:14]
    width, hidden = up_w_ref.shape
    tile = width
    steps = hidden // tile

    def tile_copies(i):
        at = pl.ds(i * tile, tile)
        return (
            pltpu.make_async_copy(up_w_any.at[:, at], up_w_ref.at[:, at], sems.at[2 * i + 1]),
            pltpu.make_async_copy(down_w_any.at[at, :], down_w_ref.at[at, :], sems.at[2 * i + 2]),
        )

    out_copy = pltpu.make_async_copy(out_w_any, out_w_ref, sems.at[0])
    out_copy.start()
    for i in range(steps):
        for copy in tile_copies(i):
            copy.start()
    out_b, norm_g, norm_s, down_b, final_g, final_s = (ref[...].astype(F32)[None] for ref in biases)
    up_b_ref[...] = up_b_1d_ref[...].astype(F32)[None]
    resid = residual(tokens_ref, prev_ref[...].astype(F32)[None], answer_ref)
    column = lambda v: jnp.sum(v, axis=0, keepdims=True)
    context_low = context_ref[...].astype(BF)
    context_t_ref[...] = context_low.T
    out_copy.wait()
    normed1, inv1 = norm_parts(resid + fwd_dot(context_low, out_w_ref[...]) + out_b)
    middle = normed1 * norm_g + norm_s
    middle_low = middle.astype(BF)
    middle_low_ref[...] = middle_low
    middle_t_ref[...] = middle_low.T
    total_ref[...] = middle + down_b

    def forward(i):
        at = pl.ds(i * tile, tile)
        for copy in tile_copies(i):
            copy.wait()
        pre = fwd_dot(middle_low_ref[...], up_w_ref[:, at]) + up_b_ref[:, at]
        cdf = 0.5 * (1.0 + lax.erf(pre * (0.5**0.5)))
        act = (pre * cdf).astype(BF)
        act_t_ref[at, :] = act.T
        slope_ref[:, at] = cdf + pre * jnp.exp(-0.5 * pre * pre) * (1.0 / math.sqrt(2 * math.pi))
        total_ref[...] += fwd_dot(act, down_w_ref[at, :])

    for i in range(steps):
        forward(i)
    normed2, inv2 = norm_parts(total_ref[...])
    mixed_ref[...] = (normed2 * final_g + final_s).astype(BF)
    cot = cot_ref[...].astype(F32)
    grad_final = norm_grad(cot, normed2, inv2, final_g)
    grad_ffn = grad_final.astype(BF)
    grad_ffn_ref[...] = grad_ffn
    total_ref[...] = grad_final

    def backward(i, carry):
        at = pl.ds(pl.multiple_of(i * tile, tile), tile)
        grad_pre = (back_dot(grad_ffn_ref[...], down_w_ref[at, :]) * slope_ref[:, at]).astype(BF)
        grad_pre_ref[:, at] = grad_pre
        up_sum_ref[:, at] = column(grad_pre.astype(F32))
        total_ref[...] += back_dot(grad_pre, up_w_ref[:, at])
        return carry

    copies = []
    if packets:
        blocks = packets
        sent_ref, down_own_ref, z_own_ref, up_sent_ref, up_own_ref, out_sems = refs[14:]
        half = width // 2
        small, size = width // blocks, hidden // blocks
        first_rows = 2 * small // 3
        z_rows, rows = first_rows + small, size - first_rows
        core = pos_ref[0]
        n_down = blocks * rows

        def leave(source, target):
            copy = pltpu.make_async_copy(source, target, out_sems.at[len(copies)])
            copy.start()
            copies.append(copy)

        def lanes_of(own):
            return pl.ds(pl.multiple_of((core if own else 1 - core) * half, 128), half)

        for own, down_ref, first_z, z_ref in ((False, sent_ref, n_down, sent_ref), (True, down_own_ref, 0, z_own_ref)):
            part = grad_ffn_ref[:, lanes_of(own)]
            for b in range(blocks):
                value = fwd_dot(act_t_ref[b * size : (b + 1) * size], part).astype(BF)
                down_ref[b * rows : (b + 1) * rows] = value[first_rows:]
                z_ref[first_z + b * z_rows : first_z + b * z_rows + first_rows] = value[:first_rows]
            leave(down_ref.at[:n_down], (anys[1] if own else anys[0].at[:n_down]))
        for i in range(steps):
            t = lax.rem(2 * (1 - core) + i, steps)
            backward(t, 0)
            value = fwd_dot(middle_t_ref[...], grad_pre_ref[:, pl.ds(pl.multiple_of(t * tile, tile), tile)]).astype(BF)
            target = up_sent_ref if i < steps // 2 else up_own_ref
            for b in range(blocks):
                for q in range(2):
                    first = b * size + (2 * (i % (steps // 2)) + q) * small
                    target[first : first + small] = value[b * small : (b + 1) * small, q * half : (q + 1) * half]
            if i == steps // 2 - 1:
                leave(up_sent_ref, anys[3])
        leave(up_own_ref, anys[4])
    else:
        lax.fori_loop(0, steps, backward, 0)
    grad_middle = total_ref[...]
    grad_mid = norm_grad(grad_middle, normed1, inv1, norm_g)
    grad_mid_ref[...] = grad_mid
    grad_attn = grad_mid.astype(BF)
    grad_attn_ref[...] = grad_attn
    if packets:
        for own, first_z, z_ref in ((False, n_down, sent_ref), (True, 0, z_own_ref)):
            value = fwd_dot(context_t_ref[...], grad_attn_ref[:, lanes_of(own)]).astype(BF)
            for b in range(blocks):
                first = first_z + b * z_rows + first_rows
                z_ref[first : first + small] = value[b * small : (b + 1) * small]
            if own:
                leave(z_own_ref, anys[2])
            else:
                leave(sent_ref.at[n_down:], anys[0].at[n_down:])
    grad_context_ref[...] = back_dot(grad_attn, out_w_ref[...]).astype(BF)
    sums_ref[0:1] = column(grad_attn.astype(F32))
    sums_ref[1:2] = column(grad_middle * normed1)
    sums_ref[2:3] = column(grad_middle)
    sums_ref[3:4] = column(grad_ffn.astype(F32))
    sums_ref[4:5] = column(cot * normed2)
    sums_ref[5:6] = column(cot)
    sums_ref[6:8] = jnp.zeros((2, sums_ref.shape[1]), F32)
    for copy in copies:
        copy.wait()


def middle_part(packets, pos, tokens, prev, answers, context, cot, out_w, up_w, down_w, up_b, *biases):
    rows, width = tokens.shape
    hidden = up_w.shape[1]
    half = width // 2
    vmem, away = pl.BlockSpec(memory_space=pltpu.VMEM), pl.BlockSpec(memory_space=pl.ANY)
    shape = lambda n, t: jax.ShapeDtypeStruct((rows, n), t)
    turned = lambda n: jax.ShapeDtypeStruct((n, rows), BF)
    inner = [turned(width), turned(width), turned(hidden), shape(width, BF), shape(hidden, BF), shape(width, BF)]
    held = lambda shapes: [pltpu.VMEM(v.shape, v.dtype) for v in shapes]
    outs = [
        shape(width, BF), shape(width, BF), shape(width, F32), jax.ShapeDtypeStruct((8, width), F32),
        jax.ShapeDtypeStruct((1, hidden), F32),
    ]
    scratch = [
        pltpu.VMEM((rows, hidden), F32), pltpu.VMEM((rows, width), F32), pltpu.VMEM((rows, width), BF),
        pltpu.VMEM(out_w.shape, BF), pltpu.VMEM(up_w.shape, BF), pltpu.VMEM(down_w.shape, BF),
        pltpu.VMEM((1, hidden), F32), pltpu.SemaphoreType.DMA((1 + 2 * (hidden // width),)),
    ]
    specs = [vmem] * 5
    if packets:
        first_rows = 2 * width // 3
        z_rows, down_rows = first_rows + width, hidden - first_rows
        packed = [
            jax.ShapeDtypeStruct((n, half), BF) for n in (down_rows + z_rows, down_rows, z_rows, hidden, hidden)
        ]
        scratch = held(inner) + scratch + held(packed) + [pltpu.SemaphoreType.DMA((6,))]
        outs, specs = outs + packed, specs + [away] * 5
    else:
        outs, specs = outs + inner, specs + [vmem] * 6
    return pl.pallas_call(
        lambda *refs: middle_kernel(packets, *refs),
        in_specs=[pl.BlockSpec(memory_space=pltpu.SMEM)] + [vmem] * 5 + [HBM] * 3 + [vmem] * 7,
        out_specs=specs,
        out_shape=outs,
        scratch_shapes=scratch,
        compiler_params=pltpu.CompilerParams(vmem_limit_bytes=60 * MIB),
        cost_estimate=pl.CostEstimate(flops=100000000, bytes_accessed=MIB, transcendentals=0),
    )(pos, tokens, prev, answers, context, cot, out_w, up_w, down_w, up_b, *biases)


def attend_back_kernel(
    q_ref, keys_ref, values_ref, prob_ref, context_ref, grad_ref, *refs
):
    grad_q_ref, grad_k_ref, grad_v_ref = refs[-3:]
    grad = grad_ref[...]
    grad_f = grad.astype(F32)
    product = grad_f * context_ref[...]
    grad_t = grad_f.T.astype(BF)
    q_t = q_ref[...].astype(F32).T.astype(BF)
    grad_q = jnp.zeros(grad.shape, F32)
    for h in range(grad.shape[1] // HEAD_DIM):
        mask = head_lanes(grad.shape, h)
        at = slice(h * HEAD_DIM, (h + 1) * HEAD_DIM)
        row_dot = jnp.sum(jnp.where(mask, product, 0.0), axis=-1, keepdims=True)
        grad_prob = back_dot(jnp.where(mask, grad, jnp.zeros_like(grad)), values_ref[...])
        prob = prob_ref[h]
        grad_score = (prob.astype(F32) * (grad_prob - row_dot)).astype(BF)
        grad_v_ref[at] = fwd_dot(grad_t[at], prob).astype(BF)
        grad_k_ref[at] = fwd_dot(q_t[at], grad_score).astype(BF)
        grad_q = jnp.where(mask, fwd_dot(grad_score, keys_ref[...]), grad_q)
    grad_q_ref[...] = (grad_q * HEAD_DIM**-0.5).astype(BF)


def attend_back(queries, keys, values, prob, context, grad_context, after):
    rows, width = queries.shape
    n_keys = keys.shape[0]
    group = LANES if n_keys <= 1024 else LANES // 2
    per = group // HEAD_DIM
    lanes = lambda n: pl.BlockSpec((n, group), lambda i: (0, i))
    return pl.pallas_call(
        attend_back_kernel,
        grid=(width // group,),
        in_specs=[
            lanes(rows), lanes(n_keys), lanes(n_keys), pl.BlockSpec((per, rows, n_keys), lambda i: (i, 0, 0)),
            lanes(rows), lanes(rows),
        ]
        + [pl.BlockSpec(memory_space=pl.ANY)] * len(after),
        out_specs=[lanes(rows)] + [pl.BlockSpec((group, n_keys), lambda i: (i, 0))] * 2,
        out_shape=[
            jax.ShapeDtypeStruct((rows, width), BF),
            jax.ShapeDtypeStruct((width, n_keys), BF),
            jax.ShapeDtypeStruct((width, n_keys), BF),
        ],
        compiler_params=pltpu.CompilerParams(vmem_limit_bytes=vmem_limit(n_keys, 60)),
        cost_estimate=LONG,
    )(queries, keys, values, prob, context, grad_context, *after)


def core_lanes(pos_ref, own, size):
    core = pos_ref[0] if own else 1 - pos_ref[0]
    return pl.ds(pl.multiple_of(core * size, 128), size)


def qkv_values(own, pos_ref, x_t_ref, grad_q_ref, grad_k_ref, grad_v_ref, blocks, store):
    half = grad_q_ref.shape[1] // 2
    n_table = x_t_ref.shape[1] - grad_q_ref.shape[0]
    small = x_t_ref.shape[0] // blocks
    at = core_lanes(pos_ref, own, half)
    core = pos_ref[0] if own else 1 - pos_ref[0]
    rows = pl.ds(pl.multiple_of(core * half, 128), half)
    values = (
        fwd_dot(x_t_ref[:, n_table:], grad_q_ref[:, at]),
        back_dot(x_t_ref[...], grad_k_ref[rows, :]),
        back_dot(x_t_ref[...], grad_v_ref[rows, :]),
    )
    for i, value in enumerate(values):
        for b in range(blocks):
            store(b, i * small, value[b * small : (b + 1) * small])


def send_kernel(make, n_in, blocks, *refs):
    pos_ref, out_ref = refs[0], refs[-1]

    def store(b, first, value):
        out_ref[b, first : first + value.shape[0]] = value.astype(BF)

    make(False, pos_ref, *refs[1 : 1 + n_in], blocks, store)


def pick(bit, first, second):
    return jnp.where(bit == 0, first, second)


def keep_qkv_kernel(
    blocks, pos_ref, x_t_ref, grad_q_ref, grad_k_ref, grad_v_ref, got_ref, table_ref, vec_ref, *outs
):
    first_kept_ref, first_sent_ref, kept_ref, sent_ref = outs
    small = x_t_ref.shape[0] // blocks
    planes = blocks // 2
    held = {}

    def store(b, first, value):
        value = (value + got_ref[b, first : first + small].astype(F32)).astype(BF)
        held[b, first] = value
        if first == small:
            query = held.pop((b, 0))
            rows = slice(b * small, (b + 1) * small)
            first_kept_ref[rows] = pick(pos_ref[1], query, value)
            first_sent_ref[rows] = pick(pos_ref[1], value, query)
        if first == 2 * small and b % 2 == 1:
            rows = slice(b // 2 * small, (b // 2 + 1) * small)
            kept_ref[rows] = pick(pos_ref[2], held[b - 1, first], value)
            sent_ref[rows] = pick(pos_ref[2], value, held[b - 1, first])

    qkv_values(True, pos_ref, x_t_ref, grad_q_ref, grad_k_ref, grad_v_ref, blocks, store)
    first_sent_ref[blocks * small :] = vec_ref[...].astype(BF)
    sent_ref[planes * small :] = table_ref[...]


def inputs_kernel(
    blocks, grad_q_ref, grad_k_ref, grad_v_ref, query_w_ref, key_w_ref, value_w_ref, grad_mid_ref, prev_ref,
    table_prev_ref, sums_ref, up_sum_ref, *refs
):
    table_kept_ref, table_sent_ref, grad_ref, vec_ref = refs[-4:]
    tab = TAB_MAX
    n_table = blocks * tab
    rows, width = grad_q_ref.shape
    half = width // 2
    own = fwd_dot(key_w_ref[...], grad_k_ref[:, n_table:]) + fwd_dot(value_w_ref[...], grad_v_ref[:, n_table:])
    grad = grad_mid_ref[...] + back_dot(grad_q_ref[...], query_w_ref[...]) + own.T
    grad_ref[...] = grad
    is_one = column_of(prev_ref[...].astype(F32)[None]) == 1.0
    one_sum = jnp.sum(jnp.where(is_one, grad, 0.0), axis=0, keepdims=True)
    zero_sum = jnp.sum(jnp.where(is_one, 0.0, grad), axis=0, keepdims=True)
    step = min(n_table, 512)
    row = lax.broadcasted_iota(jnp.int32, (8, step), 0)
    for first in range(0, n_table, step):
        at = slice(first, first + step)
        part = (fwd_dot(key_w_ref[...], grad_k_ref[:, at]) + fwd_dot(value_w_ref[...], grad_v_ref[:, at])).astype(BF)
        marks = table_prev_ref[:, at]
        marks = jnp.where(row == 0, marks, 1.0 - marks).astype(BF)
        table_sums = back_dot(marks, part)
        one_sum += table_sums[0:1]
        zero_sum += table_sums[1:2]
        for j in range(step // 128):
            pair = part[:, j * 128 : (j + 1) * 128].T
            slot = first // 128 + j
            for k, ref in enumerate((table_kept_ref, table_sent_ref)):
                for side in range(2):
                    ref[(slot * 2 + side) * tab : (slot * 2 + side + 1) * tab] = pair[
                        k * tab : (k + 1) * tab, side * half : (side + 1) * half
                    ]
    ones = jnp.ones((8, grad_v_ref.shape[1]), BF)
    lines = [
        zero_sum,
        one_sum,
        jnp.sum(grad_q_ref[...].astype(F32), axis=0, keepdims=True),
        back_dot(ones, grad_v_ref[...])[0:1],
    ]
    lines += [sums_ref[i : i + 1] for i in range(6)]
    lines += [up_sum_ref[:, i * width : (i + 1) * width] for i in range(up_sum_ref.shape[1] // width)]
    vec_ref[...] = jnp.zeros(vec_ref.shape, F32)
    for i, line in enumerate(lines):
        for side in range(2):
            vec_ref[side * 16 + i : side * 16 + i + 1] = line[:, side * half : (side + 1) * half]


def input_grads(blocks, grad_q, grad_k, grad_v, query_w, key_w, value_w, grad_mid, prev, table_prev, sums, up_sum, after):
    rows, width = grad_q.shape
    n_half = blocks * TAB_MAX
    vmem = pl.BlockSpec(memory_space=pltpu.VMEM)
    args = (grad_q, grad_k, grad_v, query_w, key_w, value_w, grad_mid, prev, table_prev, sums, up_sum)
    return pl.pallas_call(
        lambda *refs: inputs_kernel(blocks, *refs),
        in_specs=[vmem] * len(args) + [pl.BlockSpec(memory_space=pl.ANY)] * len(after),
        out_specs=[vmem] * 4,
        out_shape=[
            jax.ShapeDtypeStruct((n_half, width // 2), BF),
            jax.ShapeDtypeStruct((n_half, width // 2), BF),
            jax.ShapeDtypeStruct((rows, width), F32),
            jax.ShapeDtypeStruct((32, width // 2), F32),
        ],
        compiler_params=pltpu.CompilerParams(vmem_limit_bytes=(20 if blocks <= 8 else 56) * MIB),
        cost_estimate=LONG,
    )(*args, *after)


def combine(pos, items, after=()):
    width = items[0][1].shape[1]
    gots, shapes, heights, places = [], [], {}, []
    for kind, kept, got, first, outer, inner, bit, message in items:
        if got is not None and not any(got is g for g in gots):
            gots.append(got)
        rows = kept.shape[0] if kind != "part" else outer * inner
        if kind != "copy":
            shapes.append(jax.ShapeDtypeStruct((rows, width), kept.dtype))
        if message is not None:
            places.append(heights.get(message, 0))
            heights[message] = places[-1] + rows
        else:
            places.append(None)
    sizes = [heights[m] for m in sorted(heights)]
    shapes += [jax.ShapeDtypeStruct((n, width), BF) for n in sizes]
    which = [next((i for i, g in enumerate(gots) if g is item[2]), None) for item in items]
    n_outs = sum(item[0] != "copy" for item in items)

    def body(pos_ref, *refs):
        kept_refs, refs = refs[: len(items)], refs[len(items) :]
        got_refs, refs = refs[: len(gots)], refs[len(gots) + len(after) :]
        out_refs, sent_refs = list(refs[:n_outs]), refs[n_outs:]
        for i, (kind, _, _, first, outer, inner, bit, message) in enumerate(items):
            kept_ref = kept_refs[i]
            n = kept_ref.shape[0]
            if kind == "copy":
                sent_refs[message][places[i] : places[i] + n] = kept_ref[...]
                continue
            got_ref, out_ref = got_refs[which[i]], out_refs.pop(0)
            if kind == "vec":
                total = kept_ref[...] + got_ref[first : first + n].astype(F32)
                out_ref[...] = total
                if message is not None:
                    sent_refs[message][places[i] : places[i] + n] = total.astype(BF)
            elif kind == "sum":
                total = kept_ref[...].astype(F32) + got_ref[first : first + n].astype(F32)
                out_ref[...] = total.astype(BF)
                if message is not None:
                    sent_refs[message][places[i] : places[i] + n] = total.astype(BF)
            else:
                for o in range(outer):
                    halves = []
                    for side in range(2):
                        at = (2 * o + side) * inner
                        total = kept_ref[at : at + inner].astype(F32)
                        total = total + got_ref[first + at : first + at + inner].astype(F32)
                        halves.append(total.astype(BF))
                    rows = slice(places[i] + o * inner, places[i] + (o + 1) * inner)
                    if bit is None:
                        out_ref[o * inner : (o + 1) * inner], sent_refs[message][rows] = halves
                    else:
                        out_ref[o * inner : (o + 1) * inner] = pick(pos_ref[bit], *halves)
                        sent_refs[message][rows] = pick(pos_ref[bit], *halves[::-1])

    vmem = pl.BlockSpec(memory_space=pltpu.VMEM)
    results = pl.pallas_call(
        body,
        in_specs=[pl.BlockSpec(memory_space=pltpu.SMEM)]
        + [vmem] * (len(items) + len(gots))
        + [pl.BlockSpec(memory_space=pl.ANY)] * len(after),
        out_specs=[vmem] * len(shapes),
        out_shape=shapes,
        compiler_params=pltpu.CompilerParams(vmem_limit_bytes=16 * MIB),
        cost_estimate=LONG,
    )(pos, *[item[1] for item in items], *gots, *after)
    return results[:n_outs], results[n_outs:]


def packet_call(kernel, shapes, pos, args, after=(), scratch=(), wide=(), cost=LONG):
    smem, vmem = pl.BlockSpec(memory_space=pltpu.SMEM), pl.BlockSpec(memory_space=pltpu.VMEM)
    outs = [jax.ShapeDtypeStruct(shape, BF) for shape in shapes]
    outs += [jax.ShapeDtypeStruct(shape, F32) for shape in wide]

    def body(*refs):
        n = 1 + len(args)
        kernel(*refs[:n], *refs[n + len(after) :])

    return pl.pallas_call(
        body,
        in_specs=[smem] + [vmem] * len(args) + [pl.BlockSpec(memory_space=pl.ANY)] * len(after),
        out_specs=[vmem] * len(outs),
        out_shape=outs,
        scratch_shapes=list(scratch),
        compiler_params=pltpu.CompilerParams(vmem_limit_bytes=20 * MIB),
        cost_estimate=cost,
    )(pos, *args, *after)


def local(
    tokens, seg_ids, turn_ids, prev_ids, answer_table, query_weight, query_bias,
    key_weight, value_weight, value_bias, out_weight, out_bias, norm_gain, norm_shift,
    up_weight, up_bias, down_weight, down_bias, final_gain, final_shift, cotangent,
):
    rows, width = tokens.shape
    blocks = lax.axis_size("blk")
    grps = lax.axis_size("grp")
    tab = TAB_MAX
    scale = HEAD_DIM ** (-0.5)
    f = lambda v: v.astype(F32)
    core_bit = lax.axis_index("grp") & 1
    x_bit = lax.axis_index("grp") >> 1
    own = lax.axis_index("blk")
    planes = blocks // 2
    n_out = width // blocks
    ff_out = up_weight.shape[1] // blocks
    half_width = width // 2
    n_table = blocks * tab
    pos = jnp.stack([core_bit, x_bit, own & 1, (own >> 1) & 1, own >> 2]).astype(jnp.int32)

    def swap_grp(value, mask):
        return lax.ppermute(value, "grp", [(i, i ^ mask) for i in range(grps)])

    def swap_blk(value, mask):
        return lax.ppermute(value, "blk", [(i, i ^ mask) for i in range(blocks)])

    payload, layer_input = entry(tokens, seg_ids, prev_ids, answer_table)
    slots = [payload] + [None] * (blocks - 1)
    for k in range(1, planes):
        slots[2 * k] = swap_blk(payload, 2 * k)
    slots[1] = swap_blk(payload, 1)
    for k in range(1, planes):
        slots[2 * k + 1] = swap_blk(slots[2 * k], 1)
    queries, own_keys, own_values, own_bias, value_row = own_part(
        layer_input, query_weight, key_weight, value_weight, query_bias, value_bias, seg_ids, turn_ids
    )
    views = [(i, 0) for i in range(blocks)]
    keys, values, prob, context, x_t, table_prev = attend(
        slots, views, layer_input, key_weight, value_weight, value_row, queries, own_keys, own_values, own_bias
    )
    first_rows = 2 * n_out // 3
    def both_cores(value):
        other = swap_grp(value, 1)
        return f(pick(core_bit, value, other)), f(pick(core_bit, other, value))

    def big_outputs(up_rows, early):
        sides = both_cores(up_rows)
        out_up = jnp.concatenate([side[i : i + n_out] for side in sides for i in range(0, ff_out, n_out)], axis=1)
        sides = both_cores(early)
        at_z = ff_out - first_rows
        out_down = jnp.concatenate(
            [
                jnp.concatenate([side[at_z : at_z + first_rows] for side in sides], axis=1),
                jnp.concatenate([side[:at_z] for side in sides], axis=1),
            ],
            axis=0,
        )
        out_out = jnp.concatenate([side[at_z + first_rows :] for side in sides], axis=1)
        return out_up, out_down, out_out

    packets = blocks if blocks == 8 and n_out % 32 == 0 else 0
    mixed, grad_context, grad_mid_sum, sums, up_sum, *made = middle_part(
        packets, pos, tokens, prev_ids, answer_table, context, cotangent, out_weight, up_weight, down_weight, up_bias,
        out_bias, norm_gain, norm_shift, down_bias, final_gain, final_shift,
    )
    first_rows = 2 * n_out // 3
    part, z_rows = (ff_out - first_rows) // 2, n_out + first_rows
    back_args = (queries, keys, values, prob, context, grad_context)
    input_args = (query_weight, key_weight, value_weight, grad_mid_sum, prev_ids, table_prev, sums, up_sum)

    if packets:
        flat = lambda rows: (rows, half_width)
        down_sent, down_kept, z_kept, up_sent, up_kept = made
        down_got = swap_grp(down_sent, 1)
        up_got = swap_grp(up_sent, 1)
        grad_queries, grad_keys_t, grad_values_t = attend_back(*back_args, ())
        (down_kept, z_kept), (down_sent, z_sent) = combine(
            pos,
            [
                ("part", down_kept, down_got, 0, blocks, part, 1, 0),
                ("part", z_kept, down_got, 2 * blocks * part, 2, 2 * z_rows, 3, 1),
            ],
            after=(grad_queries,),
        )
        down_got = swap_grp(down_sent, 2)
        z_got = swap_blk(z_sent, 2)
        (up_kept,), (up_sent,) = combine(
            pos, [("part", up_kept, up_got, 0, planes, ff_out, 2, 0)], after=(down_sent,)
        )
        up_got = swap_blk(up_sent, 1)
        qkv_args = (x_t, grad_queries, grad_keys_t, grad_values_t)
        (qkv_sent,) = packet_call(
            lambda *refs: send_kernel(qkv_values, 4, blocks, *refs),
            [(blocks, 3 * n_out, half_width)], pos, qkv_args, after=(up_sent,),
        )
        qkv_got = swap_grp(qkv_sent, 1)
        table_kept, table_sent, grad_input_local, vectors = input_grads(
            blocks, grad_queries, grad_keys_t, grad_values_t, *input_args, (qkv_sent,)
        )
        (z_kept,), (z_sent,) = combine(pos, [("part", z_kept, z_got, 0, 1, 2 * z_rows, 4, 0)], after=(table_sent,))
        z_got = swap_blk(z_sent, 4)
        n_first, n_value, n_rows = blocks * n_out, planes * n_out, blocks * tab
        first_kept, first_sent, value_kept, value_sent = packet_call(
            lambda *refs: keep_qkv_kernel(blocks, *refs),
            [flat(n_first), flat(n_first + 32), flat(n_value), flat(n_value + n_rows)],
            pos, qkv_args + (qkv_got, table_sent, vectors), after=(z_sent,),
        )
        first_got = swap_grp(first_sent, 2)
        value_got = swap_blk(value_sent, 1)
        (down_kept,), (down_sent,) = combine(
            pos, [("part", down_kept, down_got, 0, 2, 2 * part, 3, 0)], after=(value_sent,)
        )
        down_got = swap_blk(down_sent, 2)
        (up_kept,), (up_sent,) = combine(
            pos, [("part", up_kept, up_got, 0, planes, ff_out // 2, 1, 0)], after=(down_sent,)
        )
        up_got = swap_grp(up_sent, 2)
        (first_kept, vectors, z_kept), (first_sent,) = combine(
            pos,
            [
                ("part", first_kept, first_got, 0, planes, n_out, 2, 0),
                ("vec", vectors, first_got, n_first, 0, 0, None, 0),
                ("part", z_kept, z_got, 0, 1, z_rows, 2, 0),
            ],
            after=(up_sent,),
        )
        first_got = swap_blk(first_sent, 1)
        (down_kept,), (down_sent,) = combine(
            pos, [("part", down_kept, down_got, 0, 1, 2 * part, 4, 0)], after=(first_sent,)
        )
        down_got = swap_blk(down_sent, 4)
        (value_kept, table_kept), (value_sent, table_sent) = combine(
            pos,
            [
                ("part", value_kept, value_got, 0, planes, n_out // 2, 1, 0),
                ("part", table_kept, value_got, n_value, 2, 2 * tab, None, 1),
            ],
            after=(down_sent,),
        )
        value_got = swap_grp(value_sent, 2)
        table_got = swap_blk(table_sent, 2)
        (down_kept, up_kept), (down_sent, up_sent) = combine(
            pos,
            [
                ("part", down_kept, down_got, 0, 1, part, 2, 0),
                ("part", up_kept, up_got, 0, 2, ff_out // 2, 3, 1),
            ],
            after=(value_sent,),
        )
        down_got = swap_blk(down_sent, 1)
        up_got = swap_blk(up_sent, 2)
        (first_kept, value_kept, vectors, z_kept), (first_sent, z_sent) = combine(
            pos,
            [
                ("part", first_kept, first_got, 0, 2, n_out, 3, 0),
                ("part", value_kept, value_got, 0, 2, n_out // 2, 3, 0),
                ("vec", vectors, first_got, n_value, 0, 0, None, 0),
                ("part", z_kept, first_got, n_value + 32, 1, z_rows // 2, 1, 1),
            ],
            after=(up_sent,),
        )
        first_got = swap_blk(first_sent, 2)
        z_got = swap_grp(z_sent, 2)
        (up_kept,), (up_sent,) = combine(
            pos, [("part", up_kept, up_got, 0, 1, ff_out // 2, 4, 0)], after=(first_sent,)
        )
        up_got = swap_blk(up_sent, 4)
        (first_kept, value_kept, table_kept, vectors), (first_sent,) = combine(
            pos,
            [
                ("part", first_kept, first_got, 0, 1, n_out, 4, 0),
                ("part", value_kept, first_got, 2 * n_out, 1, n_out // 2, 4, 0),
                ("part", table_kept, table_got, 0, 1, 2 * tab, None, 0),
                ("vec", vectors, first_got, 3 * n_out, 0, 0, None, 0),
            ],
            after=(up_sent,),
        )
        first_got = swap_blk(first_sent, 4)
        early, (early_sent,) = combine(
            pos,
            [
                ("sum", down_kept, down_got, 0, 0, 0, None, 0),
                ("sum", z_kept, z_got, 0, 0, 0, None, 0),
            ],
            after=(first_sent,),
        )
        early_got = swap_grp(early_sent, 2)
        (up_part,), _ = combine(
            pos, [("sum", up_kept, up_got, 0, 0, 0, None, None)], after=(early_sent,)
        )
        def whole(value, other):
            return pick(x_bit, value, other), pick(x_bit, other, value)

        low, high = whole(early_sent, early_got)
        early = jnp.concatenate([low[:part], high[:part], low[part:], high[part:]], axis=0)
        up_rows = jnp.concatenate(whole(up_part, swap_grp(up_part, 2)), axis=0)
        out_up, out_down, out_out = big_outputs(up_rows, early)
        n_small = n_out + n_out // 2
        (first_part, value_part, table_part, vectors), _ = combine(
            pos,
            [
                ("sum", first_kept, first_got, 0, 0, 0, None, None),
                ("sum", value_kept, first_got, n_out, 0, 0, None, None),
                ("sum", table_kept, first_got, n_small, 0, 0, None, None),
                ("vec", vectors, first_got, n_small + 2 * tab, 0, 0, None, None),
            ],
            after=(out_up, out_down),
        )

        square = jnp.concatenate([first_part, value_part], axis=0)
        near_core = swap_grp(jnp.concatenate([square, vectors.astype(BF)], axis=0), 1)
        near, far = (square, swap_grp(square, 2)), (near_core[:n_small], swap_grp(square, 3))
        vectors = vectors + f(near_core[n_small:])
        sides = []
        for value, other in (near, far):
            low, high = pick(x_bit, value, other), pick(x_bit, other, value)
            sides.append(jnp.concatenate([low[:n_out], high[:n_out], low[n_out:], high[n_out:]], axis=0))
        square = (f(pick(core_bit, *sides)), f(pick(core_bit, *sides[::-1])))
        table_share = f(table_part)
    else:
        context_t, middle_t, act_t, grad_ffn, grad_pre, grad_attn = made
        lanes = lambda value, index: lax.dynamic_slice_in_dim(value, index * (value.shape[1] // 2), value.shape[1] // 2, 1)
        rows_of = lambda value, index: lax.dynamic_slice_in_dim(value, index * (value.shape[0] // 2), value.shape[0] // 2, 0)
        blocked = lambda value: value.reshape(blocks, value.shape[0] // blocks, value.shape[1])
        grad_queries, grad_keys_t, grad_values_t = attend_back(*back_args, ())
        table_kept, table_sent, grad_input_local, vectors = input_grads(
            blocks, grad_queries, grad_keys_t, grad_values_t, *input_args, ()
        )

        def packet(index):
            up = blocked(fwd_dot(middle_t, lanes(grad_pre, index)))
            return jnp.concatenate(
                [
                    blocked(fwd_dot(x_t[:, n_table:], lanes(grad_queries, index))),
                    blocked(back_dot(x_t, rows_of(grad_keys_t, index))),
                    blocked(back_dot(x_t, rows_of(grad_values_t, index))),
                    blocked(fwd_dot(context_t, lanes(grad_attn, index))),
                ]
                + [up[:, :, i : i + half_width] for i in range(0, up.shape[2], half_width)]
                + [blocked(fwd_dot(act_t, lanes(grad_ffn, index)))],
                axis=1,
            )

        total = (packet(core_bit) + f(swap_grp(packet(1 - core_bit).astype(BF), 1))).astype(BF)
        total = lax.psum_scatter(total, "blk", scatter_dimension=0, tiled=False)
        total = (f(total) + f(swap_grp(total, 2))).astype(BF)
        at = 4 * n_out
        square = total[: 3 * n_out]
        up_rows = total[at : at + ff_out]
        down_all = total[at + ff_out :]
        z_rows = jnp.concatenate([down_all[:first_rows], total[3 * n_out : at]], axis=0)
        down_rows = down_all[first_rows:]
        table_rows = jnp.stack([blocked_half.reshape(planes, 2 * tab, half_width) for blocked_half in (table_kept, table_sent)], axis=1)
        table_rows = table_rows.reshape(blocks, 2 * tab, half_width)
        table_rows = jnp.take(table_rows, jnp.arange(blocks) ^ own, axis=0)
        table_share = f(lax.psum_scatter(table_rows, "blk", scatter_dimension=0, tiled=False))
        vectors = lax.psum(vectors, ("blk", "grp"))
        early = jnp.concatenate([down_rows, z_rows], axis=0)
        out_up, out_down, out_out = big_outputs(up_rows, early)

    square = jnp.concatenate(square if packets else both_cores(square), axis=1)
    table_share = jnp.concatenate([table_share[:tab], table_share[tab:]], axis=1)
    vectors = jnp.concatenate([vectors[:16], vectors[16:]], axis=1)
    mine = lax.dynamic_slice_in_dim(vectors[:10], own * n_out, n_out, 1)
    up_bias_out = lax.dynamic_slice_in_dim(vectors[10:14].reshape(-1), own * ff_out, ff_out, 0)
    grad_input = grad_input_local.at[:tab].add(table_share)
    return (
        mixed,
        grad_input,
        mine[:2],
        square[:n_out],
        mine[2],
        square[n_out : 2 * n_out],
        square[2 * n_out :],
        mine[3],
        out_out,
        mine[4],
        mine[5],
        mine[6],
        out_up,
        up_bias_out,
        out_down,
        mine[7],
        mine[8],
        mine[9],
    )


def solution(mesh):
    both = ("grp", "blk")
    placed = (P(both, None), P(both), P(both), P(both)) + (P(),) * 16 + (P(both, None),)
    vec, mat = P("blk"), P("blk", None)
    return jax.shard_map(
        local,
        mesh=mesh,
        in_specs=placed,
        out_specs=(
            P(both, None), P(both, None), P(None, "blk"), mat, vec, mat, mat, vec, mat, vec,
            vec, vec, mat, vec, mat, vec, vec, vec,
        ),
        check_vma=False,
    )
```

```python
import math

import jax
import jax.numpy as jnp
from jax import lax
from jax.experimental import pallas as pl
from jax.experimental.pallas import tpu as pltpu
from jax.sharding import PartitionSpec as P

HEADS = 12
HEAD_DIM = 64
TAB_MAX = 64
LANES = 256
far_below = -1e30
BF = jnp.bfloat16
F32 = jnp.float32
MIB = 1 << 20
LONG = pl.CostEstimate(flops=40_000_000_000, bytes_accessed=MIB, transcendentals=0)
SHORT = pl.CostEstimate(flops=100000000, bytes_accessed=MIB, transcendentals=0)
HBM = pl.BlockSpec(memory_space=pltpu.HBM)


def outer_sum(left, right):
    return lax.dot_general(left, right, (((0,), (0,)), ((), ())), preferred_element_type=F32)


def back_dot(left, right):
    return lax.dot_general(left, right, (((1,), (1,)), ((), ())), preferred_element_type=F32)


def fwd_dot(left, right):
    return jnp.dot(left, right, preferred_element_type=F32)


def norm_parts(values):
    centred = values - jnp.mean(values, axis=-1, keepdims=True)
    spread = jnp.mean(centred * centred, axis=-1, keepdims=True)
    inv = lax.rsqrt(spread + 1e-06)
    return centred * inv, inv


def norm_grad(grad, normed, inv, gain):
    scaled = grad * gain
    return inv * (
        scaled
        - jnp.mean(scaled, axis=-1, keepdims=True)
        - normed * jnp.mean(scaled * normed, axis=-1, keepdims=True)
    )


def head_lanes(shape, index):
    lane = lax.broadcasted_iota(jnp.int32, shape, len(shape) - 1)
    return (lane >= index * HEAD_DIM) & (lane < (index + 1) * HEAD_DIM)


def column_of(row):
    return jnp.broadcast_to(row, (128, row.shape[1])).T[:, :1]


def start_copies(sources, targets, sems):
    copies = [pltpu.make_async_copy(a, b, sems.at[i]) for i, (a, b) in enumerate(zip(sources, targets))]
    for copy in copies:
        copy.start()
    return copies


def entry_kernel(tokens_any, seg_any, prev_any, answer_any, payload_ref, input_ref, *scratch):
    tab = TAB_MAX
    *held, sems = scratch
    for copy in start_copies((tokens_any, seg_any, prev_any, answer_any), held, sems):
        copy.wait()
    tokens_ref, seg_ref, prev_ref, answer_ref = held
    prev = prev_ref[...].astype(F32)[None]
    low = residual(tokens_ref, prev, answer_ref).astype(BF)
    input_ref[...] = low
    payload_ref[:tab] = low[:tab]
    payload_ref[tab:] = jnp.zeros((16, low.shape[1]), BF)
    lane = lax.broadcasted_iota(jnp.int32, (1, 128), 1)

    def twice(row):
        row = row[:, :128]
        return jnp.where(lane < tab, row, pltpu.roll(row, tab, 1))

    is_open = twice(jnp.where(seg_ref[...] == 0, 1.0, 0.0)[None])
    both = jnp.concatenate([is_open, twice(prev)], axis=1)
    payload_ref[tab:, :256] = jnp.broadcast_to(both, (16, 256)).astype(BF)


def residual(tokens_ref, prev, answer_ref):
    answers = answer_ref[...].astype(F32)
    return tokens_ref[...].astype(F32) + jnp.where(column_of(prev) == 1.0, answers[1:2], answers[0:1])


def entry(tokens, seg, prev, answers):
    rows, width = tokens.shape
    vmem = pl.BlockSpec(memory_space=pltpu.VMEM)
    return pl.pallas_call(
        entry_kernel,
        in_specs=[HBM] * 4,
        out_specs=[vmem] * 2,
        out_shape=[jax.ShapeDtypeStruct((TAB_MAX + 16, width), BF), jax.ShapeDtypeStruct((rows, width), BF)],
        scratch_shapes=[pltpu.VMEM(v.shape, v.dtype) for v in (tokens, seg, prev, answers)]
        + [pltpu.SemaphoreType.DMA((4,))],
        compiler_params=pltpu.CompilerParams(vmem_limit_bytes=60 * MIB),
    )(tokens, seg, prev, answers)


def own_kernel(
    input_ref, query_w_any, key_w_any, value_w_any, query_b_any, value_b_any, seg_any, turn_any,
    q_ref, k_ref, v_ref, bias_ref, value_row_ref, *scratch
):
    *held, sems = scratch
    query_w_ref, key_w_ref, value_w_ref, query_b_ref, value_b_ref, seg_ref, turn_ref = held
    sources = (query_w_any, key_w_any, value_w_any, query_b_any, value_b_any, seg_any, turn_any)
    for copy in start_copies(sources, held, sems):
        copy.wait()
    low = input_ref[...]
    query = fwd_dot(low, query_w_ref[...]) + query_b_ref[...].astype(F32)[None]
    q_ref[...] = (query.astype(BF).astype(F32) * HEAD_DIM**-0.5).astype(BF)
    k_ref[...] = fwd_dot(low, key_w_ref[...]).astype(BF)
    value_b = value_b_ref[...].astype(F32)[None]
    value_row_ref[...] = value_b
    v_ref[...] = (fwd_dot(low, value_w_ref[...]) + value_b).astype(BF)
    turn = turn_ref[...].astype(F32)[None]
    seg = seg_ref[...].astype(F32)[None]
    same = (column_of(turn) == turn) & (seg != 0.0)
    bias_ref[...] = jnp.where(same, 0.0, far_below)


def own_part(layer_input, query_w, key_w, value_w, query_b, value_b, seg, turn):
    rows, width = layer_input.shape
    vmem = pl.BlockSpec(memory_space=pltpu.VMEM)
    return pl.pallas_call(
        own_kernel,
        in_specs=[vmem] + [HBM] * 7,
        out_specs=[vmem] * 5,
        out_shape=[jax.ShapeDtypeStruct((rows, width), BF)] * 3
        + [jax.ShapeDtypeStruct((rows, rows), F32), jax.ShapeDtypeStruct((1, width), F32)],
        scratch_shapes=[
            pltpu.VMEM(v.shape, v.dtype) for v in (query_w, key_w, value_w, query_b, value_b, seg, turn)
        ]
        + [pltpu.SemaphoreType.DMA((7,))],
        compiler_params=pltpu.CompilerParams(vmem_limit_bytes=60 * MIB),
        cost_estimate=pl.CostEstimate(flops=100000000, bytes_accessed=MIB, transcendentals=0),
    )(layer_input, query_w, key_w, value_w, query_b, value_b, seg, turn)


def attend_kernel(
    views, input_ref, key_w_ref, value_w_ref, value_b_ref, q_ref, own_k_ref, own_v_ref, own_bias_ref, *refs
):
    *parts, keys_ref, values_ref, prob_ref, context_ref, x_t_ref, prev_ref, table_ref, bias_ref = refs
    n_table = table_ref.shape[0]
    tab = TAB_MAX
    slots = [parts[part].at[first : first + tab + 16] for part, first in views]

    @pl.when(pl.program_id(0) == 0)
    def _():
        lane = lax.broadcasted_iota(jnp.int32, (1, 128), 1)
        for i, slot in enumerate(slots):
            table_ref[i * tab : (i + 1) * tab] = slot[:tab]
        for i in range(0, len(slots), 2):
            marks = jnp.where(
                lax.broadcasted_iota(jnp.int32, (16, 256), 1) % 128 < tab,
                slots[i][tab:, :256].astype(F32), slots[i + 1][tab:, :256].astype(F32),
            )
            at = slice(i * tab, (i + 2) * tab)
            closed = jnp.where(marks[:1, :128] > 0.5, 0.0, far_below)
            bias_ref[:, at] = jnp.broadcast_to(closed, (bias_ref.shape[0], 128))
            prev_ref[:, at] = marks[:8, 128:]
        bias_ref[:, n_table:] = own_bias_ref[...]
        x_t_ref[:, :n_table] = table_ref[...].T
        x_t_ref[:, n_table:] = input_ref[...].T

    table = table_ref[...]
    keys_ref[:n_table] = fwd_dot(table, key_w_ref[...]).astype(BF)
    values_ref[:n_table] = (fwd_dot(table, value_w_ref[...]) + value_b_ref[...]).astype(BF)
    keys_ref[n_table:] = own_k_ref[...]
    values_ref[n_table:] = own_v_ref[...]
    queries = q_ref[...]
    context = jnp.zeros(context_ref.shape, F32)
    for h in range(queries.shape[1] // HEAD_DIM):
        mask = head_lanes(queries.shape, h)
        picked = jnp.where(mask, queries, jnp.zeros_like(queries))
        scores = back_dot(picked, keys_ref[...]) + bias_ref[...]
        top = jnp.max(scores, axis=-1, keepdims=True)
        weights = jnp.exp(scores - top)
        prob = (weights * (1.0 / jnp.sum(weights, axis=-1, keepdims=True))).astype(BF)
        prob_ref[h] = prob
        context = jnp.where(mask, fwd_dot(prob, values_ref[...]), context)
    context_ref[...] = context


def vmem_limit(n_keys, small):
    return (small if n_keys <= 1024 else 60) * MIB


def attend(parts, views, layer_input, key_w, value_w, value_b, queries, own_k, own_v, own_bias):
    rows, width = queries.shape
    n_table = len(views) * TAB_MAX
    n_keys = n_table + rows
    group = LANES if n_keys <= 1024 else LANES // 2
    per = group // HEAD_DIM
    steady = {} if n_keys <= 1024 else {"pipeline_mode": pl.Buffered(1)}
    whole = lambda shape: pl.BlockSpec(shape, lambda i: (0, 0), **steady)
    lanes = lambda n: pl.BlockSpec((n, group), lambda i: (0, i))
    return pl.pallas_call(
        lambda *refs: attend_kernel(views, *refs),
        grid=(width // group,),
        in_specs=[
            whole((rows, width)), lanes(width), lanes(width), lanes(1), lanes(rows), lanes(rows), lanes(rows),
            whole((rows, rows)),
        ]
        + [whole(part.shape) for part in parts],
        out_specs=[
            lanes(n_keys), lanes(n_keys), pl.BlockSpec((per, rows, n_keys), lambda i: (i, 0, 0)), lanes(rows),
            whole((width, n_keys)), whole((8, n_table)),
        ],
        out_shape=[
            jax.ShapeDtypeStruct((n_keys, width), BF),
            jax.ShapeDtypeStruct((n_keys, width), BF),
            jax.ShapeDtypeStruct((HEADS, rows, n_keys), BF),
            jax.ShapeDtypeStruct((rows, width), F32),
            jax.ShapeDtypeStruct((width, n_keys), BF),
            jax.ShapeDtypeStruct((8, n_table), F32),
        ],
        scratch_shapes=[pltpu.VMEM((n_table, width), BF), pltpu.VMEM((rows, n_keys), F32)],
        compiler_params=pltpu.CompilerParams(vmem_limit_bytes=vmem_limit(n_keys, 60)),
        cost_estimate=pl.CostEstimate(flops=100000000, bytes_accessed=MIB, transcendentals=0),
    )(layer_input, key_w, value_w, value_b, queries, own_k, own_v, own_bias, *parts)


def middle_kernel(
    packets, pos_ref, tokens_ref, prev_ref, answer_ref, context_ref, cot_ref, out_w_any, up_w_any, down_w_any,
    up_b_1d_ref, *refs
):
    biases, refs = refs[:6], refs[6:]
    mixed_ref, grad_context_ref, grad_mid_ref, sums_ref, up_sum_ref = refs[:5]
    refs = refs[5:]
    if packets:
        anys, refs = refs[:5], refs[5:]
    context_t_ref, middle_t_ref, act_t_ref, grad_ffn_ref, grad_pre_ref, grad_attn_ref = refs[:6]
    slope_ref, total_ref, middle_low_ref, out_w_ref, up_w_ref, down_w_ref, up_b_ref, sems = refs[6:14]
    width, hidden = up_w_ref.shape
    tile = width
    steps = hidden // tile

    def tile_copies(i):
        at = pl.ds(i * tile, tile)
        return (
            pltpu.make_async_copy(up_w_any.at[:, at], up_w_ref.at[:, at], sems.at[2 * i + 1]),
            pltpu.make_async_copy(down_w_any.at[at, :], down_w_ref.at[at, :], sems.at[2 * i + 2]),
        )

    out_copy = pltpu.make_async_copy(out_w_any, out_w_ref, sems.at[0])
    out_copy.start()
    for i in range(steps):
        for copy in tile_copies(i):
            copy.start()
    out_b, norm_g, norm_s, down_b, final_g, final_s = (ref[...].astype(F32)[None] for ref in biases)
    up_b_ref[...] = up_b_1d_ref[...].astype(F32)[None]
    resid = residual(tokens_ref, prev_ref[...].astype(F32)[None], answer_ref)
    column = lambda v: jnp.sum(v, axis=0, keepdims=True)
    context_low = context_ref[...].astype(BF)
    context_t_ref[...] = context_low.T
    out_copy.wait()
    normed1, inv1 = norm_parts(resid + fwd_dot(context_low, out_w_ref[...]) + out_b)
    middle = normed1 * norm_g + norm_s
    middle_low = middle.astype(BF)
    middle_low_ref[...] = middle_low
    middle_t_ref[...] = middle_low.T
    total_ref[...] = middle + down_b

    def forward(i):
        at = pl.ds(i * tile, tile)
        for copy in tile_copies(i):
            copy.wait()
        pre = fwd_dot(middle_low_ref[...], up_w_ref[:, at]) + up_b_ref[:, at]
        cdf = 0.5 * (1.0 + lax.erf(pre * (0.5**0.5)))
        act = (pre * cdf).astype(BF)
        act_t_ref[at, :] = act.T
        slope_ref[:, at] = cdf + pre * jnp.exp(-0.5 * pre * pre) * (1.0 / math.sqrt(2 * math.pi))
        total_ref[...] += fwd_dot(act, down_w_ref[at, :])

    for i in range(steps):
        forward(i)
    normed2, inv2 = norm_parts(total_ref[...])
    mixed_ref[...] = (normed2 * final_g + final_s).astype(BF)
    cot = cot_ref[...].astype(F32)
    grad_final = norm_grad(cot, normed2, inv2, final_g)
    grad_ffn = grad_final.astype(BF)
    grad_ffn_ref[...] = grad_ffn
    total_ref[...] = grad_final

    def backward(i, carry):
        at = pl.ds(pl.multiple_of(i * tile, tile), tile)
        grad_pre = (back_dot(grad_ffn_ref[...], down_w_ref[at, :]) * slope_ref[:, at]).astype(BF)
        grad_pre_ref[:, at] = grad_pre
        up_sum_ref[:, at] = column(grad_pre.astype(F32))
        total_ref[...] += back_dot(grad_pre, up_w_ref[:, at])
        return carry

    copies = []
    if packets:
        blocks = packets
        sent_ref, down_own_ref, z_own_ref, up_sent_ref, up_own_ref, out_sems = refs[14:]
        half = width // 2
        small, size = width // blocks, hidden // blocks
        first_rows = 2 * small // 3
        z_rows, rows = first_rows + small, size - first_rows
        core = pos_ref[0]
        n_down = blocks * rows

        def leave(source, target):
            copy = pltpu.make_async_copy(source, target, out_sems.at[len(copies)])
            copy.start()
            copies.append(copy)

        def lanes_of(own):
            return pl.ds(pl.multiple_of((core if own else 1 - core) * half, 128), half)

        for own, down_ref, first_z, z_ref in ((False, sent_ref, n_down, sent_ref), (True, down_own_ref, 0, z_own_ref)):
            part = grad_ffn_ref[:, lanes_of(own)]
            for b in range(blocks):
                value = fwd_dot(act_t_ref[b * size : (b + 1) * size], part).astype(BF)
                down_ref[b * rows : (b + 1) * rows] = value[first_rows:]
                z_ref[first_z + b * z_rows : first_z + b * z_rows + first_rows] = value[:first_rows]
            leave(down_ref.at[:n_down], (anys[1] if own else anys[0].at[:n_down]))
        for i in range(steps):
            t = lax.rem(2 * (1 - core) + i, steps)
            backward(t, 0)
            value = fwd_dot(middle_t_ref[...], grad_pre_ref[:, pl.ds(pl.multiple_of(t * tile, tile), tile)]).astype(BF)
            target = up_sent_ref if i < steps // 2 else up_own_ref
            for b in range(blocks):
                for q in range(2):
                    first = b * size + (2 * (i % (steps // 2)) + q) * small
                    target[first : first + small] = value[b * small : (b + 1) * small, q * half : (q + 1) * half]
            if i == steps // 2 - 1:
                leave(up_sent_ref, anys[3])
        leave(up_own_ref, anys[4])
    else:
        lax.fori_loop(0, steps, backward, 0)
    grad_middle = total_ref[...]
    grad_mid = norm_grad(grad_middle, normed1, inv1, norm_g)
    grad_mid_ref[...] = grad_mid
    grad_attn = grad_mid.astype(BF)
    grad_attn_ref[...] = grad_attn
    if packets:
        for own, first_z, z_ref in ((False, n_down, sent_ref), (True, 0, z_own_ref)):
            value = fwd_dot(context_t_ref[...], grad_attn_ref[:, lanes_of(own)]).astype(BF)
            for b in range(blocks):
                first = first_z + b * z_rows + first_rows
                z_ref[first : first + small] = value[b * small : (b + 1) * small]
            if own:
                leave(z_own_ref, anys[2])
            else:
                leave(sent_ref.at[n_down:], anys[0].at[n_down:])
    grad_context_ref[...] = back_dot(grad_attn, out_w_ref[...]).astype(BF)
    sums_ref[0:1] = column(grad_attn.astype(F32))
    sums_ref[1:2] = column(grad_middle * normed1)
    sums_ref[2:3] = column(grad_middle)
    sums_ref[3:4] = column(grad_ffn.astype(F32))
    sums_ref[4:5] = column(cot * normed2)
    sums_ref[5:6] = column(cot)
    sums_ref[6:8] = jnp.zeros((2, sums_ref.shape[1]), F32)
    for copy in copies:
        copy.wait()


def middle_part(packets, pos, tokens, prev, answers, context, cot, out_w, up_w, down_w, up_b, *biases):
    rows, width = tokens.shape
    hidden = up_w.shape[1]
    half = width // 2
    vmem, away = pl.BlockSpec(memory_space=pltpu.VMEM), pl.BlockSpec(memory_space=pl.ANY)
    shape = lambda n, t: jax.ShapeDtypeStruct((rows, n), t)
    turned = lambda n: jax.ShapeDtypeStruct((n, rows), BF)
    inner = [turned(width), turned(width), turned(hidden), shape(width, BF), shape(hidden, BF), shape(width, BF)]
    held = lambda shapes: [pltpu.VMEM(v.shape, v.dtype) for v in shapes]
    outs = [
        shape(width, BF), shape(width, BF), shape(width, F32), jax.ShapeDtypeStruct((8, width), F32),
        jax.ShapeDtypeStruct((1, hidden), F32),
    ]
    scratch = [
        pltpu.VMEM((rows, hidden), F32), pltpu.VMEM((rows, width), F32), pltpu.VMEM((rows, width), BF),
        pltpu.VMEM(out_w.shape, BF), pltpu.VMEM(up_w.shape, BF), pltpu.VMEM(down_w.shape, BF),
        pltpu.VMEM((1, hidden), F32), pltpu.SemaphoreType.DMA((1 + 2 * (hidden // width),)),
    ]
    specs = [vmem] * 5
    if packets:
        first_rows = 2 * width // 3
        z_rows, down_rows = first_rows + width, hidden - first_rows
        packed = [
            jax.ShapeDtypeStruct((n, half), BF) for n in (down_rows + z_rows, down_rows, z_rows, hidden, hidden)
        ]
        scratch = held(inner) + scratch + held(packed) + [pltpu.SemaphoreType.DMA((6,))]
        outs, specs = outs + packed, specs + [away] * 5
    else:
        outs, specs = outs + inner, specs + [vmem] * 6
    return pl.pallas_call(
        lambda *refs: middle_kernel(packets, *refs),
        in_specs=[pl.BlockSpec(memory_space=pltpu.SMEM)] + [vmem] * 5 + [HBM] * 3 + [vmem] * 7,
        out_specs=specs,
        out_shape=outs,
        scratch_shapes=scratch,
        compiler_params=pltpu.CompilerParams(vmem_limit_bytes=60 * MIB),
        cost_estimate=pl.CostEstimate(flops=100000000, bytes_accessed=MIB, transcendentals=0),
    )(pos, tokens, prev, answers, context, cot, out_w, up_w, down_w, up_b, *biases)


def attend_back_kernel(
    q_ref, keys_ref, values_ref, prob_ref, context_ref, grad_ref, *refs
):
    grad_q_ref, grad_k_ref, grad_v_ref = refs[-3:]
    grad = grad_ref[...]
    grad_f = grad.astype(F32)
    product = grad_f * context_ref[...]
    grad_t = grad_f.T.astype(BF)
    q_t = q_ref[...].astype(F32).T.astype(BF)
    grad_q = jnp.zeros(grad.shape, F32)
    for h in range(grad.shape[1] // HEAD_DIM):
        mask = head_lanes(grad.shape, h)
        at = slice(h * HEAD_DIM, (h + 1) * HEAD_DIM)
        row_dot = jnp.sum(jnp.where(mask, product, 0.0), axis=-1, keepdims=True)
        grad_prob = back_dot(jnp.where(mask, grad, jnp.zeros_like(grad)), values_ref[...])
        prob = prob_ref[h]
        grad_score = (prob.astype(F32) * (grad_prob - row_dot)).astype(BF)
        grad_v_ref[at] = fwd_dot(grad_t[at], prob).astype(BF)
        grad_k_ref[at] = fwd_dot(q_t[at], grad_score).astype(BF)
        grad_q = jnp.where(mask, fwd_dot(grad_score, keys_ref[...]), grad_q)
    grad_q_ref[...] = (grad_q * HEAD_DIM**-0.5).astype(BF)


def attend_back(queries, keys, values, prob, context, grad_context, after):
    rows, width = queries.shape
    n_keys = keys.shape[0]
    group = LANES if n_keys <= 1024 else LANES // 2
    per = group // HEAD_DIM
    lanes = lambda n: pl.BlockSpec((n, group), lambda i: (0, i))
    return pl.pallas_call(
        attend_back_kernel,
        grid=(width // group,),
        in_specs=[
            lanes(rows), lanes(n_keys), lanes(n_keys), pl.BlockSpec((per, rows, n_keys), lambda i: (i, 0, 0)),
            lanes(rows), lanes(rows),
        ]
        + [pl.BlockSpec(memory_space=pl.ANY)] * len(after),
        out_specs=[lanes(rows)] + [pl.BlockSpec((group, n_keys), lambda i: (i, 0))] * 2,
        out_shape=[
            jax.ShapeDtypeStruct((rows, width), BF),
            jax.ShapeDtypeStruct((width, n_keys), BF),
            jax.ShapeDtypeStruct((width, n_keys), BF),
        ],
        compiler_params=pltpu.CompilerParams(vmem_limit_bytes=vmem_limit(n_keys, 54)),
        cost_estimate=LONG,
    )(queries, keys, values, prob, context, grad_context, *after)


def core_lanes(pos_ref, own, size):
    core = pos_ref[0] if own else 1 - pos_ref[0]
    return pl.ds(pl.multiple_of(core * size, 128), size)


def qkv_values(own, pos_ref, x_t_ref, grad_q_ref, grad_k_ref, grad_v_ref, blocks, store):
    half = grad_q_ref.shape[1] // 2
    n_table = x_t_ref.shape[1] - grad_q_ref.shape[0]
    small = x_t_ref.shape[0] // blocks
    at = core_lanes(pos_ref, own, half)
    core = pos_ref[0] if own else 1 - pos_ref[0]
    rows = pl.ds(pl.multiple_of(core * half, 128), half)
    values = (
        fwd_dot(x_t_ref[:, n_table:], grad_q_ref[:, at]),
        back_dot(x_t_ref[...], grad_k_ref[rows, :]),
        back_dot(x_t_ref[...], grad_v_ref[rows, :]),
    )
    for i, value in enumerate(values):
        for b in range(blocks):
            store(b, i * small, value[b * small : (b + 1) * small])


def send_kernel(make, n_in, blocks, *refs):
    pos_ref, out_ref = refs[0], refs[-1]

    def store(b, first, value):
        out_ref[b, first : first + value.shape[0]] = value.astype(BF)

    make(False, pos_ref, *refs[1 : 1 + n_in], blocks, store)


def pick(bit, first, second):
    return jnp.where(bit == 0, first, second)


def keep_qkv_kernel(
    blocks, pos_ref, x_t_ref, grad_q_ref, grad_k_ref, grad_v_ref, got_ref, table_ref, vec_ref, *outs
):
    first_kept_ref, first_sent_ref, kept_ref, sent_ref = outs
    small = x_t_ref.shape[0] // blocks
    planes = blocks // 2
    held = {}

    def store(b, first, value):
        value = (value + got_ref[b, first : first + small].astype(F32)).astype(BF)
        held[b, first] = value
        if first == small:
            query = held.pop((b, 0))
            rows = slice(b * small, (b + 1) * small)
            first_kept_ref[rows] = pick(pos_ref[1], query, value)
            first_sent_ref[rows] = pick(pos_ref[1], value, query)
        if first == 2 * small and b % 2 == 1:
            rows = slice(b // 2 * small, (b // 2 + 1) * small)
            kept_ref[rows] = pick(pos_ref[2], held[b - 1, first], value)
            sent_ref[rows] = pick(pos_ref[2], value, held[b - 1, first])

    qkv_values(True, pos_ref, x_t_ref, grad_q_ref, grad_k_ref, grad_v_ref, blocks, store)
    first_sent_ref[blocks * small :] = vec_ref[...].astype(BF)
    sent_ref[planes * small :] = table_ref[...]


def inputs_kernel(
    blocks, grad_q_ref, grad_k_ref, grad_v_ref, query_w_ref, key_w_ref, value_w_ref, grad_mid_ref, prev_ref,
    table_prev_ref, sums_ref, up_sum_ref, *refs
):
    table_kept_ref, table_sent_ref, grad_ref, vec_ref = refs[-4:]
    tab = TAB_MAX
    n_table = blocks * tab
    rows, width = grad_q_ref.shape
    half = width // 2
    own = fwd_dot(key_w_ref[...], grad_k_ref[:, n_table:]) + fwd_dot(value_w_ref[...], grad_v_ref[:, n_table:])
    grad = grad_mid_ref[...] + back_dot(grad_q_ref[...], query_w_ref[...]) + own.T
    grad_ref[...] = grad
    is_one = column_of(prev_ref[...].astype(F32)[None]) == 1.0
    one_sum = jnp.sum(jnp.where(is_one, grad, 0.0), axis=0, keepdims=True)
    zero_sum = jnp.sum(jnp.where(is_one, 0.0, grad), axis=0, keepdims=True)
    step = min(n_table, 512)
    row = lax.broadcasted_iota(jnp.int32, (8, step), 0)
    for first in range(0, n_table, step):
        at = slice(first, first + step)
        part = (fwd_dot(key_w_ref[...], grad_k_ref[:, at]) + fwd_dot(value_w_ref[...], grad_v_ref[:, at])).astype(BF)
        marks = table_prev_ref[:, at]
        marks = jnp.where(row == 0, marks, 1.0 - marks).astype(BF)
        table_sums = back_dot(marks, part)
        one_sum += table_sums[0:1]
        zero_sum += table_sums[1:2]
        for j in range(step // 128):
            pair = part[:, j * 128 : (j + 1) * 128].T
            slot = first // 128 + j
            for k, ref in enumerate((table_kept_ref, table_sent_ref)):
                for side in range(2):
                    ref[(slot * 2 + side) * tab : (slot * 2 + side + 1) * tab] = pair[
                        k * tab : (k + 1) * tab, side * half : (side + 1) * half
                    ]
    ones = jnp.ones((8, grad_v_ref.shape[1]), BF)
    lines = [
        zero_sum,
        one_sum,
        jnp.sum(grad_q_ref[...].astype(F32), axis=0, keepdims=True),
        back_dot(ones, grad_v_ref[...])[0:1],
    ]
    lines += [sums_ref[i : i + 1] for i in range(6)]
    lines += [up_sum_ref[:, i * width : (i + 1) * width] for i in range(up_sum_ref.shape[1] // width)]
    vec_ref[...] = jnp.zeros(vec_ref.shape, F32)
    for i, line in enumerate(lines):
        for side in range(2):
            vec_ref[side * 16 + i : side * 16 + i + 1] = line[:, side * half : (side + 1) * half]


def input_grads(blocks, grad_q, grad_k, grad_v, query_w, key_w, value_w, grad_mid, prev, table_prev, sums, up_sum, after):
    rows, width = grad_q.shape
    n_half = blocks * TAB_MAX
    vmem = pl.BlockSpec(memory_space=pltpu.VMEM)
    args = (grad_q, grad_k, grad_v, query_w, key_w, value_w, grad_mid, prev, table_prev, sums, up_sum)
    return pl.pallas_call(
        lambda *refs: inputs_kernel(blocks, *refs),
        in_specs=[vmem] * len(args) + [pl.BlockSpec(memory_space=pl.ANY)] * len(after),
        out_specs=[vmem] * 4,
        out_shape=[
            jax.ShapeDtypeStruct((n_half, width // 2), BF),
            jax.ShapeDtypeStruct((n_half, width // 2), BF),
            jax.ShapeDtypeStruct((rows, width), F32),
            jax.ShapeDtypeStruct((32, width // 2), F32),
        ],
        compiler_params=pltpu.CompilerParams(vmem_limit_bytes=(20 if blocks <= 8 else 56) * MIB),
        cost_estimate=LONG,
    )(*args, *after)


def combine(pos, items, after=()):
    width = items[0][1].shape[1]
    gots, shapes, heights, places = [], [], {}, []
    for kind, kept, got, first, outer, inner, bit, message in items:
        if got is not None and not any(got is g for g in gots):
            gots.append(got)
        rows = kept.shape[0] if kind != "part" else outer * inner
        if kind != "copy":
            shapes.append(jax.ShapeDtypeStruct((rows, width), kept.dtype))
        if message is not None:
            places.append(heights.get(message, 0))
            heights[message] = places[-1] + rows
        else:
            places.append(None)
    sizes = [heights[m] for m in sorted(heights)]
    shapes += [jax.ShapeDtypeStruct((n, width), BF) for n in sizes]
    which = [next((i for i, g in enumerate(gots) if g is item[2]), None) for item in items]
    n_outs = sum(item[0] != "copy" for item in items)

    def body(pos_ref, *refs):
        kept_refs, refs = refs[: len(items)], refs[len(items) :]
        got_refs, refs = refs[: len(gots)], refs[len(gots) + len(after) :]
        out_refs, sent_refs = list(refs[:n_outs]), refs[n_outs:]
        for i, (kind, _, _, first, outer, inner, bit, message) in enumerate(items):
            kept_ref = kept_refs[i]
            n = kept_ref.shape[0]
            if kind == "copy":
                sent_refs[message][places[i] : places[i] + n] = kept_ref[...]
                continue
            got_ref, out_ref = got_refs[which[i]], out_refs.pop(0)
            if kind == "vec":
                total = kept_ref[...] + got_ref[first : first + n].astype(F32)
                out_ref[...] = total
                if message is not None:
                    sent_refs[message][places[i] : places[i] + n] = total.astype(BF)
            elif kind == "sum":
                total = kept_ref[...].astype(F32) + got_ref[first : first + n].astype(F32)
                out_ref[...] = total.astype(BF)
                if message is not None:
                    sent_refs[message][places[i] : places[i] + n] = total.astype(BF)
            else:
                for o in range(outer):
                    halves = []
                    for side in range(2):
                        at = (2 * o + side) * inner
                        total = kept_ref[at : at + inner].astype(F32)
                        total = total + got_ref[first + at : first + at + inner].astype(F32)
                        halves.append(total.astype(BF))
                    rows = slice(places[i] + o * inner, places[i] + (o + 1) * inner)
                    if bit is None:
                        out_ref[o * inner : (o + 1) * inner], sent_refs[message][rows] = halves
                    else:
                        out_ref[o * inner : (o + 1) * inner] = pick(pos_ref[bit], *halves)
                        sent_refs[message][rows] = pick(pos_ref[bit], *halves[::-1])

    vmem = pl.BlockSpec(memory_space=pltpu.VMEM)
    results = pl.pallas_call(
        body,
        in_specs=[pl.BlockSpec(memory_space=pltpu.SMEM)]
        + [vmem] * (len(items) + len(gots))
        + [pl.BlockSpec(memory_space=pl.ANY)] * len(after),
        out_specs=[vmem] * len(shapes),
        out_shape=shapes,
        compiler_params=pltpu.CompilerParams(vmem_limit_bytes=16 * MIB),
        cost_estimate=LONG,
    )(pos, *[item[1] for item in items], *gots, *after)
    return results[:n_outs], results[n_outs:]


def packet_call(kernel, shapes, pos, args, after=(), scratch=(), wide=(), cost=LONG):
    smem, vmem = pl.BlockSpec(memory_space=pltpu.SMEM), pl.BlockSpec(memory_space=pltpu.VMEM)
    outs = [jax.ShapeDtypeStruct(shape, BF) for shape in shapes]
    outs += [jax.ShapeDtypeStruct(shape, F32) for shape in wide]

    def body(*refs):
        n = 1 + len(args)
        kernel(*refs[:n], *refs[n + len(after) :])

    return pl.pallas_call(
        body,
        in_specs=[smem] + [vmem] * len(args) + [pl.BlockSpec(memory_space=pl.ANY)] * len(after),
        out_specs=[vmem] * len(outs),
        out_shape=outs,
        scratch_shapes=list(scratch),
        compiler_params=pltpu.CompilerParams(vmem_limit_bytes=20 * MIB),
        cost_estimate=cost,
    )(pos, *args, *after)


def local(
    tokens, seg_ids, turn_ids, prev_ids, answer_table, query_weight, query_bias,
    key_weight, value_weight, value_bias, out_weight, out_bias, norm_gain, norm_shift,
    up_weight, up_bias, down_weight, down_bias, final_gain, final_shift, cotangent,
):
    rows, width = tokens.shape
    blocks = lax.axis_size("blk")
    grps = lax.axis_size("grp")
    tab = TAB_MAX
    scale = HEAD_DIM ** (-0.5)
    f = lambda v: v.astype(F32)
    core_bit = lax.axis_index("grp") & 1
    x_bit = lax.axis_index("grp") >> 1
    own = lax.axis_index("blk")
    planes = blocks // 2
    n_out = width // blocks
    ff_out = up_weight.shape[1] // blocks
    half_width = width // 2
    n_table = blocks * tab
    pos = jnp.stack([core_bit, x_bit, own & 1, (own >> 1) & 1, own >> 2]).astype(jnp.int32)

    def swap_grp(value, mask):
        return lax.ppermute(value, "grp", [(i, i ^ mask) for i in range(grps)])

    def swap_blk(value, mask):
        return lax.ppermute(value, "blk", [(i, i ^ mask) for i in range(blocks)])

    payload, layer_input = entry(tokens, seg_ids, prev_ids, answer_table)
    slots = [payload] + [None] * (blocks - 1)
    for k in range(1, planes):
        slots[2 * k] = swap_blk(payload, 2 * k)
    slots[1] = swap_blk(payload, 1)
    for k in range(1, planes):
        slots[2 * k + 1] = swap_blk(slots[2 * k], 1)
    queries, own_keys, own_values, own_bias, value_row = own_part(
        layer_input, query_weight, key_weight, value_weight, query_bias, value_bias, seg_ids, turn_ids
    )
    views = [(i, 0) for i in range(blocks)]
    keys, values, prob, context, x_t, table_prev = attend(
        slots, views, layer_input, key_weight, value_weight, value_row, queries, own_keys, own_values, own_bias
    )
    first_rows = 2 * n_out // 3
    def both_cores(value):
        other = swap_grp(value, 1)
        return f(pick(core_bit, value, other)), f(pick(core_bit, other, value))

    def big_outputs(up_rows, early):
        sides = both_cores(up_rows)
        out_up = jnp.concatenate([side[i : i + n_out] for side in sides for i in range(0, ff_out, n_out)], axis=1)
        sides = both_cores(early)
        at_z = ff_out - first_rows
        out_down = jnp.concatenate(
            [
                jnp.concatenate([side[at_z : at_z + first_rows] for side in sides], axis=1),
                jnp.concatenate([side[:at_z] for side in sides], axis=1),
            ],
            axis=0,
        )
        out_out = jnp.concatenate([side[at_z + first_rows :] for side in sides], axis=1)
        return out_up, out_down, out_out

    packets = blocks if blocks == 8 and n_out % 32 == 0 else 0
    mixed, grad_context, grad_mid_sum, sums, up_sum, *made = middle_part(
        packets, pos, tokens, prev_ids, answer_table, context, cotangent, out_weight, up_weight, down_weight, up_bias,
        out_bias, norm_gain, norm_shift, down_bias, final_gain, final_shift,
    )
    first_rows = 2 * n_out // 3
    part, z_rows = (ff_out - first_rows) // 2, n_out + first_rows
    back_args = (queries, keys, values, prob, context, grad_context)
    input_args = (query_weight, key_weight, value_weight, grad_mid_sum, prev_ids, table_prev, sums, up_sum)

    if packets:
        flat = lambda rows: (rows, half_width)
        down_sent, down_kept, z_kept, up_sent, up_kept = made
        down_got = swap_grp(down_sent, 1)
        up_got = swap_grp(up_sent, 1)
        grad_queries, grad_keys_t, grad_values_t = attend_back(*back_args, ())
        (down_kept, z_kept), (down_sent, z_sent) = combine(
            pos,
            [
                ("part", down_kept, down_got, 0, blocks, part, 1, 0),
                ("part", z_kept, down_got, 2 * blocks * part, 2, 2 * z_rows, 3, 1),
            ],
            after=(grad_queries,),
        )
        down_got = swap_grp(down_sent, 2)
        z_got = swap_blk(z_sent, 2)
        (up_kept,), (up_sent,) = combine(
            pos, [("part", up_kept, up_got, 0, planes, ff_out, 2, 0)], after=(down_sent,)
        )
        up_got = swap_blk(up_sent, 1)
        qkv_args = (x_t, grad_queries, grad_keys_t, grad_values_t)
        (qkv_sent,) = packet_call(
            lambda *refs: send_kernel(qkv_values, 4, blocks, *refs),
            [(blocks, 3 * n_out, half_width)], pos, qkv_args, after=(up_sent,),
        )
        qkv_got = swap_grp(qkv_sent, 1)
        table_kept, table_sent, grad_input_local, vectors = input_grads(
            blocks, grad_queries, grad_keys_t, grad_values_t, *input_args, (qkv_sent,)
        )
        (z_kept,), (z_sent,) = combine(pos, [("part", z_kept, z_got, 0, 1, 2 * z_rows, 4, 0)], after=(table_sent,))
        z_got = swap_blk(z_sent, 4)
        n_first, n_value, n_rows = blocks * n_out, planes * n_out, blocks * tab
        first_kept, first_sent, value_kept, value_sent = packet_call(
            lambda *refs: keep_qkv_kernel(blocks, *refs),
            [flat(n_first), flat(n_first + 32), flat(n_value), flat(n_value + n_rows)],
            pos, qkv_args + (qkv_got, table_sent, vectors), after=(z_sent,),
        )
        first_got = swap_grp(first_sent, 2)
        value_got = swap_blk(value_sent, 1)
        (down_kept,), (down_sent,) = combine(
            pos, [("part", down_kept, down_got, 0, 2, 2 * part, 3, 0)], after=(value_sent,)
        )
        down_got = swap_blk(down_sent, 2)
        (up_kept,), (up_sent,) = combine(
            pos, [("part", up_kept, up_got, 0, planes, ff_out // 2, 1, 0)], after=(down_sent,)
        )
        up_got = swap_grp(up_sent, 2)
        (first_kept, vectors), (first_sent,) = combine(
            pos,
            [
                ("part", first_kept, first_got, 0, planes, n_out, 2, 0),
                ("vec", vectors, first_got, n_first, 0, 0, None, 0),
            ],
            after=(up_sent,),
        )
        first_got = swap_blk(first_sent, 1)
        (down_kept,), (down_sent,) = combine(
            pos, [("part", down_kept, down_got, 0, 1, 2 * part, 4, 0)], after=(first_sent,)
        )
        down_got = swap_blk(down_sent, 4)
        (value_kept, table_kept), (value_sent, table_sent) = combine(
            pos,
            [
                ("part", value_kept, value_got, 0, planes, n_out // 2, 1, 0),
                ("part", table_kept, value_got, n_value, 2, 2 * tab, None, 1),
            ],
            after=(down_sent,),
        )
        value_got = swap_grp(value_sent, 2)
        table_got = swap_blk(table_sent, 2)
        (down_kept, z_kept, up_kept), (down_sent, up_sent) = combine(
            pos,
            [
                ("part", down_kept, down_got, 0, 1, part, 2, 0),
                ("part", z_kept, z_got, 0, 1, z_rows, 2, 0),
                ("part", up_kept, up_got, 0, 2, ff_out // 2, 3, 1),
            ],
            after=(value_sent,),
        )
        down_got = swap_blk(down_sent, 1)
        up_got = swap_blk(up_sent, 2)
        (first_kept, value_kept, vectors), (first_sent,) = combine(
            pos,
            [
                ("part", first_kept, first_got, 0, 2, n_out, 3, 0),
                ("part", value_kept, value_got, 0, 2, n_out // 2, 3, 0),
                ("vec", vectors, first_got, n_value, 0, 0, None, 0),
            ],
            after=(up_sent,),
        )
        first_got = swap_blk(first_sent, 2)
        (up_kept, z_kept), (up_sent, z_sent) = combine(
            pos,
            [
                ("part", up_kept, up_got, 0, 1, ff_out // 2, 4, 0),
                ("part", z_kept, down_got, part, 1, z_rows // 2, 1, 1),
            ],
            after=(first_sent,),
        )
        up_got = swap_blk(up_sent, 4)
        z_got = swap_grp(z_sent, 2)
        (first_kept, value_kept, table_kept, vectors), (first_sent,) = combine(
            pos,
            [
                ("part", first_kept, first_got, 0, 1, n_out, 4, 0),
                ("part", value_kept, first_got, 2 * n_out, 1, n_out // 2, 4, 0),
                ("part", table_kept, table_got, 0, 1, 2 * tab, None, 0),
                ("vec", vectors, first_got, 3 * n_out, 0, 0, None, 0),
            ],
            after=(up_sent,),
        )
        first_got = swap_blk(first_sent, 4)
        early, (early_sent,) = combine(
            pos,
            [
                ("sum", down_kept, down_got, 0, 0, 0, None, 0),
                ("sum", z_kept, z_got, 0, 0, 0, None, 0),
            ],
            after=(first_sent,),
        )
        early_got = swap_grp(early_sent, 2)
        (up_part,), _ = combine(
            pos, [("sum", up_kept, up_got, 0, 0, 0, None, None)], after=(early_sent,)
        )
        def whole(value, other):
            return pick(x_bit, value, other), pick(x_bit, other, value)

        low, high = whole(early_sent, early_got)
        early = jnp.concatenate([low[:part], high[:part], low[part:], high[part:]], axis=0)
        up_rows = jnp.concatenate(whole(up_part, swap_grp(up_part, 2)), axis=0)
        out_up, out_down, out_out = big_outputs(up_rows, early)
        n_small = n_out + n_out // 2
        (first_part, value_part, table_part, vectors), _ = combine(
            pos,
            [
                ("sum", first_kept, first_got, 0, 0, 0, None, None),
                ("sum", value_kept, first_got, n_out, 0, 0, None, None),
                ("sum", table_kept, first_got, n_small, 0, 0, None, None),
                ("vec", vectors, first_got, n_small + 2 * tab, 0, 0, None, None),
            ],
            after=(out_up, out_down),
        )

        square = jnp.concatenate([first_part, value_part], axis=0)
        near_core = swap_grp(jnp.concatenate([square, vectors.astype(BF)], axis=0), 1)
        near, far = (square, swap_grp(square, 2)), (near_core[:n_small], swap_grp(square, 3))
        vectors = vectors + f(near_core[n_small:])
        sides = []
        for value, other in (near, far):
            low, high = pick(x_bit, value, other), pick(x_bit, other, value)
            sides.append(jnp.concatenate([low[:n_out], high[:n_out], low[n_out:], high[n_out:]], axis=0))
        square = (f(pick(core_bit, *sides)), f(pick(core_bit, *sides[::-1])))
        table_share = f(table_part)
    else:
        context_t, middle_t, act_t, grad_ffn, grad_pre, grad_attn = made
        lanes = lambda value, index: lax.dynamic_slice_in_dim(value, index * (value.shape[1] // 2), value.shape[1] // 2, 1)
        rows_of = lambda value, index: lax.dynamic_slice_in_dim(value, index * (value.shape[0] // 2), value.shape[0] // 2, 0)
        blocked = lambda value: value.reshape(blocks, value.shape[0] // blocks, value.shape[1])
        grad_queries, grad_keys_t, grad_values_t = attend_back(*back_args, ())
        table_kept, table_sent, grad_input_local, vectors = input_grads(
            blocks, grad_queries, grad_keys_t, grad_values_t, *input_args, ()
        )

        def packet(index):
            up = blocked(fwd_dot(middle_t, lanes(grad_pre, index)))
            return jnp.concatenate(
                [
                    blocked(fwd_dot(x_t[:, n_table:], lanes(grad_queries, index))),
                    blocked(back_dot(x_t, rows_of(grad_keys_t, index))),
                    blocked(back_dot(x_t, rows_of(grad_values_t, index))),
                    blocked(fwd_dot(context_t, lanes(grad_attn, index))),
                ]
                + [up[:, :, i : i + half_width] for i in range(0, up.shape[2], half_width)]
                + [blocked(fwd_dot(act_t, lanes(grad_ffn, index)))],
                axis=1,
            )

        total = (packet(core_bit) + f(swap_grp(packet(1 - core_bit).astype(BF), 1))).astype(BF)
        total = lax.psum_scatter(total, "blk", scatter_dimension=0, tiled=False)
        total = (f(total) + f(swap_grp(total, 2))).astype(BF)
        at = 4 * n_out
        square = total[: 3 * n_out]
        up_rows = total[at : at + ff_out]
        down_all = total[at + ff_out :]
        z_rows = jnp.concatenate([down_all[:first_rows], total[3 * n_out : at]], axis=0)
        down_rows = down_all[first_rows:]
        table_rows = jnp.stack([blocked_half.reshape(planes, 2 * tab, half_width) for blocked_half in (table_kept, table_sent)], axis=1)
        table_rows = table_rows.reshape(blocks, 2 * tab, half_width)
        table_rows = jnp.take(table_rows, jnp.arange(blocks) ^ own, axis=0)
        table_share = f(lax.psum_scatter(table_rows, "blk", scatter_dimension=0, tiled=False))
        vectors = lax.psum(vectors, ("blk", "grp"))
        early = jnp.concatenate([down_rows, z_rows], axis=0)
        out_up, out_down, out_out = big_outputs(up_rows, early)

    square = jnp.concatenate(square if packets else both_cores(square), axis=1)
    table_share = jnp.concatenate([table_share[:tab], table_share[tab:]], axis=1)
    vectors = jnp.concatenate([vectors[:16], vectors[16:]], axis=1)
    mine = lax.dynamic_slice_in_dim(vectors[:10], own * n_out, n_out, 1)
    up_bias_out = lax.dynamic_slice_in_dim(vectors[10:14].reshape(-1), own * ff_out, ff_out, 0)
    grad_input = grad_input_local.at[:tab].add(table_share)
    return (
        mixed,
        grad_input,
        mine[:2],
        square[:n_out],
        mine[2],
        square[n_out : 2 * n_out],
        square[2 * n_out :],
        mine[3],
        out_out,
        mine[4],
        mine[5],
        mine[6],
        out_up,
        up_bias_out,
        out_down,
        mine[7],
        mine[8],
        mine[9],
    )


def solution(mesh):
    both = ("grp", "blk")
    placed = (P(both, None), P(both), P(both), P(both)) + (P(),) * 16 + (P(both, None),)
    vec, mat = P("blk"), P("blk", None)
    return jax.shard_map(
        local,
        mesh=mesh,
        in_specs=placed,
        out_specs=(
            P(both, None), P(both, None), P(None, "blk"), mat, vec, mat, mat, vec, mat, vec,
            vec, vec, mat, vec, mat, vec, vec, vec,
        ),
        check_vma=False,
    )
```

```python
import math

import jax
import jax.numpy as jnp
from jax import lax
from jax.experimental import pallas as pl
from jax.experimental.pallas import tpu as pltpu
from jax.sharding import PartitionSpec as P

HEADS = 12
HEAD_DIM = 64
TAB_MAX = 64
LANES = 256
far_below = -1e30
BF = jnp.bfloat16
F32 = jnp.float32
MIB = 1 << 20
LONG = pl.CostEstimate(flops=40_000_000_000, bytes_accessed=MIB, transcendentals=0)
SHORT = pl.CostEstimate(flops=100000000, bytes_accessed=MIB, transcendentals=0)
HBM = pl.BlockSpec(memory_space=pltpu.HBM)


def outer_sum(left, right):
    return lax.dot_general(left, right, (((0,), (0,)), ((), ())), preferred_element_type=F32)


def back_dot(left, right):
    return lax.dot_general(left, right, (((1,), (1,)), ((), ())), preferred_element_type=F32)


def fwd_dot(left, right):
    return jnp.dot(left, right, preferred_element_type=F32)


def norm_parts(values):
    centred = values - jnp.mean(values, axis=-1, keepdims=True)
    spread = jnp.mean(centred * centred, axis=-1, keepdims=True)
    inv = lax.rsqrt(spread + 1e-06)
    return centred * inv, inv


def norm_grad(grad, normed, inv, gain):
    scaled = grad * gain
    return inv * (
        scaled
        - jnp.mean(scaled, axis=-1, keepdims=True)
        - normed * jnp.mean(scaled * normed, axis=-1, keepdims=True)
    )


def head_lanes(shape, index):
    lane = lax.broadcasted_iota(jnp.int32, shape, len(shape) - 1)
    return (lane >= index * HEAD_DIM) & (lane < (index + 1) * HEAD_DIM)


def column_of(row):
    return jnp.broadcast_to(row, (128, row.shape[1])).T[:, :1]


def start_copies(sources, targets, sems):
    copies = [pltpu.make_async_copy(a, b, sems.at[i]) for i, (a, b) in enumerate(zip(sources, targets))]
    for copy in copies:
        copy.start()
    return copies


def entry_kernel(tokens_any, seg_any, prev_any, answer_any, payload_ref, input_ref, *scratch):
    tab = TAB_MAX
    *held, sems = scratch
    for copy in start_copies((tokens_any, seg_any, prev_any, answer_any), held, sems):
        copy.wait()
    tokens_ref, seg_ref, prev_ref, answer_ref = held
    prev = prev_ref[...].astype(F32)[None]
    low = residual(tokens_ref, prev, answer_ref).astype(BF)
    input_ref[...] = low
    payload_ref[:tab] = low[:tab]
    payload_ref[tab:] = jnp.zeros((16, low.shape[1]), BF)
    lane = lax.broadcasted_iota(jnp.int32, (1, 128), 1)

    def twice(row):
        row = row[:, :128]
        return jnp.where(lane < tab, row, pltpu.roll(row, tab, 1))

    is_open = twice(jnp.where(seg_ref[...] == 0, 1.0, 0.0)[None])
    both = jnp.concatenate([is_open, twice(prev)], axis=1)
    payload_ref[tab:, :256] = jnp.broadcast_to(both, (16, 256)).astype(BF)


def residual(tokens_ref, prev, answer_ref):
    answers = answer_ref[...].astype(F32)
    return tokens_ref[...].astype(F32) + jnp.where(column_of(prev) == 1.0, answers[1:2], answers[0:1])


def entry(tokens, seg, prev, answers):
    rows, width = tokens.shape
    vmem = pl.BlockSpec(memory_space=pltpu.VMEM)
    return pl.pallas_call(
        entry_kernel,
        in_specs=[HBM] * 4,
        out_specs=[vmem] * 2,
        out_shape=[jax.ShapeDtypeStruct((TAB_MAX + 16, width), BF), jax.ShapeDtypeStruct((rows, width), BF)],
        scratch_shapes=[pltpu.VMEM(v.shape, v.dtype) for v in (tokens, seg, prev, answers)]
        + [pltpu.SemaphoreType.DMA((4,))],
        compiler_params=pltpu.CompilerParams(vmem_limit_bytes=60 * MIB),
    )(tokens, seg, prev, answers)


def own_kernel(
    input_ref, query_w_any, key_w_any, value_w_any, query_b_any, value_b_any, seg_any, turn_any,
    q_ref, k_ref, v_ref, bias_ref, value_row_ref, *scratch
):
    *held, sems = scratch
    query_w_ref, key_w_ref, value_w_ref, query_b_ref, value_b_ref, seg_ref, turn_ref = held
    sources = (query_w_any, key_w_any, value_w_any, query_b_any, value_b_any, seg_any, turn_any)
    for copy in start_copies(sources, held, sems):
        copy.wait()
    low = input_ref[...]
    query = fwd_dot(low, query_w_ref[...]) + query_b_ref[...].astype(F32)[None]
    q_ref[...] = (query.astype(BF).astype(F32) * HEAD_DIM**-0.5).astype(BF)
    k_ref[...] = fwd_dot(low, key_w_ref[...]).astype(BF)
    value_b = value_b_ref[...].astype(F32)[None]
    value_row_ref[...] = value_b
    v_ref[...] = (fwd_dot(low, value_w_ref[...]) + value_b).astype(BF)
    turn = turn_ref[...].astype(F32)[None]
    seg = seg_ref[...].astype(F32)[None]
    same = (column_of(turn) == turn) & (seg != 0.0)
    bias_ref[...] = jnp.where(same, 0.0, far_below)


def own_part(layer_input, query_w, key_w, value_w, query_b, value_b, seg, turn):
    rows, width = layer_input.shape
    vmem = pl.BlockSpec(memory_space=pltpu.VMEM)
    return pl.pallas_call(
        own_kernel,
        in_specs=[vmem] + [HBM] * 7,
        out_specs=[vmem] * 5,
        out_shape=[jax.ShapeDtypeStruct((rows, width), BF)] * 3
        + [jax.ShapeDtypeStruct((rows, rows), F32), jax.ShapeDtypeStruct((1, width), F32)],
        scratch_shapes=[
            pltpu.VMEM(v.shape, v.dtype) for v in (query_w, key_w, value_w, query_b, value_b, seg, turn)
        ]
        + [pltpu.SemaphoreType.DMA((7,))],
        compiler_params=pltpu.CompilerParams(vmem_limit_bytes=54 * MIB),
        cost_estimate=pl.CostEstimate(flops=100000000, bytes_accessed=MIB, transcendentals=0),
    )(layer_input, query_w, key_w, value_w, query_b, value_b, seg, turn)


def attend_kernel(
    views, input_ref, key_w_ref, value_w_ref, value_b_ref, q_ref, own_k_ref, own_v_ref, own_bias_ref, *refs
):
    *parts, keys_ref, values_ref, prob_ref, context_ref, x_t_ref, prev_ref, table_ref, bias_ref = refs
    n_table = table_ref.shape[0]
    tab = TAB_MAX
    slots = [parts[part].at[first : first + tab + 16] for part, first in views]

    @pl.when(pl.program_id(0) == 0)
    def _():
        lane = lax.broadcasted_iota(jnp.int32, (1, 128), 1)
        for i, slot in enumerate(slots):
            table_ref[i * tab : (i + 1) * tab] = slot[:tab]
        for i in range(0, len(slots), 2):
            marks = jnp.where(
                lax.broadcasted_iota(jnp.int32, (16, 256), 1) % 128 < tab,
                slots[i][tab:, :256].astype(F32), slots[i + 1][tab:, :256].astype(F32),
            )
            at = slice(i * tab, (i + 2) * tab)
            closed = jnp.where(marks[:1, :128] > 0.5, 0.0, far_below)
            bias_ref[:, at] = jnp.broadcast_to(closed, (bias_ref.shape[0], 128))
            prev_ref[:, at] = marks[:8, 128:]
        bias_ref[:, n_table:] = own_bias_ref[...]
        x_t_ref[:, :n_table] = table_ref[...].T
        x_t_ref[:, n_table:] = input_ref[...].T

    table = table_ref[...]
    keys_ref[:n_table] = fwd_dot(table, key_w_ref[...]).astype(BF)
    values_ref[:n_table] = (fwd_dot(table, value_w_ref[...]) + value_b_ref[...]).astype(BF)
    keys_ref[n_table:] = own_k_ref[...]
    values_ref[n_table:] = own_v_ref[...]
    queries = q_ref[...]
    context = jnp.zeros(context_ref.shape, F32)
    for h in range(queries.shape[1] // HEAD_DIM):
        mask = head_lanes(queries.shape, h)
        picked = jnp.where(mask, queries, jnp.zeros_like(queries))
        scores = back_dot(picked, keys_ref[...]) + bias_ref[...]
        top = jnp.max(scores, axis=-1, keepdims=True)
        weights = jnp.exp(scores - top)
        prob = (weights * (1.0 / jnp.sum(weights, axis=-1, keepdims=True))).astype(BF)
        prob_ref[h] = prob
        context = jnp.where(mask, fwd_dot(prob, values_ref[...]), context)
    context_ref[...] = context


def vmem_limit(n_keys, small):
    return (small if n_keys <= 1024 else 60) * MIB


def attend(parts, views, layer_input, key_w, value_w, value_b, queries, own_k, own_v, own_bias):
    rows, width = queries.shape
    n_table = len(views) * TAB_MAX
    n_keys = n_table + rows
    group = LANES if n_keys <= 1024 else LANES // 2
    per = group // HEAD_DIM
    steady = {} if n_keys <= 1024 else {"pipeline_mode": pl.Buffered(1)}
    whole = lambda shape: pl.BlockSpec(shape, lambda i: (0, 0), **steady)
    lanes = lambda n: pl.BlockSpec((n, group), lambda i: (0, i))
    return pl.pallas_call(
        lambda *refs: attend_kernel(views, *refs),
        grid=(width // group,),
        in_specs=[
            whole((rows, width)), lanes(width), lanes(width), lanes(1), lanes(rows), lanes(rows), lanes(rows),
            whole((rows, rows)),
        ]
        + [whole(part.shape) for part in parts],
        out_specs=[
            lanes(n_keys), lanes(n_keys), pl.BlockSpec((per, rows, n_keys), lambda i: (i, 0, 0)), lanes(rows),
            whole((width, n_keys)), whole((8, n_table)),
        ],
        out_shape=[
            jax.ShapeDtypeStruct((n_keys, width), BF),
            jax.ShapeDtypeStruct((n_keys, width), BF),
            jax.ShapeDtypeStruct((HEADS, rows, n_keys), BF),
            jax.ShapeDtypeStruct((rows, width), F32),
            jax.ShapeDtypeStruct((width, n_keys), BF),
            jax.ShapeDtypeStruct((8, n_table), F32),
        ],
        scratch_shapes=[pltpu.VMEM((n_table, width), BF), pltpu.VMEM((rows, n_keys), F32)],
        compiler_params=pltpu.CompilerParams(vmem_limit_bytes=vmem_limit(n_keys, 60)),
        cost_estimate=pl.CostEstimate(flops=100000000, bytes_accessed=MIB, transcendentals=0),
    )(layer_input, key_w, value_w, value_b, queries, own_k, own_v, own_bias, *parts)


def middle_kernel(
    packets, pos_ref, tokens_ref, prev_ref, answer_ref, context_ref, cot_ref, out_w_any, up_w_any, down_w_any,
    up_b_1d_ref, *refs
):
    biases, refs = refs[:6], refs[6:]
    mixed_ref, grad_context_ref, grad_mid_ref, sums_ref, up_sum_ref = refs[:5]
    refs = refs[5:]
    if packets:
        anys, refs = refs[:5], refs[5:]
    context_t_ref, middle_t_ref, act_t_ref, grad_ffn_ref, grad_pre_ref, grad_attn_ref = refs[:6]
    slope_ref, total_ref, middle_low_ref, out_w_ref, up_w_ref, down_w_ref, up_b_ref, sems = refs[6:14]
    width, hidden = up_w_ref.shape
    tile = width
    steps = hidden // tile

    def tile_copies(i):
        at = pl.ds(i * tile, tile)
        return (
            pltpu.make_async_copy(up_w_any.at[:, at], up_w_ref.at[:, at], sems.at[2 * i + 1]),
            pltpu.make_async_copy(down_w_any.at[at, :], down_w_ref.at[at, :], sems.at[2 * i + 2]),
        )

    out_copy = pltpu.make_async_copy(out_w_any, out_w_ref, sems.at[0])
    out_copy.start()
    for i in range(steps):
        for copy in tile_copies(i):
            copy.start()
    out_b, norm_g, norm_s, down_b, final_g, final_s = (ref[...].astype(F32)[None] for ref in biases)
    up_b_ref[...] = up_b_1d_ref[...].astype(F32)[None]
    resid = residual(tokens_ref, prev_ref[...].astype(F32)[None], answer_ref)
    column = lambda v: jnp.sum(v, axis=0, keepdims=True)
    context_low = context_ref[...].astype(BF)
    context_t_ref[...] = context_low.T
    out_copy.wait()
    normed1, inv1 = norm_parts(resid + fwd_dot(context_low, out_w_ref[...]) + out_b)
    middle = normed1 * norm_g + norm_s
    middle_low = middle.astype(BF)
    middle_low_ref[...] = middle_low
    middle_t_ref[...] = middle_low.T
    total_ref[...] = middle + down_b

    def forward(i):
        at = pl.ds(i * tile, tile)
        for copy in tile_copies(i):
            copy.wait()
        pre = fwd_dot(middle_low_ref[...], up_w_ref[:, at]) + up_b_ref[:, at]
        cdf = 0.5 * (1.0 + lax.erf(pre * (0.5**0.5)))
        act = (pre * cdf).astype(BF)
        act_t_ref[at, :] = act.T
        slope_ref[:, at] = cdf + pre * jnp.exp(-0.5 * pre * pre) * (1.0 / math.sqrt(2 * math.pi))
        total_ref[...] += fwd_dot(act, down_w_ref[at, :])

    for i in range(steps):
        forward(i)
    normed2, inv2 = norm_parts(total_ref[...])
    mixed_ref[...] = (normed2 * final_g + final_s).astype(BF)
    cot = cot_ref[...].astype(F32)
    grad_final = norm_grad(cot, normed2, inv2, final_g)
    grad_ffn = grad_final.astype(BF)
    grad_ffn_ref[...] = grad_ffn
    total_ref[...] = grad_final

    def backward(i, carry):
        at = pl.ds(pl.multiple_of(i * tile, tile), tile)
        grad_pre = (back_dot(grad_ffn_ref[...], down_w_ref[at, :]) * slope_ref[:, at]).astype(BF)
        grad_pre_ref[:, at] = grad_pre
        up_sum_ref[:, at] = column(grad_pre.astype(F32))
        total_ref[...] += back_dot(grad_pre, up_w_ref[:, at])
        return carry

    copies = []
    if packets:
        blocks = packets
        sent_ref, down_own_ref, z_own_ref, up_sent_ref, up_own_ref, out_sems = refs[14:]
        half = width // 2
        small, size = width // blocks, hidden // blocks
        first_rows = 2 * small // 3
        z_rows, rows = first_rows + small, size - first_rows
        core = pos_ref[0]
        n_down = blocks * rows

        def leave(source, target):
            copy = pltpu.make_async_copy(source, target, out_sems.at[len(copies)])
            copy.start()
            copies.append(copy)

        def lanes_of(own):
            return pl.ds(pl.multiple_of((core if own else 1 - core) * half, 128), half)

        for own, down_ref, first_z, z_ref in ((False, sent_ref, n_down, sent_ref), (True, down_own_ref, 0, z_own_ref)):
            part = grad_ffn_ref[:, lanes_of(own)]
            for b in range(blocks):
                value = fwd_dot(act_t_ref[b * size : (b + 1) * size], part).astype(BF)
                down_ref[b * rows : (b + 1) * rows] = value[first_rows:]
                z_ref[first_z + b * z_rows : first_z + b * z_rows + first_rows] = value[:first_rows]
            leave(down_ref.at[:n_down], (anys[1] if own else anys[0].at[:n_down]))
        for i in range(steps):
            t = lax.rem(2 * (1 - core) + i, steps)
            backward(t, 0)
            value = fwd_dot(middle_t_ref[...], grad_pre_ref[:, pl.ds(pl.multiple_of(t * tile, tile), tile)]).astype(BF)
            target = up_sent_ref if i < steps // 2 else up_own_ref
            for b in range(blocks):
                for q in range(2):
                    first = b * size + (2 * (i % (steps // 2)) + q) * small
                    target[first : first + small] = value[b * small : (b + 1) * small, q * half : (q + 1) * half]
            if i == steps // 2 - 1:
                leave(up_sent_ref, anys[3])
        leave(up_own_ref, anys[4])
    else:
        lax.fori_loop(0, steps, backward, 0)
    grad_middle = total_ref[...]
    grad_mid = norm_grad(grad_middle, normed1, inv1, norm_g)
    grad_mid_ref[...] = grad_mid
    grad_attn = grad_mid.astype(BF)
    grad_attn_ref[...] = grad_attn
    if packets:
        for own, first_z, z_ref in ((False, n_down, sent_ref), (True, 0, z_own_ref)):
            value = fwd_dot(context_t_ref[...], grad_attn_ref[:, lanes_of(own)]).astype(BF)
            for b in range(blocks):
                first = first_z + b * z_rows + first_rows
                z_ref[first : first + small] = value[b * small : (b + 1) * small]
            if own:
                leave(z_own_ref, anys[2])
            else:
                leave(sent_ref.at[n_down:], anys[0].at[n_down:])
    grad_context_ref[...] = back_dot(grad_attn, out_w_ref[...]).astype(BF)
    sums_ref[0:1] = column(grad_attn.astype(F32))
    sums_ref[1:2] = column(grad_middle * normed1)
    sums_ref[2:3] = column(grad_middle)
    sums_ref[3:4] = column(grad_ffn.astype(F32))
    sums_ref[4:5] = column(cot * normed2)
    sums_ref[5:6] = column(cot)
    sums_ref[6:8] = jnp.zeros((2, sums_ref.shape[1]), F32)
    for copy in copies:
        copy.wait()


def middle_part(packets, pos, tokens, prev, answers, context, cot, out_w, up_w, down_w, up_b, *biases):
    rows, width = tokens.shape
    hidden = up_w.shape[1]
    half = width // 2
    vmem, away = pl.BlockSpec(memory_space=pltpu.VMEM), pl.BlockSpec(memory_space=pl.ANY)
    shape = lambda n, t: jax.ShapeDtypeStruct((rows, n), t)
    turned = lambda n: jax.ShapeDtypeStruct((n, rows), BF)
    inner = [turned(width), turned(width), turned(hidden), shape(width, BF), shape(hidden, BF), shape(width, BF)]
    held = lambda shapes: [pltpu.VMEM(v.shape, v.dtype) for v in shapes]
    outs = [
        shape(width, BF), shape(width, BF), shape(width, F32), jax.ShapeDtypeStruct((8, width), F32),
        jax.ShapeDtypeStruct((1, hidden), F32),
    ]
    scratch = [
        pltpu.VMEM((rows, hidden), F32), pltpu.VMEM((rows, width), F32), pltpu.VMEM((rows, width), BF),
        pltpu.VMEM(out_w.shape, BF), pltpu.VMEM(up_w.shape, BF), pltpu.VMEM(down_w.shape, BF),
        pltpu.VMEM((1, hidden), F32), pltpu.SemaphoreType.DMA((1 + 2 * (hidden // width),)),
    ]
    specs = [vmem] * 5
    if packets:
        first_rows = 2 * width // 3
        z_rows, down_rows = first_rows + width, hidden - first_rows
        packed = [
            jax.ShapeDtypeStruct((n, half), BF) for n in (down_rows + z_rows, down_rows, z_rows, hidden, hidden)
        ]
        scratch = held(inner) + scratch + held(packed) + [pltpu.SemaphoreType.DMA((6,))]
        outs, specs = outs + packed, specs + [away] * 5
    else:
        outs, specs = outs + inner, specs + [vmem] * 6
    return pl.pallas_call(
        lambda *refs: middle_kernel(packets, *refs),
        in_specs=[pl.BlockSpec(memory_space=pltpu.SMEM)] + [vmem] * 5 + [HBM] * 3 + [vmem] * 7,
        out_specs=specs,
        out_shape=outs,
        scratch_shapes=scratch,
        compiler_params=pltpu.CompilerParams(vmem_limit_bytes=60 * MIB),
        cost_estimate=pl.CostEstimate(flops=100000000, bytes_accessed=MIB, transcendentals=0),
    )(pos, tokens, prev, answers, context, cot, out_w, up_w, down_w, up_b, *biases)


def attend_back_kernel(
    q_ref, keys_ref, values_ref, prob_ref, context_ref, grad_ref, *refs
):
    grad_q_ref, grad_k_ref, grad_v_ref = refs[-3:]
    grad = grad_ref[...]
    grad_f = grad.astype(F32)
    product = grad_f * context_ref[...]
    grad_t = grad_f.T.astype(BF)
    q_t = q_ref[...].astype(F32).T.astype(BF)
    grad_q = jnp.zeros(grad.shape, F32)
    for h in range(grad.shape[1] // HEAD_DIM):
        mask = head_lanes(grad.shape, h)
        at = slice(h * HEAD_DIM, (h + 1) * HEAD_DIM)
        row_dot = jnp.sum(jnp.where(mask, product, 0.0), axis=-1, keepdims=True)
        grad_prob = back_dot(jnp.where(mask, grad, jnp.zeros_like(grad)), values_ref[...])
        prob = prob_ref[h]
        grad_score = (prob.astype(F32) * (grad_prob - row_dot)).astype(BF)
        grad_v_ref[at] = fwd_dot(grad_t[at], prob).astype(BF)
        grad_k_ref[at] = fwd_dot(q_t[at], grad_score).astype(BF)
        grad_q = jnp.where(mask, fwd_dot(grad_score, keys_ref[...]), grad_q)
    grad_q_ref[...] = (grad_q * HEAD_DIM**-0.5).astype(BF)


def attend_back(queries, keys, values, prob, context, grad_context, after):
    rows, width = queries.shape
    n_keys = keys.shape[0]
    group = LANES if n_keys <= 1024 else LANES // 2
    per = group // HEAD_DIM
    lanes = lambda n: pl.BlockSpec((n, group), lambda i: (0, i))
    return pl.pallas_call(
        attend_back_kernel,
        grid=(width // group,),
        in_specs=[
            lanes(rows), lanes(n_keys), lanes(n_keys), pl.BlockSpec((per, rows, n_keys), lambda i: (i, 0, 0)),
            lanes(rows), lanes(rows),
        ]
        + [pl.BlockSpec(memory_space=pl.ANY)] * len(after),
        out_specs=[lanes(rows)] + [pl.BlockSpec((group, n_keys), lambda i: (i, 0))] * 2,
        out_shape=[
            jax.ShapeDtypeStruct((rows, width), BF),
            jax.ShapeDtypeStruct((width, n_keys), BF),
            jax.ShapeDtypeStruct((width, n_keys), BF),
        ],
        compiler_params=pltpu.CompilerParams(vmem_limit_bytes=vmem_limit(n_keys, 54)),
        cost_estimate=LONG,
    )(queries, keys, values, prob, context, grad_context, *after)


def core_lanes(pos_ref, own, size):
    core = pos_ref[0] if own else 1 - pos_ref[0]
    return pl.ds(pl.multiple_of(core * size, 128), size)


def qkv_values(own, pos_ref, x_t_ref, grad_q_ref, grad_k_ref, grad_v_ref, blocks, store):
    half = grad_q_ref.shape[1] // 2
    n_table = x_t_ref.shape[1] - grad_q_ref.shape[0]
    small = x_t_ref.shape[0] // blocks
    at = core_lanes(pos_ref, own, half)
    core = pos_ref[0] if own else 1 - pos_ref[0]
    rows = pl.ds(pl.multiple_of(core * half, 128), half)
    values = (
        fwd_dot(x_t_ref[:, n_table:], grad_q_ref[:, at]),
        back_dot(x_t_ref[...], grad_k_ref[rows, :]),
        back_dot(x_t_ref[...], grad_v_ref[rows, :]),
    )
    for i, value in enumerate(values):
        for b in range(blocks):
            store(b, i * small, value[b * small : (b + 1) * small])


def send_kernel(make, n_in, blocks, *refs):
    pos_ref, out_ref = refs[0], refs[-1]

    def store(b, first, value):
        out_ref[b, first : first + value.shape[0]] = value.astype(BF)

    make(False, pos_ref, *refs[1 : 1 + n_in], blocks, store)


def pick(bit, first, second):
    return jnp.where(bit == 0, first, second)


def keep_qkv_kernel(
    blocks, pos_ref, x_t_ref, grad_q_ref, grad_k_ref, grad_v_ref, got_ref, table_ref, vec_ref, *outs
):
    first_kept_ref, first_sent_ref, kept_ref, sent_ref = outs
    small = x_t_ref.shape[0] // blocks
    planes = blocks // 2
    held = {}

    def store(b, first, value):
        value = (value + got_ref[b, first : first + small].astype(F32)).astype(BF)
        held[b, first] = value
        if first == small:
            query = held.pop((b, 0))
            rows = slice(b * small, (b + 1) * small)
            first_kept_ref[rows] = pick(pos_ref[1], query, value)
            first_sent_ref[rows] = pick(pos_ref[1], value, query)
        if first == 2 * small and b % 2 == 1:
            rows = slice(b // 2 * small, (b // 2 + 1) * small)
            kept_ref[rows] = pick(pos_ref[2], held[b - 1, first], value)
            sent_ref[rows] = pick(pos_ref[2], value, held[b - 1, first])

    qkv_values(True, pos_ref, x_t_ref, grad_q_ref, grad_k_ref, grad_v_ref, blocks, store)
    first_sent_ref[blocks * small :] = vec_ref[...].astype(BF)
    sent_ref[planes * small :] = table_ref[...]


def inputs_kernel(
    blocks, grad_q_ref, grad_k_ref, grad_v_ref, query_w_ref, key_w_ref, value_w_ref, grad_mid_ref, prev_ref,
    table_prev_ref, sums_ref, up_sum_ref, *refs
):
    table_kept_ref, table_sent_ref, grad_ref, vec_ref = refs[-4:]
    tab = TAB_MAX
    n_table = blocks * tab
    rows, width = grad_q_ref.shape
    half = width // 2
    own = fwd_dot(key_w_ref[...], grad_k_ref[:, n_table:]) + fwd_dot(value_w_ref[...], grad_v_ref[:, n_table:])
    grad = grad_mid_ref[...] + back_dot(grad_q_ref[...], query_w_ref[...]) + own.T
    grad_ref[...] = grad
    is_one = column_of(prev_ref[...].astype(F32)[None]) == 1.0
    one_sum = jnp.sum(jnp.where(is_one, grad, 0.0), axis=0, keepdims=True)
    zero_sum = jnp.sum(jnp.where(is_one, 0.0, grad), axis=0, keepdims=True)
    step = min(n_table, 512)
    row = lax.broadcasted_iota(jnp.int32, (8, step), 0)
    for first in range(0, n_table, step):
        at = slice(first, first + step)
        part = (fwd_dot(key_w_ref[...], grad_k_ref[:, at]) + fwd_dot(value_w_ref[...], grad_v_ref[:, at])).astype(BF)
        marks = table_prev_ref[:, at]
        marks = jnp.where(row == 0, marks, 1.0 - marks).astype(BF)
        table_sums = back_dot(marks, part)
        one_sum += table_sums[0:1]
        zero_sum += table_sums[1:2]
        for j in range(step // 128):
            pair = part[:, j * 128 : (j + 1) * 128].T
            slot = first // 128 + j
            for k, ref in enumerate((table_kept_ref, table_sent_ref)):
                for side in range(2):
                    ref[(slot * 2 + side) * tab : (slot * 2 + side + 1) * tab] = pair[
                        k * tab : (k + 1) * tab, side * half : (side + 1) * half
                    ]
    ones = jnp.ones((8, grad_v_ref.shape[1]), BF)
    lines = [
        zero_sum,
        one_sum,
        jnp.sum(grad_q_ref[...].astype(F32), axis=0, keepdims=True),
        back_dot(ones, grad_v_ref[...])[0:1],
    ]
    lines += [sums_ref[i : i + 1] for i in range(6)]
    lines += [up_sum_ref[:, i * width : (i + 1) * width] for i in range(up_sum_ref.shape[1] // width)]
    vec_ref[...] = jnp.zeros(vec_ref.shape, F32)
    for i, line in enumerate(lines):
        for side in range(2):
            vec_ref[side * 16 + i : side * 16 + i + 1] = line[:, side * half : (side + 1) * half]


def input_grads(blocks, grad_q, grad_k, grad_v, query_w, key_w, value_w, grad_mid, prev, table_prev, sums, up_sum, after):
    rows, width = grad_q.shape
    n_half = blocks * TAB_MAX
    vmem = pl.BlockSpec(memory_space=pltpu.VMEM)
    args = (grad_q, grad_k, grad_v, query_w, key_w, value_w, grad_mid, prev, table_prev, sums, up_sum)
    return pl.pallas_call(
        lambda *refs: inputs_kernel(blocks, *refs),
        in_specs=[vmem] * len(args) + [pl.BlockSpec(memory_space=pl.ANY)] * len(after),
        out_specs=[vmem] * 4,
        out_shape=[
            jax.ShapeDtypeStruct((n_half, width // 2), BF),
            jax.ShapeDtypeStruct((n_half, width // 2), BF),
            jax.ShapeDtypeStruct((rows, width), F32),
            jax.ShapeDtypeStruct((32, width // 2), F32),
        ],
        compiler_params=pltpu.CompilerParams(vmem_limit_bytes=(20 if blocks <= 8 else 56) * MIB),
        cost_estimate=LONG,
    )(*args, *after)


def combine(pos, items, after=()):
    width = items[0][1].shape[1]
    gots, shapes, heights, places = [], [], {}, []
    for kind, kept, got, first, outer, inner, bit, message in items:
        if got is not None and not any(got is g for g in gots):
            gots.append(got)
        rows = kept.shape[0] if kind != "part" else outer * inner
        if kind != "copy":
            shapes.append(jax.ShapeDtypeStruct((rows, width), kept.dtype))
        if message is not None:
            places.append(heights.get(message, 0))
            heights[message] = places[-1] + rows
        else:
            places.append(None)
    sizes = [heights[m] for m in sorted(heights)]
    shapes += [jax.ShapeDtypeStruct((n, width), BF) for n in sizes]
    which = [next((i for i, g in enumerate(gots) if g is item[2]), None) for item in items]
    n_outs = sum(item[0] != "copy" for item in items)

    def body(pos_ref, *refs):
        kept_refs, refs = refs[: len(items)], refs[len(items) :]
        got_refs, refs = refs[: len(gots)], refs[len(gots) + len(after) :]
        out_refs, sent_refs = list(refs[:n_outs]), refs[n_outs:]
        for i, (kind, _, _, first, outer, inner, bit, message) in enumerate(items):
            kept_ref = kept_refs[i]
            n = kept_ref.shape[0]
            if kind == "copy":
                sent_refs[message][places[i] : places[i] + n] = kept_ref[...]
                continue
            got_ref, out_ref = got_refs[which[i]], out_refs.pop(0)
            if kind == "vec":
                total = kept_ref[...] + got_ref[first : first + n].astype(F32)
                out_ref[...] = total
                if message is not None:
                    sent_refs[message][places[i] : places[i] + n] = total.astype(BF)
            elif kind == "sum":
                total = kept_ref[...].astype(F32) + got_ref[first : first + n].astype(F32)
                out_ref[...] = total.astype(BF)
                if message is not None:
                    sent_refs[message][places[i] : places[i] + n] = total.astype(BF)
            else:
                for o in range(outer):
                    halves = []
                    for side in range(2):
                        at = (2 * o + side) * inner
                        total = kept_ref[at : at + inner].astype(F32)
                        total = total + got_ref[first + at : first + at + inner].astype(F32)
                        halves.append(total.astype(BF))
                    rows = slice(places[i] + o * inner, places[i] + (o + 1) * inner)
                    if bit is None:
                        out_ref[o * inner : (o + 1) * inner], sent_refs[message][rows] = halves
                    else:
                        out_ref[o * inner : (o + 1) * inner] = pick(pos_ref[bit], *halves)
                        sent_refs[message][rows] = pick(pos_ref[bit], *halves[::-1])

    vmem = pl.BlockSpec(memory_space=pltpu.VMEM)
    results = pl.pallas_call(
        body,
        in_specs=[pl.BlockSpec(memory_space=pltpu.SMEM)]
        + [vmem] * (len(items) + len(gots))
        + [pl.BlockSpec(memory_space=pl.ANY)] * len(after),
        out_specs=[vmem] * len(shapes),
        out_shape=shapes,
        compiler_params=pltpu.CompilerParams(vmem_limit_bytes=16 * MIB),
        cost_estimate=LONG,
    )(pos, *[item[1] for item in items], *gots, *after)
    return results[:n_outs], results[n_outs:]


def packet_call(kernel, shapes, pos, args, after=(), scratch=(), wide=(), cost=LONG):
    smem, vmem = pl.BlockSpec(memory_space=pltpu.SMEM), pl.BlockSpec(memory_space=pltpu.VMEM)
    outs = [jax.ShapeDtypeStruct(shape, BF) for shape in shapes]
    outs += [jax.ShapeDtypeStruct(shape, F32) for shape in wide]

    def body(*refs):
        n = 1 + len(args)
        kernel(*refs[:n], *refs[n + len(after) :])

    return pl.pallas_call(
        body,
        in_specs=[smem] + [vmem] * len(args) + [pl.BlockSpec(memory_space=pl.ANY)] * len(after),
        out_specs=[vmem] * len(outs),
        out_shape=outs,
        scratch_shapes=list(scratch),
        compiler_params=pltpu.CompilerParams(vmem_limit_bytes=20 * MIB),
        cost_estimate=cost,
    )(pos, *args, *after)


def local(
    tokens, seg_ids, turn_ids, prev_ids, answer_table, query_weight, query_bias,
    key_weight, value_weight, value_bias, out_weight, out_bias, norm_gain, norm_shift,
    up_weight, up_bias, down_weight, down_bias, final_gain, final_shift, cotangent,
):
    rows, width = tokens.shape
    blocks = lax.axis_size("blk")
    grps = lax.axis_size("grp")
    tab = TAB_MAX
    scale = HEAD_DIM ** (-0.5)
    f = lambda v: v.astype(F32)
    core_bit = lax.axis_index("grp") & 1
    x_bit = lax.axis_index("grp") >> 1
    own = lax.axis_index("blk")
    planes = blocks // 2
    n_out = width // blocks
    ff_out = up_weight.shape[1] // blocks
    half_width = width // 2
    n_table = blocks * tab
    pos = jnp.stack([core_bit, x_bit, own & 1, (own >> 1) & 1, own >> 2]).astype(jnp.int32)

    def swap_grp(value, mask):
        return lax.ppermute(value, "grp", [(i, i ^ mask) for i in range(grps)])

    def swap_blk(value, mask):
        return lax.ppermute(value, "blk", [(i, i ^ mask) for i in range(blocks)])

    payload, layer_input = entry(tokens, seg_ids, prev_ids, answer_table)
    slots = [payload] + [None] * (blocks - 1)
    for k in range(1, planes):
        slots[2 * k] = swap_blk(payload, 2 * k)
    slots[1] = swap_blk(payload, 1)
    for k in range(1, planes):
        slots[2 * k + 1] = swap_blk(slots[2 * k], 1)
    queries, own_keys, own_values, own_bias, value_row = own_part(
        layer_input, query_weight, key_weight, value_weight, query_bias, value_bias, seg_ids, turn_ids
    )
    views = [(i, 0) for i in range(blocks)]
    keys, values, prob, context, x_t, table_prev = attend(
        slots, views, layer_input, key_weight, value_weight, value_row, queries, own_keys, own_values, own_bias
    )
    first_rows = 2 * n_out // 3
    def both_cores(value):
        other = swap_grp(value, 1)
        return f(pick(core_bit, value, other)), f(pick(core_bit, other, value))

    def big_outputs(up_rows, early):
        sides = both_cores(up_rows)
        out_up = jnp.concatenate([side[i : i + n_out] for side in sides for i in range(0, ff_out, n_out)], axis=1)
        sides = both_cores(early)
        at_z = ff_out - first_rows
        out_down = jnp.concatenate(
            [
                jnp.concatenate([side[at_z : at_z + first_rows] for side in sides], axis=1),
                jnp.concatenate([side[:at_z] for side in sides], axis=1),
            ],
            axis=0,
        )
        out_out = jnp.concatenate([side[at_z + first_rows :] for side in sides], axis=1)
        return out_up, out_down, out_out

    packets = blocks if blocks == 8 and n_out % 32 == 0 else 0
    mixed, grad_context, grad_mid_sum, sums, up_sum, *made = middle_part(
        packets, pos, tokens, prev_ids, answer_table, context, cotangent, out_weight, up_weight, down_weight, up_bias,
        out_bias, norm_gain, norm_shift, down_bias, final_gain, final_shift,
    )
    first_rows = 2 * n_out // 3
    part, z_rows = (ff_out - first_rows) // 2, n_out + first_rows
    back_args = (queries, keys, values, prob, context, grad_context)
    input_args = (query_weight, key_weight, value_weight, grad_mid_sum, prev_ids, table_prev, sums, up_sum)

    if packets:
        flat = lambda rows: (rows, half_width)
        down_sent, down_kept, z_kept, up_sent, up_kept = made
        down_got = swap_grp(down_sent, 1)
        up_got = swap_grp(up_sent, 1)
        grad_queries, grad_keys_t, grad_values_t = attend_back(*back_args, ())
        (down_kept, z_kept), (down_sent, z_sent) = combine(
            pos,
            [
                ("part", down_kept, down_got, 0, blocks, part, 1, 0),
                ("part", z_kept, down_got, 2 * blocks * part, 2, 2 * z_rows, 3, 1),
            ],
            after=(grad_queries,),
        )
        down_got = swap_grp(down_sent, 2)
        z_got = swap_blk(z_sent, 2)
        (up_kept,), (up_sent,) = combine(
            pos, [("part", up_kept, up_got, 0, planes, ff_out, 2, 0)], after=(down_sent,)
        )
        up_got = swap_blk(up_sent, 1)
        qkv_args = (x_t, grad_queries, grad_keys_t, grad_values_t)
        (qkv_sent,) = packet_call(
            lambda *refs: send_kernel(qkv_values, 4, blocks, *refs),
            [(blocks, 3 * n_out, half_width)], pos, qkv_args, after=(up_sent,),
        )
        qkv_got = swap_grp(qkv_sent, 1)
        table_kept, table_sent, grad_input_local, vectors = input_grads(
            blocks, grad_queries, grad_keys_t, grad_values_t, *input_args, (qkv_sent,)
        )
        (z_kept,), (z_sent,) = combine(pos, [("part", z_kept, z_got, 0, 1, 2 * z_rows, 4, 0)], after=(table_sent,))
        z_got = swap_blk(z_sent, 4)
        n_first, n_value, n_rows = blocks * n_out, planes * n_out, blocks * tab
        first_kept, first_sent, value_kept, value_sent = packet_call(
            lambda *refs: keep_qkv_kernel(blocks, *refs),
            [flat(n_first), flat(n_first + 32), flat(n_value), flat(n_value + n_rows)],
            pos, qkv_args + (qkv_got, table_sent, vectors), after=(z_sent,),
        )
        first_got = swap_grp(first_sent, 2)
        value_got = swap_blk(value_sent, 1)
        (down_kept,), (down_sent,) = combine(
            pos, [("part", down_kept, down_got, 0, 2, 2 * part, 3, 0)], after=(value_sent,)
        )
        down_got = swap_blk(down_sent, 2)
        (up_kept,), (up_sent,) = combine(
            pos, [("part", up_kept, up_got, 0, planes, ff_out // 2, 1, 0)], after=(down_sent,)
        )
        up_got = swap_grp(up_sent, 2)
        (first_kept, vectors), (first_sent,) = combine(
            pos,
            [
                ("part", first_kept, first_got, 0, planes, n_out, 2, 0),
                ("vec", vectors, first_got, n_first, 0, 0, None, 0),
            ],
            after=(up_sent,),
        )
        first_got = swap_blk(first_sent, 1)
        (down_kept,), (down_sent,) = combine(
            pos, [("part", down_kept, down_got, 0, 1, 2 * part, 4, 0)], after=(first_sent,)
        )
        down_got = swap_blk(down_sent, 4)
        (value_kept, table_kept), (value_sent, table_sent) = combine(
            pos,
            [
                ("part", value_kept, value_got, 0, planes, n_out // 2, 1, 0),
                ("part", table_kept, value_got, n_value, 2, 2 * tab, None, 1),
            ],
            after=(down_sent,),
        )
        value_got = swap_grp(value_sent, 2)
        table_got = swap_blk(table_sent, 2)
        (down_kept, z_kept, up_kept), (down_sent, up_sent) = combine(
            pos,
            [
                ("part", down_kept, down_got, 0, 1, part, 2, 0),
                ("part", z_kept, z_got, 0, 1, z_rows, 2, 0),
                ("part", up_kept, up_got, 0, 2, ff_out // 2, 3, 1),
            ],
            after=(value_sent,),
        )
        down_got = swap_blk(down_sent, 1)
        up_got = swap_blk(up_sent, 2)
        (first_kept, value_kept, vectors), (first_sent,) = combine(
            pos,
            [
                ("part", first_kept, first_got, 0, 2, n_out, 3, 0),
                ("part", value_kept, value_got, 0, 2, n_out // 2, 3, 0),
                ("vec", vectors, first_got, n_value, 0, 0, None, 0),
            ],
            after=(up_sent,),
        )
        first_got = swap_blk(first_sent, 2)
        (up_kept, z_kept), (up_sent, z_sent) = combine(
            pos,
            [
                ("part", up_kept, up_got, 0, 1, ff_out // 2, 4, 0),
                ("part", z_kept, down_got, part, 1, z_rows // 2, 1, 1),
            ],
            after=(first_sent,),
        )
        up_got = swap_blk(up_sent, 4)
        z_got = swap_grp(z_sent, 2)
        (first_kept, value_kept, table_kept, vectors), (first_sent,) = combine(
            pos,
            [
                ("part", first_kept, first_got, 0, 1, n_out, 4, 0),
                ("part", value_kept, first_got, 2 * n_out, 1, n_out // 2, 4, 0),
                ("part", table_kept, table_got, 0, 1, 2 * tab, None, 0),
                ("vec", vectors, first_got, 3 * n_out, 0, 0, None, 0),
            ],
            after=(up_sent,),
        )
        first_got = swap_blk(first_sent, 4)
        early, (early_sent,) = combine(
            pos,
            [
                ("sum", down_kept, down_got, 0, 0, 0, None, 0),
                ("sum", z_kept, z_got, 0, 0, 0, None, 0),
            ],
            after=(first_sent,),
        )
        early_got = swap_grp(early_sent, 2)
        (up_part,), _ = combine(
            pos, [("sum", up_kept, up_got, 0, 0, 0, None, None)], after=(early_sent,)
        )
        def whole(value, other):
            return pick(x_bit, value, other), pick(x_bit, other, value)

        low, high = whole(early_sent, early_got)
        early = jnp.concatenate([low[:part], high[:part], low[part:], high[part:]], axis=0)
        up_rows = jnp.concatenate(whole(up_part, swap_grp(up_part, 2)), axis=0)
        out_up, out_down, out_out = big_outputs(up_rows, early)
        n_small = n_out + n_out // 2
        (first_part, value_part, table_part, vectors), _ = combine(
            pos,
            [
                ("sum", first_kept, first_got, 0, 0, 0, None, None),
                ("sum", value_kept, first_got, n_out, 0, 0, None, None),
                ("sum", table_kept, first_got, n_small, 0, 0, None, None),
                ("vec", vectors, first_got, n_small + 2 * tab, 0, 0, None, None),
            ],
            after=(out_up, out_down),
        )

        square = jnp.concatenate([first_part, value_part], axis=0)
        near_core = swap_grp(jnp.concatenate([square, vectors.astype(BF)], axis=0), 1)
        near, far = (square, swap_grp(square, 2)), (near_core[:n_small], swap_grp(square, 3))
        vectors = vectors + f(near_core[n_small:])
        sides = []
        for value, other in (near, far):
            low, high = pick(x_bit, value, other), pick(x_bit, other, value)
            sides.append(jnp.concatenate([low[:n_out], high[:n_out], low[n_out:], high[n_out:]], axis=0))
        square = (f(pick(core_bit, *sides)), f(pick(core_bit, *sides[::-1])))
        table_share = f(table_part)
    else:
        context_t, middle_t, act_t, grad_ffn, grad_pre, grad_attn = made
        lanes = lambda value, index: lax.dynamic_slice_in_dim(value, index * (value.shape[1] // 2), value.shape[1] // 2, 1)
        rows_of = lambda value, index: lax.dynamic_slice_in_dim(value, index * (value.shape[0] // 2), value.shape[0] // 2, 0)
        blocked = lambda value: value.reshape(blocks, value.shape[0] // blocks, value.shape[1])
        grad_queries, grad_keys_t, grad_values_t = attend_back(*back_args, ())
        table_kept, table_sent, grad_input_local, vectors = input_grads(
            blocks, grad_queries, grad_keys_t, grad_values_t, *input_args, ()
        )

        def packet(index):
            up = blocked(fwd_dot(middle_t, lanes(grad_pre, index)))
            return jnp.concatenate(
                [
                    blocked(fwd_dot(x_t[:, n_table:], lanes(grad_queries, index))),
                    blocked(back_dot(x_t, rows_of(grad_keys_t, index))),
                    blocked(back_dot(x_t, rows_of(grad_values_t, index))),
                    blocked(fwd_dot(context_t, lanes(grad_attn, index))),
                ]
                + [up[:, :, i : i + half_width] for i in range(0, up.shape[2], half_width)]
                + [blocked(fwd_dot(act_t, lanes(grad_ffn, index)))],
                axis=1,
            )

        total = (packet(core_bit) + f(swap_grp(packet(1 - core_bit).astype(BF), 1))).astype(BF)
        total = lax.psum_scatter(total, "blk", scatter_dimension=0, tiled=False)
        total = (f(total) + f(swap_grp(total, 2))).astype(BF)
        at = 4 * n_out
        square = total[: 3 * n_out]
        up_rows = total[at : at + ff_out]
        down_all = total[at + ff_out :]
        z_rows = jnp.concatenate([down_all[:first_rows], total[3 * n_out : at]], axis=0)
        down_rows = down_all[first_rows:]
        table_rows = jnp.stack([blocked_half.reshape(planes, 2 * tab, half_width) for blocked_half in (table_kept, table_sent)], axis=1)
        table_rows = table_rows.reshape(blocks, 2 * tab, half_width)
        table_rows = jnp.take(table_rows, jnp.arange(blocks) ^ own, axis=0)
        table_share = f(lax.psum_scatter(table_rows, "blk", scatter_dimension=0, tiled=False))
        vectors = lax.psum(vectors, ("blk", "grp"))
        early = jnp.concatenate([down_rows, z_rows], axis=0)
        out_up, out_down, out_out = big_outputs(up_rows, early)

    square = jnp.concatenate(square if packets else both_cores(square), axis=1)
    table_share = jnp.concatenate([table_share[:tab], table_share[tab:]], axis=1)
    vectors = jnp.concatenate([vectors[:16], vectors[16:]], axis=1)
    mine = lax.dynamic_slice_in_dim(vectors[:10], own * n_out, n_out, 1)
    up_bias_out = lax.dynamic_slice_in_dim(vectors[10:14].reshape(-1), own * ff_out, ff_out, 0)
    grad_input = grad_input_local.at[:tab].add(table_share)
    return (
        mixed,
        grad_input,
        mine[:2],
        square[:n_out],
        mine[2],
        square[n_out : 2 * n_out],
        square[2 * n_out :],
        mine[3],
        out_out,
        mine[4],
        mine[5],
        mine[6],
        out_up,
        up_bias_out,
        out_down,
        mine[7],
        mine[8],
        mine[9],
    )


def solution(mesh):
    both = ("grp", "blk")
    placed = (P(both, None), P(both), P(both), P(both)) + (P(),) * 16 + (P(both, None),)
    vec, mat = P("blk"), P("blk", None)
    return jax.shard_map(
        local,
        mesh=mesh,
        in_specs=placed,
        out_specs=(
            P(both, None), P(both, None), P(None, "blk"), mat, vec, mat, mat, vec, mat, vec,
            vec, vec, mat, vec, mat, vec, vec, vec,
        ),
        check_vma=False,
    )
```
